128 devices in a mesh: batch: 4 (over z), chan: 32 (over y, x, core).
Axes of the slice: x: 4, y: 4, z: 4, core: 2. Of those that a mesh axis runs over, the one named last changes fastest.
Arguments:
- features: bfloat16 [512, 128, 196], P('chan', 'batch'), may hold values from -6 to 6
- labels: int32 [128], P('batch'), may hold values from 0 to 999, as said below
- partner: int32 [128], P('batch'), may hold values from 0 to 127, as said below
- class_weight: float32 [1000], replicated, may hold values from 0.3 to 3
- point_one: float32 [512, 512], P(None, 'chan'), may hold values from -0.25 to 0.25
- momentum_one: float32 [512, 512], P(None, 'chan'), may hold values from -0.00012207031 to 0.00012207031
- point_two: float32 [512, 512], P(None, 'chan'), may hold values from -0.25 to 0.25
- momentum_two: float32 [512, 512], P(None, 'chan'), may hold values from -0.00012207031 to 0.00012207031
- expand: float32 [512, 2048], P(None, 'chan'), may hold values from -0.25 to 0.25
- momentum_up: float32 [512, 2048], P(None, 'chan'), may hold values from -0.00012207031 to 0.00012207031
- shrink: float32 [512, 2048], P(None, 'chan'), may hold values from -0.125 to 0.125
- momentum_down: float32 [512, 2048], P(None, 'chan'), may hold values from -0.00012207031 to 0.00012207031
- transit: float32 [512, 1024], P(None, 'chan'), may hold values from -0.25 to 0.25
- momentum_transit: float32 [512, 1024], P(None, 'chan'), may hold values from -0.00012207031 to 0.00012207031
- classifier: float32 [1024, 1000], P('chan'), may hold values from -0.1875 to 0.1875
- classifier_first: float32 [1024, 1000], P('chan'), may hold values from -1.5258789e-05 to 1.5258789e-05
- classifier_second: float32 [1024, 1000], P('chan'), may hold values from 2.7785758e-11 to 1.1328039e-10
- big_kernel: float32 [512, 31, 31], P('chan'), may hold values from -0.4375 to 0.4375
- big_first: float32 [512, 31, 31], P('chan'), may hold values from -1.5258789e-05 to 1.5258789e-05
- big_second: float32 [512, 31, 31], P('chan'), may hold values from 2.7785758e-11 to 1.1328039e-10
- small_kernel: float32 [512, 5, 5], P('chan'), may hold values from -0.4375 to 0.4375
- small_first: float32 [512, 5, 5], P('chan'), may hold values from -1.5258789e-05 to 1.5258789e-05
- small_second: float32 [512, 5, 5], P('chan'), may hold values from 2.7785758e-11 to 1.1328039e-10
- norm_gains: float32 [4, 512], P(None, 'chan'), may hold values from -0.5 to 2.2
- gains_first: float32 [4, 512], P(None, 'chan'), may hold values from -7.6293945e-05 to 7.6293945e-05
- gains_second: float32 [4, 512], P(None, 'chan'), may hold values from 2.7785758e-11 to 1.1328039e-10
- head_gains: float32 [2, 1024], P(None, 'chan'), may hold values from -0.5 to 2.2
- head_first: float32 [2, 1024], P(None, 'chan'), may hold values from -7.6293945e-05 to 7.6293945e-05
- head_second: float32 [2, 1024], P(None, 'chan'), may hold values from 1.7098928e-10 to 6.839571e-10
Outputs:
- loss_sum: float32 [], replicated
- weight_sum: float32 [], replicated
- grad_norm: float32 [], replicated
- point_one_new: float32 [512, 512], P(None, 'chan')
- momentum_one_new: float32 [512, 512], P(None, 'chan')
- point_two_new: float32 [512, 512], P(None, 'chan')
- momentum_two_new: float32 [512, 512], P(None, 'chan')
- expand_new: float32 [512, 2048], P(None, 'chan')
- momentum_up_new: float32 [512, 2048], P(None, 'chan')
- shrink_new: float32 [512, 2048], P(None, 'chan')
- momentum_down_new: float32 [512, 2048], P(None, 'chan')
- transit_new: float32 [512, 1024], P(None, 'chan')
- momentum_transit_new: float32 [512, 1024], P(None, 'chan')
- classifier_first_new: float32 [1024, 1000], P('chan')
- classifier_second_new: float32 [1024, 1000], P('chan')
- classifier_new: float32 [1024, 1000], P('chan')
- big_first_new: float32 [512, 31, 31], P('chan')
- big_second_new: float32 [512, 31, 31], P('chan')
- big_kernel_new: float32 [512, 31, 31], P('chan')
- small_first_new: float32 [512, 5, 5], P('chan')
- small_second_new: float32 [512, 5, 5], P('chan')
- small_kernel_new: float32 [512, 5, 5], P('chan')
- gains_first_new: float32 [4, 512], P(None, 'chan')
- gains_second_new: float32 [4, 512], P(None, 'chan')
- norm_gains_new: float32 [4, 512], P(None, 'chan')
- head_first_new: float32 [2, 1024], P(None, 'chan')
- head_second_new: float32 [2, 1024], P(None, 'chan')
- head_gains_new: float32 [2, 1024], P(None, 'chan')
The draws below stay inside these ranges and needn't reach their ends.
Inputs may be any that keep to these rules, and one draw needn't show every extreme that they name: `labels`: the two crops of one image carry the same label. partner pairs every crop of the first 64 with one of the last 64, both ways.
All inputs are finite; a program needn't handle non-finite values.
Results may differ from the reference program's by a relative error of at most 0.013.
Values may be sent and summed in bfloat16 or wider, within the bound.
No kernel may reach another device: no remote copies, remote signals or barrier semaphores. Data moves between devices by JAX's collectives and lax.ppermute only.
A program may use at most 192 MiB of HBM per device.

```python
import math
import jax
import jax.numpy as jnp
import numpy as np
from jax import lax

C = 512
FF = 2048
CT = 1024
K = 1000
S = 14
KB = 31
KS = 5
NS_STEPS = 5
STEP = 10
CROPS = 128
HW = 196
PARAMS = 4678656


def pair_plan(key):
    half = CROPS // 2
    order = jax.random.permutation(jax.random.fold_in(key, 11), half)
    inverse = jnp.argsort(order)
    kinds = jax.random.randint(jax.random.fold_in(key, 12), (half,), 0, K)
    partner = jnp.concatenate([order + half, inverse]).astype(jnp.int32)
    labels = jnp.concatenate([kinds, kinds[inverse]]).astype(jnp.int32)
    return (partner, labels)


def gain_rows(key, rows, width):
    noise = jax.random.uniform(jax.random.fold_in(key, 21), (rows, width), jnp.float32, -1.0, 1.0)
    offset = jax.random.uniform(jax.random.fold_in(key, 22), (rows, width), jnp.float32, -1.0, 1.0)
    ramp = 0.6 + 1.2 * jnp.arange(width, dtype=jnp.float32)[None, :] / width
    is_gain = (jnp.arange(rows) % 2 == 0)[:, None]
    return jnp.where(is_gain, ramp * (1.0 + 0.2 * noise), 0.5 * offset).astype(jnp.float32)


def draw_labels(key, part):
    plan = pair_plan(key)
    return plan[1]


def draw_partner(key, part):
    plan = pair_plan(key)
    return plan[0]


def draw_norm_gains(key, part):
    key = jax.random.fold_in(key, 3)
    return gain_rows(key, 4, C)


def draw_head_gains(key, part):
    key = jax.random.fold_in(key, 4)
    return gain_rows(key, 2, CT)


def block_scale(key, dims, split, low, high):
    level, own = 1.0, jax.random.fold_in(key, 6)
    for position, shards_of in split:
        steps = jnp.exp(jax.random.uniform(jax.random.fold_in(own, position), (shards_of,), jnp.float32, low / len(split), high / len(split)))
        level = level * jnp.repeat(steps, dims[position] // shards_of).reshape([-1 if axis == position else 1 for axis in range(len(dims))])
    return level


def gaussian(stream_key, extent, scale, reach, cuts=(), kind=jnp.bfloat16):
    values = jax.random.normal(stream_key, extent, jnp.float32) * scale
    if len(cuts) > 0:
        values = block_scale(stream_key, extent, cuts, -0.22, 0.18) * values
    return jnp.clip(values, min=-reach, max=reach).astype(kind)


def setup_inputs(seed: int = 0) -> dict:
    streams_of = jax.random.split(jax.random.key(seed), 30)
    return {
        "features": gaussian(streams_of[0], (C, CROPS, HW), 1.0, 6.0, ((0, 32), (1, 4))),
        "labels": draw_labels(jax.random.fold_in(streams_of[29], 71), 0),
        "partner": draw_partner(jax.random.fold_in(streams_of[29], 71), 0),
        "class_weight": jnp.clip(jnp.exp(jax.random.uniform(streams_of[3], (K,), jnp.float32, math.log(0.3), math.log(3.0))), 0.3, 3.0),
        "point_one": gaussian(streams_of[4], (C, C), C ** -0.5, 0.25, ((1, 32),), jnp.float32),
        "momentum_one": gaussian(streams_of[5], (C, C), (0.05 / PARAMS ** 0.5), 0.00012207031, ((1, 32),), jnp.float32),
        "point_two": gaussian(streams_of[6], (C, C), C ** -0.5, 0.25, ((1, 32),), jnp.float32),
        "momentum_two": gaussian(streams_of[7], (C, C), (0.05 / PARAMS ** 0.5), 0.00012207031, ((1, 32),), jnp.float32),
        "expand": gaussian(streams_of[8], (C, FF), C ** -0.5, 0.25, ((1, 32),), jnp.float32),
        "momentum_up": gaussian(streams_of[9], (C, FF), (0.05 / PARAMS ** 0.5), 0.00012207031, ((1, 32),), jnp.float32),
        "shrink": gaussian(streams_of[10], (C, FF), FF ** -0.5, 0.125, ((1, 32),), jnp.float32),
        "momentum_down": gaussian(streams_of[11], (C, FF), (0.05 / PARAMS ** 0.5), 0.00012207031, ((1, 32),), jnp.float32),
        "transit": gaussian(streams_of[12], (C, CT), C ** -0.5, 0.25, ((1, 32),), jnp.float32),
        "momentum_transit": gaussian(streams_of[13], (C, CT), (0.05 / PARAMS ** 0.5), 0.00012207031, ((1, 32),), jnp.float32),
        "classifier": gaussian(streams_of[14], (CT, K), CT ** -0.5, 0.1875, ((0, 32),), jnp.float32),
        "classifier_first": gaussian(streams_of[15], (CT, K), (0.0055 / PARAMS ** 0.5), 1.52587890625e-05, ((0, 32),), jnp.float32),
        "classifier_second": jnp.clip(jnp.exp(math.log(1.1328039201119466e-10) - 1.4053425 * jax.random.uniform(streams_of[16], (CT, K), jnp.float32) ** block_scale(streams_of[16], (CT, K), ((0, 32),), -0.2, 0.2)), 2.7785758069387434e-11, 1.1328039201119466e-10),
        "big_kernel": gaussian(streams_of[17], (C, KB, KB), (S * S) ** -0.5, 0.4375, ((0, 32),), jnp.float32),
        "big_first": gaussian(streams_of[18], (C, KB, KB), (0.0055 / PARAMS ** 0.5), 1.52587890625e-05, ((0, 32),), jnp.float32),
        "big_second": jnp.clip(jnp.exp(math.log(1.1328039201119466e-10) - 1.4053425 * jax.random.uniform(streams_of[19], (C, KB, KB), jnp.float32) ** block_scale(streams_of[19], (C, KB, KB), ((0, 32),), -0.2, 0.2)), 2.7785758069387434e-11, 1.1328039201119466e-10),
        "small_kernel": gaussian(streams_of[20], (C, KS, KS), (S * S) ** -0.5, 0.4375, ((0, 32),), jnp.float32),
        "small_first": gaussian(streams_of[21], (C, KS, KS), (0.0055 / PARAMS ** 0.5), 1.52587890625e-05, ((0, 32),), jnp.float32),
        "small_second": jnp.clip(jnp.exp(math.log(1.1328039201119466e-10) - 1.4053425 * jax.random.uniform(streams_of[22], (C, KS, KS), jnp.float32) ** block_scale(streams_of[22], (C, KS, KS), ((0, 32),), -0.2, 0.2)), 2.7785758069387434e-11, 1.1328039201119466e-10),
        "norm_gains": draw_norm_gains(jax.random.fold_in(streams_of[29], 71), 0),
        "gains_first": gaussian(streams_of[24], (4, C), (0.027 / PARAMS ** 0.5), 7.62939453125e-05, ((1, 32),), jnp.float32),
        "gains_second": jnp.clip(jnp.exp(math.log(1.1328039201119466e-10) - 1.4053425 * jax.random.uniform(streams_of[25], (4, C), jnp.float32) ** block_scale(streams_of[25], (4, C), ((1, 32),), -0.2, 0.2)), 2.7785758069387434e-11, 1.1328039201119466e-10),
        "head_gains": draw_head_gains(jax.random.fold_in(streams_of[29], 71), 0),
        "head_first": gaussian(streams_of[27], (2, CT), (0.027 / PARAMS ** 0.5), 7.62939453125e-05, ((1, 32),), jnp.float32),
        "head_second": jnp.clip(jnp.exp(math.log(6.839571131678213e-10) - 1.3862944 * jax.random.uniform(streams_of[28], (2, CT), jnp.float32) ** block_scale(streams_of[28], (2, CT), ((1, 32),), -0.2, 0.2)), 1.7098927829195532e-10, 6.839571131678213e-10),
    }


@jax.custom_vjp
def low(v):
    return lax.optimization_barrier(v.astype(jnp.bfloat16)).astype(jnp.float32)

@jax.custom_vjp
def low_back(v):
    return v

def low_keep(v):
    return (low(v), None)

def low_pass(kept, grad):
    return (grad,)

def back_keep(v):
    return (v, None)

def back_low(kept, grad):
    return (low(grad),)
low.defvjp(low_keep, low_pass)
low_back.defvjp(back_keep, back_low)
epsilon = 1e-05
highest = lax.Precision.HIGHEST
coef_first = 3.4445
coef_second = -4.775
coef_third = 2.0315
clip_limit = 0.05
momentum_decay = 0.95
muon_rate = 0.05
adam_rate = 0.05
norm_rate = 0.2
beta_first = 0.9
beta_second = 0.95
weight_decay = 0.01
contract_first = (((0,), (0,)), ((), ()))

def tap_table():
    rows = np.repeat(np.arange(S), S)
    cols = np.tile(np.arange(S), S)
    down = rows[:, None] - rows[None, :] + KB // 2
    across = cols[:, None] - cols[None, :] + KB // 2
    return jnp.asarray(down * KB + across, dtype=jnp.int32)

def batchnorm(values, gain, shift):
    center = lax.optimization_barrier(jnp.mean(values, axis=1, keepdims=True))
    spread = lax.optimization_barrier(jnp.mean(jnp.square(values - center), axis=1, keepdims=True))
    return (values - center) * lax.rsqrt(spread + epsilon) * gain[:, None] + shift[:, None]

def matmul_in(weight, values):
    return low_back(lax.dot_general(low(weight), low(values), contract_first, precision=highest))

def forward(weights, feats, labels, partner, class_weight):
    point_one, point_two, expand, shrink, transit, classifier, big_kernel, small_kernel, norm_gains, head_gains = weights
    count = CROPS * HW
    flatten = feats.reshape(C, count)
    normed = batchnorm(flatten, norm_gains[0], norm_gains[1])
    first = matmul_in(point_one, normed)
    margin = (KB - KS) // 2
    kernel = big_kernel + jnp.pad(small_kernel, ((0, 0), (margin, margin), (margin, margin)))
    taps = low(kernel).reshape(C, KB * KB)[:, tap_table()]
    source = low(jax.nn.gelu(first)).reshape(C, CROPS, HW)
    mixed = low_back(jnp.einsum('cqp,cnp->cnq', taps, source, precision=highest))
    middle = flatten + matmul_in(point_two, jax.nn.gelu(mixed).reshape(C, count))
    hidden = jax.nn.gelu(matmul_in(expand, batchnorm(middle, norm_gains[2], norm_gains[3])))
    final = middle + low_back(jnp.dot(low(shrink), low(hidden), precision=highest))
    trans = jax.nn.gelu(matmul_in(transit, final))
    pooled = lax.optimization_barrier(jnp.mean(trans.reshape(CT, CROPS, HW), axis=2))
    head_in = batchnorm(pooled, head_gains[0], head_gains[1])
    logits = low_back(lax.dot_general(low(head_in), low(classifier), contract_first, precision=highest))
    average = 0.5 * (logits + logits[partner])
    logprob = jax.nn.log_softmax(average, axis=1)
    onehot = (labels[:, None] == jnp.arange(K)[None, :]).astype(jnp.float32)
    crop_weight = 0.5 * lax.optimization_barrier(jnp.sum(onehot * class_weight[None, :], axis=1))
    loss_sum = -jnp.sum(crop_weight * lax.optimization_barrier(jnp.sum(onehot * logprob, axis=1)))
    weight_sum = jnp.sum(crop_weight)
    return (loss_sum / weight_sum, (loss_sum, weight_sum))

def orthogonal(update):
    current = update / (jnp.sqrt(jnp.sum(update * update)) + 1e-07)
    for number in range(NS_STEPS):
        gram = jnp.dot(current, current.T, precision=highest)
        mixing = coef_second * gram + coef_third * jnp.dot(gram, gram, precision=highest)
        current = coef_first * current + jnp.dot(mixing, current, precision=highest)
    return current

def muon(weight, moment, gradient):
    fresh = momentum_decay * moment + gradient
    direction = orthogonal(gradient + momentum_decay * fresh)
    factor = 0.2 * math.sqrt(max(weight.shape))
    return (weight * (1.0 - muon_rate * weight_decay) - muon_rate * factor * direction, fresh)

def adamw(weight, first, second, gradient, rate):
    first = beta_first * first + (1.0 - beta_first) * gradient
    second = beta_second * second + (1.0 - beta_second) * gradient * gradient
    ratio = first / (1.0 - beta_first ** STEP) / (jnp.sqrt(second / (1.0 - beta_second ** STEP)) + 1e-08)
    return (first, second, weight - rate * (ratio + weight_decay * weight))

def reference(features, labels, partner, class_weight, point_one, momentum_one, point_two, momentum_two, expand, momentum_up, shrink, momentum_down, transit, momentum_transit, classifier, classifier_first, classifier_second, big_kernel, big_first, big_second, small_kernel, small_first, small_second, norm_gains, gains_first, gains_second, head_gains, head_first, head_second):
    weights = (point_one, point_two, expand, shrink, transit, classifier, big_kernel, small_kernel, norm_gains, head_gains)
    feats = features.astype(jnp.float32)

    def objective(params):
        return forward(params, feats, labels, partner, class_weight)
    loss, pull, sums = jax.vjp(objective, weights, has_aux=True)
    grads = pull(jnp.ones_like(loss))[0]
    squares = sum((jnp.sum(item * item) for item in grads))
    grad_norm = jnp.sqrt(squares)
    factor = jnp.minimum(1.0, clip_limit / (grad_norm + 1e-06))
    clipped = [item * factor for item in grads]
    moments = (momentum_one, momentum_two, momentum_up, momentum_down, momentum_transit)
    updated = [muon(weights[index], moments[index], clipped[index]) for index in range(5)]
    head_out = adamw(classifier, classifier_first, classifier_second, clipped[5], adam_rate)
    big_out = adamw(big_kernel, big_first, big_second, clipped[6], adam_rate)
    small_out = adamw(small_kernel, small_first, small_second, clipped[7], adam_rate)
    norm_out = adamw(norm_gains, gains_first, gains_second, clipped[8], norm_rate)
    hnorm_out = adamw(head_gains, head_first, head_second, clipped[9], norm_rate)
    return (sums[0], sums[1], grad_norm, updated[0][0], updated[0][1], updated[1][0], updated[1][1], updated[2][0], updated[2][1], updated[3][0], updated[3][1], updated[4][0], updated[4][1], head_out[0], head_out[1], head_out[2], big_out[0], big_out[1], big_out[2], small_out[0], small_out[1], small_out[2], norm_out[0], norm_out[1], norm_out[2], hnorm_out[0], hnorm_out[1], hnorm_out[2])
```

```python
import math

import jax
import jax.numpy as jnp
import numpy as np
from jax import lax
from jax.experimental import pallas as pl
from jax.experimental.pallas import tpu as pltpu
from jax.sharding import PartitionSpec as P

S = 14
KB = 31
KS = 5
NS_STEPS = 5
STEP = 10
AREA = S * S
WIDE = S * 16
TAPS = 2 * S - 1

f32 = jnp.float32
bf16 = jnp.bfloat16
epsilon = 1e-05
highest = lax.Precision.HIGHEST
coef_first = 3.4445
coef_second = -4.775
coef_third = 2.0315
clip_limit = 0.05
momentum_decay = 0.95
muon_rate = 0.05
adam_rate = 0.05
norm_rate = 0.2
beta_first = 0.9
beta_second = 0.95
weight_decay = 0.01
root_two_pi = math.sqrt(2.0 / math.pi)
both = ("batch", "chan")


def dot(a, b, left=1, right=0, precision=None):
    return lax.dot_general(
        a, b, (((left,), (right,)), ((), ())), precision=precision, preferred_element_type=f32
    )


def gelu_pair(x):
    square = x * x
    t = jnp.tanh(root_two_pi * x * (1.0 + 0.044715 * square))
    half = 0.5 * (1.0 + t)
    slope = half + 0.5 * x * (1.0 - t * t) * (root_two_pi * (1.0 + 0.134145 * square))
    return x * half, slope


def three(x):
    high = lax.reduce_precision(x, 8, 7)
    rest = x - high
    mid = lax.reduce_precision(rest, 8, 7)
    return [high.astype(bf16), mid.astype(bf16), (rest - mid).astype(bf16)]


def core_swap(x):
    return lax.ppermute(x, "chan", [(i, i ^ 1) for i in range(32)])


def same_core():
    return [[2 * i + k for i in range(16)] for k in range(2)]


def z_shifts(x):
    return [lax.ppermute(x, "batch", [(i, (i + k) % 4) for i in range(4)]) for k in range(1, 4)]


def groups_all_to_all(x):
    return lax.all_to_all(x, "chan", 0, 0, tiled=True, axis_index_groups=same_core())


def z_gather(x):
    z = lax.axis_index("batch")
    got = [x] + z_shifts(x)
    rows = []
    for j in range(4):
        k = lax.rem(z - j + 4, 4)
        rows.append(
            jnp.where(k == 0, got[0], jnp.where(k == 1, got[1], jnp.where(k == 2, got[2], got[3])))
        )
    return jnp.stack(rows)


def widen_matrix():
    e = np.zeros((256, 256), np.float32)
    for y in range(S):
        for x in range(S):
            e[y * S + x, y * 16 + x] = 1
    return jnp.asarray(e, bf16)


def compact_matrix():
    e = np.zeros((896, 512), np.float32)
    for f in range(TAPS):
        for x in range(S):
            e[f * 32 + x, f * S + x] = 1
    return jnp.asarray(e, bf16)


def whole(body, outs, name, scratch=(), scalars=0, limit=32):
    space = pl.BlockSpec(memory_space=pltpu.VMEM)
    small = pl.BlockSpec(memory_space=pltpu.SMEM)

    def call(*args):
        return pl.pallas_call(
            body,
            out_shape=[jax.ShapeDtypeStruct(*item) for item in outs],
            in_specs=[small] * scalars + [space] * (len(args) - scalars),
            out_specs=[space] * len(outs),
            scratch_shapes=list(scratch),
            name=name,
            compiler_params=pltpu.CompilerParams(vmem_limit_bytes=limit * 1024 * 1024),
        )(*args)

    return call


def valid(rows):
    return lax.broadcasted_iota(jnp.int32, (rows, 256), 1) < AREA


def column(tail, i):
    at = AREA - 128 + 3 * i
    return (tail[:, at : at + 1] + tail[:, at + 1 : at + 2]) + tail[:, at + 2 : at + 3]


def row_sums(x):
    return dot(jnp.ones((8, x.shape[1]), f32), x, 1, 1, highest)[0:1]


def pack_row(row):
    return jnp.concatenate([row[:, j * 128 : (j + 1) * 128] for j in range(8)], axis=0)


def as_columns(packed):
    rows = lax.broadcasted_iota(jnp.int32, (8, 128), 0)
    lanes = lax.broadcasted_iota(jnp.int32, (8, 128), 1)
    turned = dot(packed, (rows == lanes).astype(f32), 0, 0, highest)
    return [
        jnp.concatenate([turned[:, j : j + 1] for j in range(4 * h, 4 * h + 4)], axis=0)
        for h in range(2)
    ]


def by_turn(k, rows):
    four = rows.reshape(16, 2, 16, 256)
    first, second = four[:, 0].reshape(256, 256), four[:, 1].reshape(256, 256)
    return jnp.where(k == 0, first, second), jnp.where(k == 0, second, first)


def taps_body(shifted, compact, table):
    z = dot(shifted[...], compact[...])
    keep = valid(256)
    for py in range(S):
        at = (S - 1 - py) * S
        rows = jnp.where(keep, z[:, at : at + 256], 0.0).astype(bf16)
        table[:, py * 16 : (py + 1) * 16, :] = rows.reshape(16, 16, 256)
    table[:, WIDE:, :] = jnp.zeros((16, 256 - WIDE, 256), bf16)


def first_body(came, act, slope, normed):
    tail = came[:, 128:256].astype(f32)
    x = came[:, :256].astype(f32) - column(tail, 0)
    a = jnp.where(valid(512), x * column(tail, 1) + column(tail, 2), 0.0).astype(bf16)
    normed[...] = a
    for i in range(2):
        rows = pl.ds(i * 256, 256)
        value, back = gelu_pair(dot(came[rows, 256:768], a))
        act[rows, :] = value.astype(bf16)
        slope[rows, :] = back


def depth_forward_body(u, table, widen, mixed, act):
    for c in range(16):
        wide = dot(u[c], widen[...]).astype(bf16)
        d = dot(wide, table[c])
        mixed[c] = d
        act[c] = gelu_pair(d)[0].astype(bf16)


def middle_body(came, gd, weight, middle, stats):
    keep = valid(512)
    x = jnp.where(keep, came[:, :256].astype(f32), 0.0) + dot(weight[...], gd[...])
    middle[...] = x
    mean = jnp.sum(x, axis=1, keepdims=True) * (1.0 / AREA)
    apart = jnp.where(keep, x - mean, 0.0)
    row = jnp.concatenate([row_sums(x), row_sums(apart * apart)], axis=1) * (1.0 / AREA)
    stats[...] = jnp.broadcast_to(pack_row(row)[None], (128, 8, 128))


def forward_body(
    k, came, middle, stats, up, down, transit, normal, factor, pack, keep_act, slope_hid, slope_t, pooled
):
    tail = came[:, 128:256].astype(f32)
    parts = stats[...]
    total = jnp.sum(parts, axis=0) * (1.0 / 128)
    apart = parts - total[None]
    spread = jnp.sum(apart * apart, axis=0) * (1.0 / 128)
    both_cols = as_columns(total)
    center = both_cols[0]
    variance = both_cols[1] + as_columns(spread)[0]
    scale = lax.rsqrt(variance + epsilon)
    gain = column(tail, 3)
    x1 = middle[...]
    xh = (x1 - center) * scale
    keep = valid(512)
    normal[...] = jnp.where(keep, xh, 0.0)
    factor[...] = jnp.broadcast_to(gain * scale, (512, 128))
    a2 = jnp.where(keep, xh * gain + column(tail, 4), 0.0).astype(bf16)
    pack[1536:2048, :] = a2
    total = x1
    for i in range(8):
        rows = pl.ds(i * 256, 256)
        value, back = gelu_pair(dot(up[rows, :], a2))
        low = value.astype(bf16)
        slope_hid[rows, :] = back
        if i < 4:
            keep_act[rows, :] = low
        else:
            pack[(i - 4) * 256 : (i - 3) * 256, :] = low
    total = x1 + dot(down[:, :1024], keep_act[...]) + dot(down[:, 1024:], pack[:1024, :])
    x2 = total.astype(bf16)
    pack[1024:1536, :] = x2
    halves = []
    keep = valid(512)
    for i in range(2):
        rows = pl.ds(i * 512, 512)
        value, back = gelu_pair(dot(transit[rows, :], x2))
        slope_t[rows, :] = jnp.where(keep, back, 0.0)
        halves.append(row_sums(value) * (1.0 / AREA))
    turn = k[0] == 1
    row = jnp.concatenate(
        [jnp.where(turn, halves[1], halves[0]), jnp.where(turn, halves[0], halves[1])], axis=1
    )
    pooled[...] = jnp.broadcast_to(pack_row(row)[None], (128, 8, 128))


def head_body(
    place,
    pooled,
    gains,
    people,
    class_weight,
    classes,
    slope_t,
    slope_hid,
    normal,
    transit,
    down,
    up,
    pack,
    keep_hid,
    keep_t,
    dx2,
    da2,
    sums,
    class_grad,
    head_grad,
    losses,
):
    k, crop, at = place[0], place[1], place[2]
    x = pooled[...]
    center = jnp.sum(x, axis=0, keepdims=True) * (1.0 / 128)
    apart = x - center
    scale = lax.rsqrt(jnp.sum(apart * apart, axis=0, keepdims=True) * (1.0 / 128) + epsilon)
    xh = apart * scale
    gain = gains[0:1, :]
    z = (xh * gain + gains[1:2, :]).astype(bf16)
    logits = dot(z, classes[...])
    lanes = lax.broadcasted_iota(jnp.int32, (128, 128), 1)
    rows = lax.broadcasted_iota(jnp.int32, (128, 128), 0)
    pairing = (people[:, 1:2] == lanes.astype(f32)).astype(f32)
    average = 0.5 * (logits + dot(pairing, logits, 1, 0, highest))
    wide = lax.broadcasted_iota(jnp.int32, (128, 1024), 1)
    average = jnp.where(wide < 1000, average, -1e30)
    top = jnp.max(average, axis=1, keepdims=True)
    moved = average - top
    expo = jnp.exp(moved)
    norm = jnp.sum(expo, axis=1, keepdims=True)
    onehot = (people[:, 0:1] == wide.astype(f32)).astype(f32)
    weight = 0.5 * jnp.sum(onehot * class_weight[...], axis=1, keepdims=True)
    picked = jnp.sum(jnp.where(onehot > 0, moved, 0.0), axis=1, keepdims=True) - jnp.log(norm)
    weight_sum = jnp.sum(weight, axis=0, keepdims=True)
    loss_sum = -jnp.sum(weight * picked, axis=0, keepdims=True)
    line = lax.broadcasted_iota(jnp.int32, (8, 128), 1)
    losses[...] = jnp.where(line == 0, loss_sum, weight_sum)
    dl = ((weight / weight_sum) * (expo / norm - onehot)).astype(bf16)
    dz = dot(dl, classes[...], 1, 1)
    dshift = jnp.sum(dz, axis=0, keepdims=True)
    dgain = jnp.sum(dz * xh, axis=0, keepdims=True)
    dp = (gain * scale) * (dz - (dshift + xh * dgain) * (1.0 / 128))
    mine = dot(dp, (rows == crop).astype(f32), 0, 0, highest)[:, 0:1] * (1.0 / AREA)
    turn = k == 1
    first = jnp.where(turn, mine[512:], mine[:512])
    second = jnp.where(turn, mine[:512], mine[512:])
    own_rows = lax.broadcasted_iota(jnp.int32, (1024, 128), 0)
    own_lanes = lax.broadcasted_iota(jnp.int32, (1024, 128), 1)
    select = ((own_rows == own_lanes + at) & (own_lanes < 32)).astype(f32)
    z_own = dot(z, select.astype(bf16)).astype(bf16)
    class_grad[...] = dot(z_own, dl, 0, 0)[:32]
    both_rows = jnp.concatenate([dgain, dshift, jnp.zeros((6, 1024), f32)], axis=0)
    head_grad[...] = dot(both_rows, select, 1, 0, highest)

    keep_t[...] = (slope_t[:512, :] * first).astype(bf16)
    pack[1024:1536, :] = (slope_t[512:, :] * second).astype(bf16)
    grad = dot(transit[:, :512], keep_t[...]) + dot(transit[:, 512:], pack[1024:1536, :])
    dx2[...] = grad
    low = grad.astype(bf16)
    pack[1536:2048, :] = low
    for i in range(8):
        rows = pl.ds(i * 256, 256)
        part = (slope_hid[rows, :] * dot(down[rows, :], low)).astype(bf16)
        if i < 4:
            keep_hid[rows, :] = part
        else:
            pack[(i - 4) * 256 : (i - 3) * 256, :] = part
    grad = dot(up[:, :1024], keep_hid[...]) + dot(up[:, 1024:], pack[:1024, :])
    da2[...] = grad
    row = jnp.concatenate([row_sums(grad * normal[...]), row_sums(grad)], axis=1)
    sums[...] = jnp.broadcast_to(pack_row(row)[None], (128, 8, 128))


def outer_body(keep_act, keep_hid, keep_t, one, two, one_in, two_in, result):
    def product(rows, v, rows_in, v_in):
        return dot(rows, v, 1, 1) + dot(rows_in, v_in, 1, 1)

    for i in range(2):
        rows = slice(i * 512, (i + 1) * 512)
        ys = slice(i * 8, (i + 1) * 8)
        result[ys, 0:64, :] = product(
            keep_hid[rows], one[1536:2048], two_in[rows], one_in[1536:2048]
        ).reshape(8, 64, 512)
        result[ys, 64:128, :] = product(
            keep_act[rows], two[1536:2048], one_in[rows], two_in[1536:2048]
        ).reshape(8, 64, 512)
    result[:, 128:160, :] = product(
        keep_t[...], one[1024:1536], two_in[1024:1536], one_in[1024:1536]
    ).reshape(16, 32, 512)


def second_body(k, sums, da2, normal, factor, dx2, weight, gd, normed, keep_rows, pack, back, norm):
    total = jnp.sum(sums[...], axis=0)
    norm[...] = total
    gain, shift = as_columns(total)
    inner = da2[...] - (shift + normal[...] * gain) * (1.0 / (128 * AREA))
    grad = dx2[...] + jnp.where(valid(512), factor[:, 0:1] * inner, 0.0)
    low = grad.astype(bf16)
    keep, send = by_turn(k[0], low)
    keep_rows[...] = keep
    pack[0:256, :] = send
    pack[256:768, :] = gd[...]
    pack[768:1280, :] = normed[...]
    back[...] = dot(weight[...], low).astype(bf16)


def depth_backward_body(u, mixed, grad, table, widen, compact, back, taps, outer):
    outer[...] = jnp.zeros_like(outer)
    for c in range(16):
        wide = dot(u[c], widen[...]).astype(bf16)
        slope = gelu_pair(mixed[c])[1]
        dd = (grad[c].astype(f32) * slope).astype(bf16)
        du = dot(dd, table[c], 1, 1).astype(bf16)
        back[c] = dot(du, widen[...], 1, 1).astype(bf16)
        outer[c, :, :256] = dot(wide, dd, 0, 0)
    total = jnp.zeros((256, 512), f32)
    for py in range(S):
        rows = outer[:, py * 16 : (py + 1) * 16, :].reshape(256, 512)
        at = (S - 1 - py) * S
        total = total + (pltpu.roll(rows, at, 1) if at else rows)
    taps[...] = dot(total, compact[...].astype(f32), 1, 1, highest)


def third_body(k, came, du, slope, weight, keep_rows, send_rows, keep_norm, send_norm):
    tail = came[:, 128:256].astype(f32)
    dh = (slope[...] * du[...].astype(f32)).astype(bf16)
    keep, send = by_turn(k[0], dh)
    keep_rows[...] = keep
    send_rows[...] = send
    da = dot(weight[...], dh)
    x = came[:, :256].astype(f32) - column(tail, 0)
    gain, shift = row_sums(da * x), row_sums(da)
    ys = lax.broadcasted_iota(jnp.int32, (16, 512), 0)
    owner = lax.broadcasted_iota(jnp.int32, (16, 512), 1) // 16
    fold_rows = lax.broadcasted_iota(jnp.int32, (512, 128), 0) % 16
    fold_lanes = lax.broadcasted_iota(jnp.int32, (512, 128), 1)
    fold_gain = (fold_rows == fold_lanes).astype(f32)
    fold_shift = (fold_rows == fold_lanes - 16).astype(f32)

    def part(core):
        own = owner == 2 * ys + core
        return dot(jnp.where(own, gain, 0.0), fold_gain, 1, 0, highest) + dot(
            jnp.where(own, shift, 0.0), fold_shift, 1, 0, highest
        )

    keep_norm[...] = part(k[0])
    send_norm[...] = part(1 - k[0])


def last_outer_body(keep_one, keep_two, pack, got_one, got_pack, keep_norm, got_norm, result):
    one = dot(keep_one[...], pack[768:1280, :], 1, 1) + dot(
        got_one[...], got_pack[768:1280, :], 1, 1
    )
    two = dot(keep_two[...], pack[256:768, :], 1, 1) + dot(
        got_pack[0:256, :], got_pack[256:768, :], 1, 1
    )
    result[:, 0:16, :] = one.reshape(16, 16, 512)
    result[:, 16:32, :] = two.reshape(16, 16, 512)
    result[:, 32:40, :] = jnp.zeros((16, 8, 512), f32)
    result[:, 32:33, 0:128] = (keep_norm[...] + got_norm[...]).reshape(16, 1, 128)


def pick(z, rows):
    blank = jnp.zeros((32, 512), f32)
    third = jnp.concatenate([rows[128:160], blank], axis=0)
    fourth = jnp.concatenate([rows[160:192], blank], axis=0)
    return jnp.where(
        z == 0, rows[0:64], jnp.where(z == 1, rows[64:128], jnp.where(z == 2, third, fourth))
    )


def gather_body(
    z, parts, parts_one, parts_two, parts_three, taps, class_grad, head_grad, norm_two, scale,
    grads, near, norm_one, message,
):
    total = (parts[...] + parts_one[...]) + (parts_two[...] + parts_three[...])
    rows = total[:192]
    grads[...] = rows
    norm = total[192:200, 0:128] * scale[...]
    norm_one[...] = norm
    tap = taps[...]
    row = lax.broadcasted_iota(jnp.int32, (32, 512), 0)
    lane = lax.broadcasted_iota(jnp.int32, (32, 512), 1)
    down = (row % 2) * 16 + lane // 32
    across = lane % 32
    centre = (down >= 11) & (down <= 15) & (across >= 11) & (across <= 15)

    def everything(x):
        return jnp.sum(jnp.sum(x, axis=1, keepdims=True), axis=0, keepdims=True)

    square = everything(rows * rows) + everything(class_grad[...] * class_grad[...])
    square = square + everything(jnp.where(centre, 2.0, 1.0) * (tap * tap))
    square = square + everything(head_grad[...] * head_grad[...])
    square = square + everything(norm_two[...] * norm_two[...]) + everything(norm * norm)
    mine = pick(z[0], rows)
    near[...] = mine
    high = square.astype(bf16)
    rest = square - high.astype(f32)
    mid = rest.astype(bf16)
    low = (rest - mid.astype(f32)).astype(bf16)
    rows16 = lax.broadcasted_iota(jnp.int32, (16, 512), 0)
    lanes16 = lax.broadcasted_iota(jnp.int32, (16, 512), 1)
    tail = jnp.where(
        lanes16 == 0,
        high.astype(f32),
        jnp.where(lanes16 == 1, mid.astype(f32), jnp.where(lanes16 == 2, low.astype(f32), 0.0)),
    )
    tail = jnp.where(rows16 == 0, tail, 0.0)
    line = jnp.concatenate([mine, tail], axis=0).astype(bf16)
    message[...] = jnp.broadcast_to(line[None], (16, 80, 512))


def split(x):
    high = x.astype(bf16)
    return high, (x - high.astype(f32)).astype(bf16)


def mul3(a, b):
    return dot(a[0], b[0]) + (dot(a[0], b[1]) + dot(a[1], b[0]))


def muon_body(
    place, got, got_other, moment, moment_other, near, near_other, near_moment, near_moment_other,
    result, scalars, u,
):
    z, k = place[0], place[1]

    def tails(ref):
        x = ref[:, 64:80, :].astype(f32)
        return jnp.sum(jnp.sum(x, axis=0), axis=0, keepdims=True)

    square = jnp.sum(tails(got) + tails(got_other), axis=1, keepdims=True)
    norm = jnp.sqrt(square)
    f = jnp.minimum(1.0, clip_limit / (norm + 1e-06))
    line = lax.broadcasted_iota(jnp.int32, (8, 128), 1)
    scalars[...] = jnp.where(line == 0, norm, f)
    alpha = (1.0 + momentum_decay) * f
    beta = momentum_decay * momentum_decay
    low = jnp.where(z == 3, k * 16, 0)
    high = jnp.where(z == 3, k * 16 + 16, 64)
    for i, (g, m) in enumerate(((got, moment), (got_other, moment_other))):
        for y in range(0, 16, 4):
            rows = lax.broadcasted_iota(jnp.int32, (4, 64, 512), 1)
            value = alpha * g[y : y + 4, :64, :].astype(f32) + beta * m[y : y + 4].astype(f32)
            value = jnp.where((rows >= low) & (rows < high), value, 0.0).astype(bf16)
            at = i * 1024 + y * 64
            u[at : at + 256, :] = value.reshape(256, 512)
    gram = dot(u[...], u[...], 0, 0)
    rows = lax.broadcasted_iota(jnp.int32, (512, 512), 0)
    cols = lax.broadcasted_iota(jnp.int32, (512, 512), 1)
    eye = (rows == cols).astype(f32)
    total = jnp.sum(jnp.sum(gram * eye, axis=0, keepdims=True), axis=1, keepdims=True)
    inverse = 1.0 / (jnp.sqrt(total) + 1e-07)
    a = gram * (inverse * inverse)
    q = None
    for step in range(NS_STEPS):
        a2 = split(a)
        square = mul3(a2, a2)
        m = coef_first * eye + coef_second * a + coef_third * square
        m2 = split(m)
        q = m if q is None else mul3(m2, split(q))
        if step < NS_STEPS - 1:
            a = mul3(split(mul3(a2, m2)), m2)
    q = split(q)
    for i, (g, m) in enumerate(((near, near_moment), (near_other, near_moment_other))):
        value = (alpha * g[...] + beta * m[...]) * inverse
        result[i * 64 : (i + 1) * 64, :] = mul3(split(value), q)


def adamw(weight, first, second, gradient, rate):
    first = beta_first * first + (1.0 - beta_first) * gradient
    second = beta_second * second + (1.0 - beta_second) * gradient * gradient
    ratio = (
        first / (1.0 - beta_first**STEP) / (jnp.sqrt(second / (1.0 - beta_second**STEP)) + 1e-08)
    )
    return (first, second, weight - rate * (ratio + weight_decay * weight))


def shards(
    features,
    labels,
    partner,
    class_weight,
    point_one,
    momentum_one,
    point_two,
    momentum_two,
    expand,
    momentum_up,
    shrink,
    momentum_down,
    transit,
    momentum_transit,
    classifier,
    classifier_first,
    classifier_second,
    big_kernel,
    big_first,
    big_second,
    small_kernel,
    small_first,
    small_second,
    norm_gains,
    gains_first,
    gains_second,
    head_gains,
    head_first,
    head_second,
):
    z = lax.axis_index("batch")
    c = lax.axis_index("chan")
    k = lax.rem(c, 2)
    crop = z * 32 + c
    widen = widen_matrix()
    compact = compact_matrix()
    k_scalar = k.reshape(1).astype(jnp.int32)
    classes = class_weight.shape[0]

    flat = features.astype(f32)
    local_mean = jnp.mean(flat, axis=(1, 2))
    local_spread = jnp.mean(jnp.square(flat - local_mean[:, None, None]), axis=(1, 2))
    vector = jnp.concatenate(
        [local_mean, local_spread, labels.astype(f32), partner.astype(f32)]
    )[None, :]
    gathered = z_gather(vector)[:, 0, :]
    means = gathered[:, :16]
    center = jnp.mean(means, axis=0)
    variance = jnp.mean(gathered[:, 16:32], axis=0) + jnp.mean(
        jnp.square(means - center[None]), axis=0
    )
    people = jnp.stack([gathered[:, 32:64].reshape(128), gathered[:, 64:96].reshape(128)], axis=1)
    scale_own = lax.rsqrt(variance + epsilon)

    class_low = jnp.pad(classifier.astype(bf16), ((0, 0), (0, 1024 - classes)))
    moments_t = jnp.concatenate(
        [m.T for m in (momentum_up, momentum_down, momentum_transit, momentum_one, momentum_two)],
        axis=0,
    )
    near_moment = pick(z, moments_t)
    packed = jnp.concatenate(
        [
            point_two.T.astype(bf16),
            expand.T.astype(bf16),
            shrink.T.astype(bf16),
            transit.T.astype(bf16),
            class_low[:, :512],
            class_low[:, 512:],
            near_moment.astype(bf16),
        ],
        axis=0,
    )
    own = lax.all_gather(packed, "chan", axis=0, tiled=False, axis_index_groups=same_core())
    near_moment_other = core_swap(near_moment)

    margin = (KB - KS) // 2
    kernel = big_kernel + jnp.pad(small_kernel, ((0, 0), (margin, margin), (margin, margin)))
    centre = kernel[:, 2:29, 2:29].astype(bf16)
    flat_kernel = jnp.pad(
        jnp.pad(centre, ((0, 0), (0, 0), (0, 5))).reshape(16, TAPS * 32), ((0, 0), (0, 48))
    )
    shifted = jnp.stack(
        [flat_kernel[:, 13 - px : 13 - px + 896] for px in range(S)]
        + [jnp.zeros((16, 896), bf16)] * 2,
        axis=1,
    ).reshape(256, 896)
    (table,) = whole(taps_body, [((16, 256, 256), bf16)], "taps")(shifted, compact)

    extra = []
    for item in (
        center,
        scale_own * norm_gains[0],
        norm_gains[1],
        norm_gains[2],
        norm_gains[3],
        head_gains[0, :16],
        head_gains[0, 16:],
        head_gains[1, :16],
        head_gains[1, 16:],
    ):
        extra += three(item)
    extra = jnp.stack(extra, axis=1)
    extra = jnp.pad(extra, ((0, 0), (0, 60 - extra.shape[1])))
    fixed = jnp.concatenate([extra, point_one.T.astype(bf16)], axis=1)
    payload = jnp.concatenate(
        [features.transpose(1, 0, 2), jnp.broadcast_to(fixed[None], (32,) + fixed.shape)], axis=2
    )
    came = lax.all_to_all(payload, "chan", 0, 0, tiled=True).reshape(512, 768)
    act_one, slope_one, a1 = whole(
        first_body, [((512, 256), bf16), ((512, 256), f32), ((512, 256), bf16)], "first"
    )(came)
    u = lax.all_to_all(act_one.reshape(32, 16, 256), "chan", 0, 0, tiled=True).transpose(1, 0, 2)
    mixed, act = whole(
        depth_forward_body, [((16, 32, 256), f32), ((16, 32, 256), bf16)], "depth_forward"
    )(u, table, widen)
    gd = lax.all_to_all(act.transpose(1, 0, 2), "chan", 0, 0, tiled=True).reshape(512, 256)

    late = act[0:1, 0:8, 0:128]
    own = lax.dynamic_update_slice(
        own, jnp.where(late < 1e30, own[0:1, 0:8, 0:128], late), (0, 0, 0)
    )
    other = core_swap(own)
    two_own, two_other = own[:, 0:16], other[:, 0:16]
    weight_two = jnp.stack(
        [jnp.where(k == 0, two_own, two_other), jnp.where(k == 0, two_other, two_own)], axis=1
    ).reshape(512, 512)

    def both_halves(start, rows):
        return jnp.concatenate(
            [
                own[:, start : start + rows].reshape(16 * rows, 512),
                other[:, start : start + rows].reshape(16 * rows, 512),
            ],
            axis=0,
        )

    weight_up = both_halves(16, 64)
    weight_down = both_halves(80, 64)
    weight_transit = both_halves(144, 32)
    weight_class = jnp.concatenate([both_halves(176, 32), both_halves(208, 32)], axis=1)
    class_pair = weight_class.reshape(2, 512, 1024)
    swap = k == 1
    weight_class = jnp.where(swap, class_pair[::-1], class_pair).reshape(1024, 1024)

    def head_row(i):
        def col(j):
            part = came[:, AREA + 3 * j : AREA + 3 * j + 3].astype(f32)
            return ((part[:, 0] + part[:, 1]) + part[:, 2]).reshape(32, 16)

        natural = jnp.stack([col(i), col(i + 1)], axis=1).reshape(16, 2, 32)
        return natural.transpose(1, 0, 2).reshape(1, 1024)

    head_rows = jnp.concatenate([head_row(5), head_row(7)], axis=0)

    middle, stats = whole(middle_body, [((512, 256), f32), ((128, 8, 128), f32)], "middle")(
        came, gd, weight_two
    )
    stats = lax.all_to_all(stats, both, 0, 0, tiled=True)
    normal_two, factor_two, pack_one, keep_act, slope_hid, slope_t, pooled = whole(
        forward_body,
        [
            ((512, 256), f32),
            ((512, 128), f32),
            ((2048, 256), bf16),
            ((1024, 256), bf16),
            ((2048, 256), f32),
            ((1024, 256), f32),
            ((128, 8, 128), f32),
        ],
        "forward",
        scalars=1,
    )(k_scalar, came, middle, stats, weight_up, weight_down.T, weight_transit)
    pooled = lax.all_to_all(pooled, both, 0, 0, tiled=True).reshape(128, 1024)
    place = jnp.stack([k, crop, k * 512 + (c // 2) * 32]).astype(jnp.int32)
    pack_two, keep_hid, keep_t, dx2, da2, sums, class_grad, head_grad, losses = whole(
        head_body,
        [
            ((2048, 256), bf16),
            ((1024, 256), bf16),
            ((512, 256), bf16),
            ((512, 256), f32),
            ((512, 256), f32),
            ((128, 8, 128), f32),
            ((32, 1024), f32),
            ((8, 128), f32),
            ((8, 128), f32),
        ],
        "head",
        scalars=1,
    )(
        place,
        pooled,
        head_rows,
        people,
        jnp.pad(class_weight, (0, 1024 - classes))[None, :],
        weight_class,
        slope_t,
        slope_hid,
        normal_two,
        weight_transit.T,
        weight_down,
        weight_up.T,
    )
    sums = lax.all_to_all(sums, both, 0, 0, tiled=True)

    (wide_parts,) = whole(outer_body, [((16, 160, 512), f32)], "outer")(
        keep_act, keep_hid, keep_t, pack_one, pack_two, core_swap(pack_one), core_swap(pack_two)
    )
    wide_sum = lax.psum_scatter(
        wide_parts, "chan", scatter_dimension=0, axis_index_groups=same_core()
    )

    keep_two, pack_three, dgd, norm_two = whole(
        second_body,
        [((256, 256), bf16), ((1280, 256), bf16), ((512, 256), bf16), ((8, 128), f32)],
        "second",
        scalars=1,
    )(k_scalar, sums, da2, normal_two, factor_two, dx2, weight_two.T, gd, a1)
    grad_mixed = lax.all_to_all(
        dgd.reshape(32, 16, 256), "chan", 0, 0, tiled=True
    ).transpose(1, 0, 2)
    back, taps = whole(
        depth_backward_body,
        [((16, 32, 256), bf16), ((256, 896), f32)],
        "depth_backward",
        scratch=[pltpu.VMEM((16, 256, 512), f32)],
    )(u, mixed, grad_mixed, table, widen, compact)
    du1 = lax.all_to_all(back.transpose(1, 0, 2), "chan", 0, 0, tiled=True).reshape(512, 256)
    taps = taps.reshape(16, 16, 896)
    tap_grad = sum(
        jnp.pad(taps[:, px], ((0, 0), (13 - px, px + 3))) for px in range(S)
    )
    tap_grad = jnp.pad(tap_grad[:, :864], ((0, 0), (0, 160))).reshape(32, 512)
    tap_grad = tap_grad + sum(z_shifts(tap_grad))
    keep_one, send_one, keep_norm, send_norm = whole(
        third_body,
        [((256, 256), bf16), ((256, 256), bf16), ((16, 128), f32), ((16, 128), f32)],
        "third",
        scalars=1,
    )(k_scalar, came, du1, slope_one, came[:, 256:].T)
    (narrow_parts,) = whole(last_outer_body, [((16, 40, 512), f32)], "last_outer")(
        keep_one,
        keep_two,
        pack_three,
        core_swap(send_one),
        core_swap(pack_three),
        keep_norm,
        core_swap(send_norm),
    )
    narrow_sum = jnp.sum(groups_all_to_all(narrow_parts), axis=0)
    parts = jnp.concatenate([wide_sum, narrow_sum], axis=0)

    norm_two_own = lax.dynamic_slice_in_dim(norm_two.reshape(2, 512), c * 16, 16, 1)
    line = jnp.concatenate([scale_own, jnp.ones((16,), f32), jnp.zeros((96,), f32)])
    scale_line = jnp.broadcast_to(line[None], (8, 128))
    grads, near, norm_one, message = whole(
        gather_body,
        [((192, 512), f32), ((64, 512), f32), ((8, 128), f32), ((16, 80, 512), bf16)],
        "gather",
        scalars=1,
    )(
        z.reshape(1).astype(jnp.int32),
        parts,
        *z_shifts(parts),
        tap_grad,
        class_grad,
        head_grad,
        norm_two_own,
        scale_line,
    )
    got = groups_all_to_all(message)
    near_other = core_swap(near)
    near_rows, scalars = whole(
        muon_body,
        [((128, 512), f32), ((8, 128), f32)],
        "muon",
        scratch=[pltpu.VMEM((2048, 512), bf16)],
        scalars=1,
    )(
        jnp.stack([z, k]).astype(jnp.int32),
        got,
        core_swap(got),
        own[:, 240:],
        other[:, 240:],
        near,
        near_other,
        near_moment,
        near_moment_other,
    )
    grad_norm, factor = scalars[0, 0], scalars[0, 1]
    row = np.arange(64)
    first_rows = jnp.asarray((row < 16).astype(np.float32))
    second_rows = jnp.asarray(((row >= 16) & (row < 32)).astype(np.float32))
    own_rows = jnp.where(z < 3, 1.0, jnp.where(k == 0, first_rows, second_rows))[:, None]
    mine_result = jnp.where(own_rows > 0, near_rows[:64], core_swap(near_rows[64:]))
    results = z_gather(mine_result)
    directions = [
        results[0],
        results[1],
        results[2, :32],
        results[3, :16],
        results[3, 16:32],
    ]
    fresh = momentum_decay * moments_t + grads * factor
    starts = [0, 64, 128, 160, 176, 192]
    order = [3, 4, 0, 1, 2]
    matrices = (point_one, point_two, expand, shrink, transit)
    renewed = []
    fresh_out = []
    for index in range(5):
        weight = matrices[index]
        at = order[index]
        factor_muon = 0.2 * math.sqrt(max(weight.shape[0], weight.shape[1] * 32))
        renewed.append(
            weight * (1.0 - muon_rate * weight_decay)
            - muon_rate * factor_muon * directions[at].T
        )
        fresh_out.append(fresh[starts[at] : starts[at + 1]].T)
    class_grad = class_grad[:, :classes]
    big_grad = tap_grad.reshape(16, 1024)[:, :864].reshape(16, TAPS, 32)[:, :, :TAPS]
    big_grad = jnp.pad(big_grad, ((0, 0), (2, 2), (2, 2)))
    small_grad = big_grad[:, margin : margin + KS, margin : margin + KS]
    norm_grad = jnp.concatenate([norm_one[0, :32].reshape(2, 16), norm_two_own], axis=0)
    head_out = adamw(classifier, classifier_first, classifier_second, class_grad * factor, adam_rate)
    big_out = adamw(big_kernel, big_first, big_second, big_grad * factor, adam_rate)
    small_out = adamw(small_kernel, small_first, small_second, small_grad * factor, adam_rate)
    norm_out = adamw(norm_gains, gains_first, gains_second, norm_grad * factor, norm_rate)
    hnorm_out = adamw(
        head_gains, head_first, head_second, head_grad[:2, :32] * factor, norm_rate
    )
    return (
        losses[0, 0],
        losses[0, 1],
        grad_norm,
        renewed[0],
        fresh_out[0],
        renewed[1],
        fresh_out[1],
        renewed[2],
        fresh_out[2],
        renewed[3],
        fresh_out[3],
        renewed[4],
        fresh_out[4],
        *head_out,
        *big_out,
        *small_out,
        *norm_out,
        *hnorm_out,
    )


def solution(mesh):
    split_columns = P(None, "chan")
    split_rows = P("chan", None)
    split_first = P("chan", None, None)
    in_specs = (
        (P("chan", "batch", None), P("batch"), P("batch"), P())
        + (split_columns,) * 10
        + (split_rows,) * 3
        + (split_first,) * 6
        + (split_columns,) * 6
    )
    out_specs = (
        (P(), P(), P())
        + (split_columns,) * 10
        + (split_rows,) * 3
        + (split_first,) * 6
        + (split_columns,) * 6
    )
    return jax.shard_map(shards, mesh=mesh, in_specs=in_specs, out_specs=out_specs, check_vma=False)
```

```python
import math

import jax
import jax.numpy as jnp
import numpy as np
from jax import lax
from jax.experimental import pallas as pl
from jax.experimental.pallas import tpu as pltpu
from jax.sharding import PartitionSpec as P

S = 14
KB = 31
KS = 5
NS_STEPS = 5
STEP = 10
AREA = S * S
WIDE = S * 16
TAPS = 2 * S - 1

f32 = jnp.float32
bf16 = jnp.bfloat16
epsilon = 1e-05
highest = lax.Precision.HIGHEST
coef_first = 3.4445
coef_second = -4.775
coef_third = 2.0315
clip_limit = 0.05
momentum_decay = 0.95
muon_rate = 0.05
adam_rate = 0.05
norm_rate = 0.2
beta_first = 0.9
beta_second = 0.95
weight_decay = 0.01
root_two_pi = math.sqrt(2.0 / math.pi)
both = ("batch", "chan")
BACK = 25
SMALL = 0
PLACES = ((160, 16), (176, 16), (0, 64), (64, 64), (128, 32))


def dot(a, b, left=1, right=0, precision=None):
    return lax.dot_general(
        a, b, (((left,), (right,)), ((), ())), precision=precision, preferred_element_type=f32
    )


def gelu_pair(x):
    square = x * x
    t = jnp.tanh(root_two_pi * x * (1.0 + 0.044715 * square))
    half = 0.5 * (1.0 + t)
    slope = half + 0.5 * x * (1.0 - t * t) * (root_two_pi * (1.0 + 0.134145 * square))
    return x * half, slope


def three(x):
    high = lax.reduce_precision(x, 8, 7)
    rest = x - high
    mid = lax.reduce_precision(rest, 8, 7)
    return [high.astype(bf16), mid.astype(bf16), (rest - mid).astype(bf16)]


def core_swap(x):
    return lax.ppermute(x, "chan", [(i, i ^ 1) for i in range(32)])


def same_core():
    return [[2 * i + k for i in range(16)] for k in range(2)]


def z_shifts(x):
    return [lax.ppermute(x, "batch", [(i, (i + k) % 4) for i in range(4)]) for k in range(1, 4)]


def groups_all_to_all(x):
    return lax.all_to_all(x, "chan", 0, 0, tiled=True, axis_index_groups=same_core())


def z_pair(x):
    return lax.ppermute(x, "batch", [(0, 1), (1, 0), (2, 3), (3, 2)])


def z_cross(x):
    return lax.ppermute(x, "batch", [(0, 3), (3, 0), (1, 2), (2, 1)])


def z_gather_rows(x):
    z = lax.axis_index("batch")
    near = z_pair(x)
    far = z_cross(jnp.concatenate([x, near], axis=0))
    rows = []
    for j in range(4):
        at = jnp.bitwise_xor(z, j)
        cross = jnp.where(j == 3 - z, far[0:1], far[1:2])
        rows.append(jnp.where(at == 0, x, jnp.where(at == 1, near, cross)))
    return jnp.concatenate(rows, axis=0)


def widen_matrix():
    e = np.zeros((256, 256), np.float32)
    for y in range(S):
        for x in range(S):
            e[y * S + x, y * 16 + x] = 1
    return jnp.asarray(e, bf16)


def compact_matrix():
    e = np.zeros((896, 512), np.float32)
    for f in range(TAPS):
        for x in range(S):
            e[f * 32 + x, f * S + x] = 1
    return jnp.asarray(e, bf16)


class Source:
    def __init__(self, buffer, copies):
        self.buffer = buffer
        self.copies = copies

    def ready(self):
        for copy in self.copies:
            copy.wait()
        self.copies = []

    def __getitem__(self, index):
        self.ready()
        return self.buffer[index]


class Target:
    def __init__(self, buffer, copies):
        self.buffer = buffer
        self.copies = copies
        self.sent = set()

    def __getitem__(self, index):
        return self.buffer[index]

    def __setitem__(self, index, value):
        self.buffer[index] = value

    @property
    def shape(self):
        return self.buffer.shape

    def send(self, part=None):
        for j in range(len(self.copies)):
            if j not in self.sent and part in (None, j):
                self.copies[j].start()
                self.sent.add(j)

    def finish(self):
        for copy in self.copies:
            copy.wait()


def whole(
    body, outs, name, scratch=(), scalars=0, limit=54, pieces=None, cost=2, small_in=SMALL, small_out=SMALL,
    parts=None, scalar_outs=0,
):
    pieces = pieces or {}
    parts = parts or {}

    def call(*args):
        arrays = args[scalars:]
        loads = []
        for i, array in enumerate(arrays):
            for load in pieces.get(i, [None]):
                loads.append((i, load))
        sizes = [array.size * array.dtype.itemsize for array in arrays]
        direct = [i not in pieces and sizes[i] <= small_in for i in range(len(arrays))]
        out_sizes = [math.prod(shape) * jnp.dtype(kind).itemsize for shape, kind in outs]
        direct_out = [size <= small_out for size in out_sizes]
        direct_out += [True] * scalar_outs
        moved = [(i, load) for i, load in loads if not direct[i]]
        moved_out = [item for item, near in zip(outs, direct_out) if not near]
        n_out_copies = sum(
            len(parts.get(j, [None])) for j, near in enumerate(direct_out) if not near
        )
        n_results = len(outs) + scalar_outs
        buffers = [
            pltpu.VMEM(arrays[i].shape if load is None else load[0], arrays[i].dtype)
            for i, load in moved
        ]
        n_copies = sum(1 if load is None else load[2] for _, load in moved)
        n_in, n_load, n_out, n_moved = len(arrays), len(moved), len(outs), len(moved_out)

        def kernel(*refs):
            small = refs[:scalars]
            refs = refs[scalars:]
            ins, refs = refs[:n_in], refs[n_in:]
            results, refs = refs[:n_results], refs[n_results:]
            in_buffers, refs = list(refs[:n_load]), refs[n_load:]
            out_buffers, refs = list(refs[:n_moved]), refs[n_moved:]
            in_sems, out_sems, rest = refs[0], refs[1], refs[2:]
            count = 0
            sources = []
            for i, load in loads:
                if direct[i]:
                    sources.append(Source(ins[i], []))
                    continue
                buffer = in_buffers.pop(0)
                ways = [(ins[i], buffer)] if load is None else load[1](ins[i], buffer, small)
                copies = []
                for origin, to in ways:
                    copy = pltpu.make_async_copy(origin, to, in_sems.at[count])
                    copy.start()
                    copies.append(copy)
                    count += 1
                sources.append(Source(buffer, copies))
            targets = []
            count = 0
            for j, (result, near) in enumerate(zip(results, direct_out)):
                if near:
                    targets.append(Target(result, []))
                    continue
                buffer = out_buffers.pop(0)
                copies = []
                for part in parts.get(j, [None]):
                    origin, to = buffer, result
                    if part is not None:
                        origin, to = buffer.at[part], result.at[part]
                    copies.append(pltpu.make_async_copy(origin, to, out_sems.at[count]))
                    count += 1
                targets.append(Target(buffer, copies))
            body(*small, *sources, *targets, *rest)
            for source in sources:
                source.ready()
            for target in targets:
                target.send()
            for target in targets:
                target.finish()

        near_space = pl.BlockSpec(memory_space=pltpu.VMEM)
        far_space = pl.BlockSpec(memory_space=pl.ANY)
        return pl.pallas_call(
            kernel,
            out_shape=[jax.ShapeDtypeStruct(*item) for item in outs]
            + [jax.ShapeDtypeStruct((1, 1), f32)] * scalar_outs,
            in_specs=[pl.BlockSpec(memory_space=pltpu.SMEM)] * scalars
            + [near_space if near else far_space for near in direct],
            out_specs=[near_space if near else far_space for near in direct_out[:n_out]]
            + [pl.BlockSpec(memory_space=pltpu.SMEM)] * scalar_outs,
            scratch_shapes=buffers
            + [pltpu.VMEM(*item) for item in moved_out]
            + [
                pltpu.SemaphoreType.DMA((max(n_copies, 1),)),
                pltpu.SemaphoreType.DMA((max(n_out_copies, 1),)),
            ]
            + list(scratch),
            name=name,
            cost_estimate=pl.CostEstimate(
                flops=cost * 1_000_000_000, bytes_accessed=0, transcendentals=0
            ),
            compiler_params=pltpu.CompilerParams(vmem_limit_bytes=limit * 1024 * 1024),
        )(*args)

    return call


def own_first(start, rows):
    def ways(origin, to, small):
        k = small[0][0]
        part = pl.ds(start, rows)
        return [(origin.at[:, k, part, :], to.at[0]), (origin.at[:, 1 - k, part, :], to.at[1])]

    return ((2, 16, rows, 512), ways, 2)


def by_core(start, rows):
    def ways(origin, to, small):
        part = pl.ds(start, rows)
        return [(origin.at[:, 0, part, :], to.at[0]), (origin.at[:, 1, part, :], to.at[1])]

    return ((2, 16, rows, 512), ways, 2)


def natural(start, rows):
    def ways(origin, to, small):
        return [(origin.at[:, :, pl.ds(start, rows), :], to)]

    return ((16, 2, rows, 512), ways, 1)


def block(ref, half, i, rows):
    n = 256 // rows
    return ref[half, i * n : (i + 1) * n].reshape(256, 512)


def half_of(ref, half, rows):
    return ref[half].reshape(16 * rows, 512)


def valid(rows):
    return lax.broadcasted_iota(jnp.int32, (rows, 256), 1) < AREA


def column(tail, i):
    at = AREA - 128 + 3 * i
    return (tail[:, at : at + 1] + tail[:, at + 1 : at + 2]) + tail[:, at + 2 : at + 3]


def row_sums(x):
    return dot(jnp.ones((8, x.shape[1]), f32), x, 1, 1, highest)[0:1]


def pack_row(row):
    return jnp.concatenate([row[:, j * 128 : (j + 1) * 128] for j in range(8)], axis=0)


def as_columns(packed):
    rows = lax.broadcasted_iota(jnp.int32, (8, 128), 0)
    lanes = lax.broadcasted_iota(jnp.int32, (8, 128), 1)
    turned = dot(packed, (rows == lanes).astype(f32), 0, 0, highest)
    return [
        jnp.concatenate([turned[:, j : j + 1] for j in range(4 * h, 4 * h + 4)], axis=0)
        for h in range(2)
    ]


def by_turn(k, rows):
    four = rows.reshape(16, 2, 16, 256)
    first, second = four[:, 0].reshape(256, 256), four[:, 1].reshape(256, 256)
    return jnp.where(k == 0, first, second), jnp.where(k == 0, second, first)


def pack_body(z, two, up, down, transit, classes, m_up, m_down, m_transit, m_one, m_two, line, packed, late, near):
    packed[0:16, :] = two[...].astype(bf16)
    packed[16:80, :] = up[...].astype(bf16)
    packed[80:144, :] = down[...].astype(bf16)
    packed[144:176, :] = transit[...].astype(bf16)
    late[0:32, :] = classes[:, 0:512].astype(bf16)
    late[32:64, :] = jnp.concatenate(
        [classes[:, 512:1000], jnp.zeros((32, 24), f32)], axis=1
    ).astype(bf16)
    rows = jnp.concatenate([m_up[...], m_down[...], m_transit[...], m_one[...], m_two[...]], axis=0)
    mine = pick(z[0], rows)
    near[...] = mine
    near.send()
    late[64:128, :] = mine.astype(bf16)
    late[128:144, :] = jnp.concatenate([line[...], jnp.zeros((15, 512), f32)], axis=0).astype(bf16)


def taps_body(shifted, compact, table):
    z = dot(shifted[...], compact[...])
    keep = valid(256)
    for py in range(S):
        at = (S - 1 - py) * S
        rows = jnp.where(keep, z[:, at : at + 256], 0.0).astype(bf16)
        table[:, py * 16 : (py + 1) * 16, :] = rows.reshape(16, 16, 256)
    table[:, WIDE:, :] = jnp.zeros((16, 256 - WIDE, 256), bf16)


def first_body(came, act, slope, normed):
    tail = came[:, 128:256].astype(f32)
    x = came[:, :256].astype(f32) - column(tail, 0)
    a = jnp.where(valid(512), x * column(tail, 1) + column(tail, 2), 0.0).astype(bf16)
    normed[...] = a
    for i in range(2):
        rows = pl.ds(i * 256, 256)
        value, back = gelu_pair(dot(came[rows, 256:768], a))
        act[rows, :] = value.astype(bf16)
        slope[rows, :] = back


def depth_forward_body(u, table, widen, mixed, act):
    for c in range(16):
        wide = dot(u[c], widen[...]).astype(bf16)
        d = dot(wide, table[c])
        mixed[c] = d
        act[c] = gelu_pair(d)[0].astype(bf16)


def middle_body(came, gd, weight, middle, stats):
    weight = weight[...].reshape(512, 512)
    keep = valid(512)
    x = jnp.where(keep, came[:, :256].astype(f32), 0.0) + dot(weight, gd[...])
    middle[...] = x
    middle.send()
    mean = jnp.sum(x, axis=1, keepdims=True) * (1.0 / AREA)
    apart = jnp.where(keep, x - mean, 0.0)
    row = jnp.concatenate([row_sums(x), row_sums(apart * apart)], axis=1) * (1.0 / AREA)
    stats[...] = jnp.broadcast_to(pack_row(row)[None], (128, 8, 128))


def forward_body(
    k, came, middle, stats, up, down, transit, normal, factor, pack, keep_act, slope_hid, slope_t, pooled
):
    tail = came[:, 128:256].astype(f32)
    parts = stats[...]
    total = jnp.sum(parts, axis=0) * (1.0 / 128)
    apart = parts - total[None]
    spread = jnp.sum(apart * apart, axis=0) * (1.0 / 128)
    both_cols = as_columns(total)
    center = both_cols[0]
    variance = both_cols[1] + as_columns(spread)[0]
    scale = lax.rsqrt(variance + epsilon)
    gain = column(tail, 3)
    x1 = middle[...]
    xh = (x1 - center) * scale
    keep = valid(512)
    normal[...] = jnp.where(keep, xh, 0.0)
    normal.send()
    factor[...] = jnp.broadcast_to(gain * scale, (512, 128))
    factor.send()
    a2 = jnp.where(keep, xh * gain + column(tail, 4), 0.0).astype(bf16)
    pack[1536:2048, :] = a2
    for i in range(8):
        rows = pl.ds(i * 256, 256)
        value, back = gelu_pair(dot(block(up, i // 4, i % 4, 64), a2))
        low = value.astype(bf16)
        slope_hid[rows, :] = back
        if i < 4:
            keep_act[rows, :] = low
        else:
            pack[(i - 4) * 256 : (i - 3) * 256, :] = low
    slope_hid.send()
    keep_act.send()
    total = x1 + dot(half_of(down, 0, 64), keep_act[...], 0, 0)
    total = total + dot(half_of(down, 1, 64), pack[:1024, :], 0, 0)
    x2 = total.astype(bf16)
    pack[1024:1536, :] = x2
    pack.send()
    halves = []
    for i in range(2):
        rows = pl.ds(i * 512, 512)
        value, back = gelu_pair(dot(half_of(transit, i, 32), x2))
        slope_t[rows, :] = jnp.where(keep, back, 0.0)
        halves.append(row_sums(value) * (1.0 / AREA))
    slope_t.send()
    turn = k[0] == 1
    row = jnp.concatenate(
        [jnp.where(turn, halves[1], halves[0]), jnp.where(turn, halves[0], halves[1])], axis=1
    )
    pooled[...] = jnp.broadcast_to(pack_row(row)[None], (128, 8, 128))


def head_body(
    place,
    pooled,
    people,
    class_weight,
    gains,
    classes,
    transit,
    down,
    up,
    slope_t,
    slope_hid,
    normal,
    pack,
    keep_hid,
    keep_t,
    dx2,
    da2,
    sums,
    class_grad,
    head_grad,
    loss_out,
    weight_out,
):
    k, crop, at = place[0], place[1], place[2]
    owner_rows = gains[:, :, 0:8, :].reshape(32, 8, 512)[:, 0, :].astype(f32)
    fold_rows = lax.broadcasted_iota(jnp.int32, (32, 1024), 0)
    fold_lanes = lax.broadcasted_iota(jnp.int32, (32, 1024), 1)
    expand = (fold_lanes % 32 == fold_rows).astype(f32)
    keep = fold_lanes // 32 == fold_rows

    def gain_row(i):
        at_lane = 128 * i
        parts = [owner_rows[:, at_lane + 32 * j : at_lane + 32 * j + 32] for j in range(3)]
        parts = jnp.concatenate([(parts[0] + parts[1]) + parts[2], jnp.zeros((32, 96), f32)], axis=1)
        full = jnp.concatenate([expand, jnp.zeros((96, 1024), f32)], axis=0)
        spread = dot(parts, full, 1, 0, highest)
        return jnp.sum(jnp.where(keep, spread, 0.0), axis=0, keepdims=True)

    gain = gain_row(0)
    shift = gain_row(1)
    x = jnp.concatenate([pooled[:, j, :] for j in range(8)], axis=1)
    center = jnp.sum(x, axis=0, keepdims=True) * (1.0 / 128)
    apart = x - center
    scale = lax.rsqrt(jnp.sum(apart * apart, axis=0, keepdims=True) * (1.0 / 128) + epsilon)
    xh = apart * scale
    z = (xh * gain + shift).astype(bf16)
    left = classes[:, :, 0:32].reshape(1024, 512)
    right = classes[:, :, 32:64].reshape(1024, 512)
    logits = jnp.concatenate([dot(z, left), dot(z, right)], axis=1)
    lanes = lax.broadcasted_iota(jnp.int32, (128, 128), 1)
    rows = lax.broadcasted_iota(jnp.int32, (128, 128), 0)
    pairing = (people[:, 1:2] == lanes.astype(f32)).astype(f32)
    average = 0.5 * (logits + dot(pairing, logits, 1, 0, highest))
    wide = lax.broadcasted_iota(jnp.int32, (128, 1024), 1)
    average = jnp.where(wide < 1000, average, -1e30)
    top = jnp.max(average, axis=1, keepdims=True)
    moved = average - top
    expo = jnp.exp(moved)
    norm = jnp.sum(expo, axis=1, keepdims=True)
    onehot = (people[:, 0:1] == wide.astype(f32)).astype(f32)
    weight = 0.5 * jnp.sum(onehot * class_weight[...], axis=1, keepdims=True)
    picked = jnp.sum(jnp.where(onehot > 0, moved, 0.0), axis=1, keepdims=True) - jnp.log(norm)
    weight_sum = jnp.sum(weight, axis=0, keepdims=True)
    loss_sum = -jnp.sum(weight * picked, axis=0, keepdims=True)
    loss_out[0, 0] = loss_sum[0, 0]
    weight_out[0, 0] = weight_sum[0, 0]
    dl = ((weight / weight_sum) * (expo / norm - onehot)).astype(bf16)
    dz = dot(dl[:, :512], left, 1, 1) + dot(dl[:, 512:], right, 1, 1)
    dshift = jnp.sum(dz, axis=0, keepdims=True)
    dgain = jnp.sum(dz * xh, axis=0, keepdims=True)
    dp = (gain * scale) * (dz - (dshift + xh * dgain) * (1.0 / 128))
    mine = dot(dp, (rows == crop).astype(f32), 0, 0, highest)[:, 0:1] * (1.0 / AREA)
    turn = k == 1
    first = jnp.where(turn, mine[512:], mine[:512])
    second = jnp.where(turn, mine[:512], mine[512:])

    keep_t[...] = (slope_t[:512, :] * first).astype(bf16)
    keep_t.send()
    pack[1024:1536, :] = (slope_t[512:, :] * second).astype(bf16)
    grad = dot(half_of(transit, 0, 32), keep_t[...], 0, 0)
    grad = grad + dot(half_of(transit, 1, 32), pack[1024:1536, :], 0, 0)
    dx2[...] = grad
    dx2.send()
    low = grad.astype(bf16)
    pack[1536:2048, :] = low
    for i in range(8):
        rows256 = pl.ds(i * 256, 256)
        part = (slope_hid[rows256, :] * dot(block(down, i // 4, i % 4, 64), low)).astype(bf16)
        if i < 4:
            keep_hid[rows256, :] = part
        else:
            pack[(i - 4) * 256 : (i - 3) * 256, :] = part
    pack.send()
    keep_hid.send()
    grad = dot(half_of(up, 0, 64), keep_hid[...], 0, 0)
    grad = grad + dot(half_of(up, 1, 64), pack[:1024, :], 0, 0)
    da2[...] = grad
    da2.send()
    row = jnp.concatenate([row_sums(grad * normal[...]), row_sums(grad)], axis=1)
    sums[...] = jnp.broadcast_to(pack_row(row)[None], (128, 8, 128))
    sums.send()
    own_rows = lax.broadcasted_iota(jnp.int32, (1024, 128), 0)
    own_lanes = lax.broadcasted_iota(jnp.int32, (1024, 128), 1)
    select = ((own_rows == own_lanes + at) & (own_lanes < 32)).astype(f32)
    z_own = dot(z, select.astype(bf16)).astype(bf16)
    class_grad[...] = dot(z_own, dl, 0, 0)[:32]
    both_rows = jnp.concatenate([dgain, dshift, jnp.zeros((6, 1024), f32)], axis=0)
    head_grad[...] = dot(both_rows, select, 1, 0, highest)


def outer_body(keep_act, keep_hid, keep_t, one, two, one_in, two_in, result):
    def product(rows, v, rows_in, v_in):
        return dot(rows, v, 1, 1) + dot(rows_in, v_in, 1, 1)

    def place(part, rows, v, rows_in, v_in, n):
        for i in range(2):
            half = slice(i * 8 * n, (i + 1) * 8 * n)
            block_rows = product(rows[half], v, rows_in[half], v_in)
            result[i * 8 : (i + 1) * 8, part, :] = block_rows.reshape(8, n, 512)

    place(slice(64, 128), keep_act[...], two[1536:2048], one_in[0:1024], two_in[1536:2048], 64)
    result.send(0)
    place(slice(0, 64), keep_hid[...], one[1536:2048], two_in[0:1024], one_in[1536:2048], 64)
    result.send(1)
    place(slice(128, 160), keep_t[...], one[1024:1536], two_in[1024:1536], one_in[1024:1536], 32)
    result.send(2)


def second_body(k, sums, da2, normal, factor, dx2, weight, gd, normed, keep_rows, pack, back, norm):
    total = jnp.sum(sums[...], axis=0)
    norm[...] = total
    gain, shift = as_columns(total)
    inner = da2[...] - (shift + normal[...] * gain) * (1.0 / (128 * AREA))
    grad = dx2[...] + jnp.where(valid(512), factor[:, 0:1] * inner, 0.0)
    low = grad.astype(bf16)
    keep, send = by_turn(k[0], low)
    keep_rows[...] = keep
    pack[0:256, :] = send
    pack[256:768, :] = gd[...]
    pack[768:1280, :] = normed[...]
    back[...] = dot(weight[...].reshape(512, 512), low, 0, 0).astype(bf16)


def depth_backward_body(u, mixed, grad, table, widen, compact, back, taps, outer):
    outer[...] = jnp.zeros_like(outer)
    for c in range(16):
        wide = dot(u[c], widen[...]).astype(bf16)
        slope = gelu_pair(mixed[c])[1]
        dd = (grad[c].astype(f32) * slope).astype(bf16)
        du = dot(dd, table[c], 1, 1).astype(bf16)
        back[c] = dot(du, widen[...], 1, 1).astype(bf16)
        outer[c, :, :256] = dot(wide, dd, 0, 0)
    total = jnp.zeros((256, 512), f32)
    for py in range(S):
        rows = outer[:, py * 16 : (py + 1) * 16, :].reshape(256, 512)
        at = (S - 1 - py) * S
        total = total + (pltpu.roll(rows, at, 1) if at else rows)
    taps[...] = dot(total, compact[...].astype(f32), 1, 1, highest)


def third_body(
    k, came, du, slope, tap, tap_one, tap_two, tap_three, keep_rows, send_rows, keep_norm, send_norm, tap_sum
):
    tap_sum[...] = (tap[...] + tap_one[...]) + (tap_two[...] + tap_three[...])
    tail = came[:, 128:256].astype(f32)
    dh = (slope[...] * du[...].astype(f32)).astype(bf16)
    keep, send = by_turn(k[0], dh)
    keep_rows[...] = keep
    send_rows[...] = send
    da = dot(came[:, 256:768], dh, 0, 0)
    x = came[:, :256].astype(f32) - column(tail, 0)
    gain, shift = row_sums(da * x), row_sums(da)
    ys = lax.broadcasted_iota(jnp.int32, (16, 512), 0)
    owner = lax.broadcasted_iota(jnp.int32, (16, 512), 1) // 16
    fold_rows = lax.broadcasted_iota(jnp.int32, (512, 128), 0) % 16
    fold_lanes = lax.broadcasted_iota(jnp.int32, (512, 128), 1)
    fold_gain = (fold_rows == fold_lanes).astype(f32)
    fold_shift = (fold_rows == fold_lanes - 16).astype(f32)

    def part(core):
        own = owner == 2 * ys + core
        return dot(jnp.where(own, gain, 0.0), fold_gain, 1, 0, highest) + dot(
            jnp.where(own, shift, 0.0), fold_shift, 1, 0, highest
        )

    keep_norm[...] = part(k[0])
    send_norm[...] = part(1 - k[0])


def last_outer_body(keep_one, keep_two, pack, got_one, got_pack, keep_norm, got_norm, result):
    one = dot(keep_one[...], pack[768:1280, :], 1, 1) + dot(
        got_one[...], got_pack[768:1280, :], 1, 1
    )
    two = dot(keep_two[...], pack[256:768, :], 1, 1) + dot(
        got_pack[0:256, :], got_pack[256:768, :], 1, 1
    )
    result[:, 0:16, :] = one.reshape(16, 16, 512)
    result[:, 16:32, :] = two.reshape(16, 16, 512)
    result[:, 32:40, :] = jnp.zeros((16, 8, 512), f32)
    result[:, 32:33, 0:128] = (keep_norm[...] + got_norm[...]).reshape(16, 1, 128)


def pick(z, rows):
    blank = jnp.zeros((32, 512), f32)
    third = jnp.concatenate([rows[128:160], blank], axis=0)
    fourth = jnp.concatenate([rows[160:192], blank], axis=0)
    return jnp.where(
        z == 0, rows[0:64], jnp.where(z == 1, rows[64:128], jnp.where(z == 2, third, fourth))
    )


def everything(x):
    return jnp.sum(jnp.sum(x, axis=1, keepdims=True), axis=0, keepdims=True)


def reduce_body(
    parts, wide, wide_one, wide_two, wide_three, big_grad, small_grad, class_grad, head_grad, norm_two,
    narrow, mine, squares,
):
    sums = (wide[...] + wide_one[...]) + (wide_two[...] + wide_three[...])
    mine[...] = sums
    square = everything(class_grad[...] * class_grad[...])
    square = square + everything(jnp.sum(big_grad[...] * big_grad[...], axis=0))
    square = square + everything(jnp.sum(small_grad[...] * small_grad[...], axis=0))
    square = square + everything(head_grad[...] * head_grad[...])
    square = square + everything(norm_two[...] * norm_two[...])
    squares[...] = jnp.broadcast_to(square, (8, 128))
    narrow[0:40, :] = jnp.sum(parts[...], axis=0)
    narrow[40:48, :] = jnp.broadcast_to(everything(sums * sums), (8, 512))


def gather_body(
    z, wide, squares, narrow, narrow_other, scale, near, norm_one, message,
):
    rest = narrow[...] + narrow_other[...]
    last = rest[:32]
    norm = rest[32:40, 0:128] * scale[...]
    norm_one[...] = norm
    square = squares[0:1, 0:1] + rest[40:41, 0:1] + everything(last * last) + everything(norm * norm)
    mine = jnp.where(z[0] == 3, jnp.concatenate([last, jnp.zeros((32, 512), f32)], axis=0), wide[...])
    near[...] = mine
    near.send()
    high = square.astype(bf16)
    rest = square - high.astype(f32)
    mid = rest.astype(bf16)
    low = (rest - mid.astype(f32)).astype(bf16)
    rows16 = lax.broadcasted_iota(jnp.int32, (16, 512), 0)
    lanes16 = lax.broadcasted_iota(jnp.int32, (16, 512), 1)
    tail = jnp.where(
        lanes16 == 0,
        high.astype(f32),
        jnp.where(lanes16 == 1, mid.astype(f32), jnp.where(lanes16 == 2, low.astype(f32), 0.0)),
    )
    tail = jnp.where(rows16 == 0, tail, 0.0)
    line = jnp.concatenate([mine, tail], axis=0).astype(bf16)
    message[...] = jnp.broadcast_to(line[None], (16, 80, 512))


def split(x):
    high = x.astype(bf16)
    return high, (x - high.astype(f32)).astype(bf16)


def mul3(a, b):
    return dot(a[0], b[0]) + (dot(a[0], b[1]) + dot(a[1], b[0]))


def muon_body(
    place, got, got_other, moment, near, near_other, near_moment, near_moment_other,
    result, result_other, scalars, norm_out, u,
):
    k, z = place[0], place[1]

    def tails(ref):
        x = ref[:, 64:80, :].astype(f32)
        return jnp.sum(jnp.sum(x, axis=0), axis=0, keepdims=True)

    square = jnp.sum(tails(got) + tails(got_other), axis=1, keepdims=True)
    norm = jnp.sqrt(square)
    f = jnp.minimum(1.0, clip_limit / (norm + 1e-06))
    line = lax.broadcasted_iota(jnp.int32, (8, 128), 1)
    scalars[...] = jnp.where(line == 0, norm, f)
    norm_out[0, 0] = norm[0, 0]
    scalars.send()
    alpha = (1.0 + momentum_decay) * f
    beta = momentum_decay * momentum_decay
    low = jnp.where(z == 3, k * 16, 0)
    high = jnp.where(z == 3, k * 16 + 16, 64)
    for i, g in enumerate((got, got_other)):
        for y in range(0, 16, 4):
            rows = lax.broadcasted_iota(jnp.int32, (4, 64, 512), 1)
            value = alpha * g[y : y + 4, :64, :].astype(f32)
            value = value + beta * moment[i, y : y + 4].astype(f32)
            value = jnp.where((rows >= low) & (rows < high), value, 0.0).astype(bf16)
            at = i * 1024 + y * 64
            u[at : at + 256, :] = value.reshape(256, 512)
    gram = dot(u[...], u[...], 0, 0)
    rows = lax.broadcasted_iota(jnp.int32, (512, 512), 0)
    cols = lax.broadcasted_iota(jnp.int32, (512, 512), 1)
    eye = (rows == cols).astype(f32)
    total = jnp.sum(jnp.sum(gram * eye, axis=0, keepdims=True), axis=1, keepdims=True)
    inverse = 1.0 / (jnp.sqrt(total) + 1e-07)
    a = gram * (inverse * inverse)
    x = jnp.concatenate(
        [
            (alpha * near[...] + beta * near_moment[...]) * inverse,
            (alpha * near_other[...] + beta * near_moment_other[...]) * inverse,
        ],
        axis=0,
    )
    for step in range(NS_STEPS):
        a2 = split(a)
        square = mul3(a2, a2)
        m2 = split(coef_first * eye + coef_second * a + coef_third * square)
        x = mul3(split(x), m2)
        if step < NS_STEPS - 1:
            a = mul3(split(mul3(a2, m2)), m2)
    result[...] = x[:64]
    result_other[...] = x[64:]


def adamw(weight, first, second, gradient, rate):
    first = beta_first * first + (1.0 - beta_first) * gradient
    second = beta_second * second + (1.0 - beta_second) * gradient * gradient
    ratio = (
        first / (1.0 - beta_first**STEP) / (jnp.sqrt(second / (1.0 - beta_second**STEP)) + 1e-08)
    )
    return (first, second, weight - rate * (ratio + weight_decay * weight))


def by_matrix(z, got):
    group = []
    for j in range(4):
        back = lax.rem(z - j + 4, 4)
        group.append(
            jnp.where(
                back == 0,
                got[0],
                jnp.where(back == 1, got[1], jnp.where(back == 2, got[2], got[3])),
            )
        )
    return [group[3][:16], group[3][16:32], group[0], group[1], group[2][:32]]


def finish_body(
    z, scalars, mine, one, two, three_back, class_grad, big_grad, small_grad, norm_one, norm_two, head_grad,
    *refs
):
    moments, refs = refs[:5], refs[5:]
    states, refs = refs[:15], refs[15:]
    fresh, updated = refs[:5], refs[5:]
    f = scalars[0:1, 1:2]
    rows = by_matrix(z[0], [mine[...], one[...], two[...], three_back[...]])
    for moment, row, out in zip(moments, rows, fresh):
        out[...] = momentum_decay * moment[...] + f * row
        out.send()
    norm = norm_one[0:1, :]
    grads = [
        class_grad[:, :1000],
        big_grad[...],
        small_grad[...],
        jnp.concatenate([norm[:, 0:16], norm[:, 16:32], norm_two[...]], axis=0),
        head_grad[0:2, 0:32],
    ]
    rates = [adam_rate, adam_rate, adam_rate, norm_rate, norm_rate]
    for i in range(5):
        factor = f if grads[i].ndim == 2 else f.reshape(1, 1, 1)
        first, second, weight = adamw(
            states[3 * i][...], states[3 * i + 1][...], states[3 * i + 2][...],
            grads[i] * factor, rates[i],
        )
        updated[3 * i][...] = first
        updated[3 * i + 1][...] = second
        updated[3 * i + 2][...] = weight
        for j in range(3):
            updated[3 * i + j].send()


def renew_body(z, mine, one, two, three_back, *refs):
    weights, outs = refs[:5], refs[5:]
    rows = by_matrix(z[0], [mine[...], one[...], two[...], three_back[...]])
    for weight, row, (_, n), out in zip(weights, rows, PLACES, outs):
        rate = muon_rate * 0.2 * math.sqrt(max(512, 32 * n))
        out[...] = weight[...] * (1.0 - muon_rate * weight_decay) - rate * row
        out.send()


def shards(
    features,
    labels,
    partner,
    class_weight,
    point_one,
    momentum_one,
    point_two,
    momentum_two,
    expand,
    momentum_up,
    shrink,
    momentum_down,
    transit,
    momentum_transit,
    classifier,
    classifier_first,
    classifier_second,
    big_kernel,
    big_first,
    big_second,
    small_kernel,
    small_first,
    small_second,
    norm_gains,
    gains_first,
    gains_second,
    head_gains,
    head_first,
    head_second,
):
    z = lax.axis_index("batch")
    c = lax.axis_index("chan")
    k = lax.rem(c, 2)
    crop = z * 32 + c
    widen = widen_matrix()
    compact = compact_matrix()
    k_scalar = k.reshape(1).astype(jnp.int32)
    classes = class_weight.shape[0]

    flat = features.astype(f32)
    local_mean = jnp.mean(flat, axis=(1, 2))
    local_spread = jnp.mean(jnp.square(flat - local_mean[:, None, None]), axis=(1, 2))
    vector = jnp.concatenate(
        [local_mean, local_spread, labels.astype(f32), partner.astype(f32)]
    )[None, :]
    gathered = z_gather_rows(vector)
    means = gathered[:, :16]
    center = jnp.mean(means, axis=0)
    variance = jnp.mean(gathered[:, 16:32], axis=0) + jnp.mean(
        jnp.square(means - center[None]), axis=0
    )
    people = jnp.stack([gathered[:, 32:64].reshape(128), gathered[:, 64:96].reshape(128)], axis=1)
    scale_own = lax.rsqrt(variance + epsilon)

    z_scalar = z.reshape(1).astype(jnp.int32)
    matrices = [w.T for w in (point_one, point_two, expand, shrink, transit)]
    moments = [
        m.T for m in (momentum_one, momentum_two, momentum_up, momentum_down, momentum_transit)
    ]
    head_line = jnp.stack(
        [
            jnp.pad(jnp.concatenate(three(head_gains[i])).astype(f32), (0, 32))
            for i in range(2)
        ]
    ).reshape(1, 256)
    head_line = jnp.pad(head_line, ((0, 0), (0, 256)))
    packed, packed_late, near_moment = whole(
        pack_body,
        [((176, 512), bf16), ((144, 512), bf16), ((64, 512), f32)], "pack", scalars=1, cost=3
    )(
        z_scalar,
        *matrices[1:],
        classifier,
        moments[2],
        moments[3],
        moments[4],
        moments[0],
        moments[1],
        head_line,
    )
    weights = lax.all_gather(packed, "chan", axis=0, tiled=False).reshape(16, 2, 176, 512)
    late_weights = lax.all_gather(packed_late, "chan", axis=0, tiled=False)
    late_weights = late_weights.reshape(16, 2, 144, 512)
    near_moment_other = core_swap(near_moment)

    margin = (KB - KS) // 2
    kernel = big_kernel + jnp.pad(small_kernel, ((0, 0), (margin, margin), (margin, margin)))
    centre = kernel[:, 2:29, 2:29].astype(bf16)
    flat_kernel = jnp.pad(
        jnp.pad(centre, ((0, 0), (0, 0), (0, 5))).reshape(16, TAPS * 32), ((0, 0), (0, 48))
    )
    shifted = jnp.stack(
        [flat_kernel[:, 13 - px : 13 - px + 896] for px in range(S)]
        + [jnp.zeros((16, 896), bf16)] * 2,
        axis=1,
    ).reshape(256, 896)
    (table,) = whole(
        taps_body, [((16, 256, 256), bf16)], "taps", small_out=0
    )(shifted, compact)

    extra = []
    for item in (
        center,
        scale_own * norm_gains[0],
        norm_gains[1],
        norm_gains[2],
        norm_gains[3],
    ):
        extra += three(item)
    extra = jnp.stack(extra, axis=1)
    extra = jnp.pad(extra, ((0, 0), (0, 60 - extra.shape[1])))
    fixed = jnp.concatenate([extra, point_one.T.astype(bf16)], axis=1)
    payload = jnp.concatenate(
        [features.transpose(1, 0, 2), jnp.broadcast_to(fixed[None], (32,) + fixed.shape)], axis=2
    )
    came = lax.all_to_all(payload, "chan", 0, 0, tiled=True).reshape(512, 768)
    act_one, slope_one, a1 = whole(
        first_body, [((512, 256), bf16), ((512, 256), f32), ((512, 256), bf16)], "first", cost=4
    )(came)
    u = lax.all_to_all(act_one.reshape(32, 16, 256), "chan", 0, 0, tiled=True).transpose(1, 0, 2)
    mixed, act = whole(
        depth_forward_body, [((16, 32, 256), f32), ((16, 32, 256), bf16)], "depth_forward", cost=4, small_in=0
    )(u, table, widen)
    gd = lax.all_to_all(act.transpose(1, 0, 2), "chan", 0, 0, tiled=True).reshape(512, 256)

    middle, stats = whole(
        middle_body,
        [((512, 256), f32), ((128, 8, 128), f32)],
        "middle",
        cost=4,
        pieces={2: [natural(0, 16)]},
    )(came, gd, weights)
    stats = lax.all_to_all(stats, both, 0, 0, tiled=True)
    normal_two, factor_two, pack_one, keep_act, slope_hid, slope_t, pooled = whole(
        forward_body,
        [
            ((512, 256), f32),
            ((512, 128), f32),
            ((2048, 256), bf16),
            ((1024, 256), bf16),
            ((2048, 256), f32),
            ((1024, 256), f32),
            ((128, 8, 128), f32),
        ],
        "forward",
        cost=4,
        scalars=1,
        pieces={3: [own_first(16, 64), own_first(80, 64), own_first(144, 32)]},
    )(k_scalar, came, middle, stats, weights)
    pooled = lax.all_to_all(pooled, both, 0, 0, tiled=True)
    place = jnp.stack([k, crop, k * 512 + (c // 2) * 32]).astype(jnp.int32)
    pack_two, keep_hid, keep_t, dx2, da2, sums, class_grad, head_grad, loss_sum, weight_sum = whole(
        head_body,
        [
            ((2048, 256), bf16),
            ((1024, 256), bf16),
            ((512, 256), bf16),
            ((512, 256), f32),
            ((512, 256), f32),
            ((128, 8, 128), f32),
            ((32, 1024), f32),
            ((8, 128), f32),
        ],
        "head",
        scalar_outs=2,
        cost=4,
        scalars=1,
        pieces={
            3: [
                by_core(128, 16),
                by_core(0, 64),
            ],
            4: [
                own_first(144, 32),
                own_first(80, 64),
                own_first(16, 64),
            ]
        },
    )(
        place,
        pooled,
        people,
        jnp.pad(class_weight, (0, 1024 - classes))[None, :],
        late_weights,
        weights,
        slope_t,
        slope_hid,
        normal_two,
    )
    sums = lax.all_to_all(sums, both, 0, 0, tiled=True)

    (wide_parts,) = whole(
        outer_body,
        [((16, 160, 512), f32)],
        "outer",
        parts={0: [np.s_[:, 64:128], np.s_[:, 0:64], np.s_[:, 128:160]]},
    )(
        keep_act, keep_hid, keep_t, pack_one, pack_two, core_swap(pack_one), core_swap(pack_two)
    )
    wide_sum = lax.psum_scatter(
        wide_parts, "chan", scatter_dimension=0, axis_index_groups=same_core()
    )

    keep_two, pack_three, dgd, norm_two = whole(
        second_body,
        [((256, 256), bf16), ((1280, 256), bf16), ((512, 256), bf16), ((8, 128), f32)],
        "second",
        cost=BACK,
        scalars=1,
        pieces={5: [natural(0, 16)]},
    )(k_scalar, sums, da2, normal_two, factor_two, dx2, weights, gd, a1)
    grad_mixed = lax.all_to_all(
        dgd.reshape(32, 16, 256), "chan", 0, 0, tiled=True
    ).transpose(1, 0, 2)
    back, taps = whole(
        depth_backward_body,
        [((16, 32, 256), bf16), ((256, 896), f32)],
        "depth_backward",
        small_in=0,
        cost=BACK,
        scratch=[pltpu.VMEM((16, 256, 512), f32)],
    )(u, mixed, grad_mixed, table, widen, compact)
    du1 = lax.all_to_all(back.transpose(1, 0, 2), "chan", 0, 0, tiled=True).reshape(512, 256)
    taps = taps.reshape(16, 16, 896)
    tap_grad = sum(
        jnp.pad(taps[:, px], ((0, 0), (13 - px, px + 3))) for px in range(S)
    )
    tap_grad = jnp.pad(tap_grad[:, :864], ((0, 0), (0, 160))).reshape(32, 512)
    keep_one, send_one, keep_norm, send_norm, tap_grad = whole(
        third_body,
        [
            ((256, 256), bf16),
            ((256, 256), bf16),
            ((16, 128), f32),
            ((16, 128), f32),
            ((32, 512), f32),
        ],
        "third",
        cost=BACK,
        scalars=1,
    )(k_scalar, came, du1, slope_one, tap_grad, *z_shifts(tap_grad))
    (narrow_parts,) = whole(last_outer_body, [((16, 40, 512), f32)], "last_outer", cost=BACK)(
        keep_one,
        keep_two,
        pack_three,
        core_swap(send_one),
        core_swap(pack_three),
        keep_norm,
        core_swap(send_norm),
    )
    big_grad = tap_grad.reshape(16, 1024)[:, :864].reshape(16, TAPS, 32)[:, :, :TAPS]
    big_grad = jnp.pad(big_grad, ((0, 0), (2, 2), (2, 2)))
    small_grad = big_grad[:, margin : margin + KS, margin : margin + KS].transpose(1, 2, 0)
    big_grad = big_grad.transpose(1, 0, 2)
    norm_two_own = lax.dynamic_slice_in_dim(norm_two.reshape(2, 512), c * 16, 16, 1)
    line = jnp.concatenate([scale_own, jnp.ones((16,), f32), jnp.zeros((96,), f32)])
    scale_line = jnp.broadcast_to(line[None], (8, 128))
    wide_sum = jnp.pad(wide_sum.reshape(160, 512), ((0, 96), (0, 0)))

    def for_group(j):
        return lax.dynamic_slice_in_dim(wide_sum, 64 * lax.rem(z + j, 4), 64, 0)

    narrow_sum, mine_wide, squares = whole(
        reduce_body, [((48, 512), f32), ((64, 512), f32), ((8, 128), f32)], "reduce", cost=4
    )(
        groups_all_to_all(narrow_parts),
        for_group(0),
        *[
            lax.ppermute(for_group(j), "batch", [(i, (i + j) % 4) for i in range(4)])
            for j in range(1, 4)
        ],
        big_grad,
        small_grad,
        class_grad,
        head_grad,
        norm_two_own,
    )
    narrow_sum = narrow_sum + z_pair(narrow_sum)
    near, norm_one, message = whole(
        gather_body,
        [((64, 512), f32), ((8, 128), f32), ((16, 80, 512), bf16)],
        "gather",
        scalars=1,
        cost=4,
    )(z_scalar, mine_wide, squares, narrow_sum, z_cross(narrow_sum), scale_line)
    got = groups_all_to_all(message)
    near_other = core_swap(near)
    near_rows, near_rows_other, scalars, grad_norm = whole(
        muon_body,
        [((64, 512), f32), ((64, 512), f32), ((8, 128), f32)],
        "muon",
        cost=4,
        scratch=[pltpu.VMEM((2048, 512), bf16)],
        scalars=1,
        scalar_outs=1,
        pieces={2: [own_first(64, 64)]},
    )(
        jnp.stack([k, z]).astype(jnp.int32),
        got,
        core_swap(got),
        late_weights,
        near,
        near_other,
        near_moment,
        near_moment_other,
    )
    row = np.arange(64)
    first_rows = jnp.asarray((row < 16).astype(np.float32))
    second_rows = jnp.asarray(((row >= 16) & (row < 32)).astype(np.float32))
    own_rows = jnp.where(z < 3, 1.0, jnp.where(k == 0, first_rows, second_rows))[:, None]
    mine_result = jnp.where(own_rows > 0, near_rows, core_swap(near_rows_other))
    def turn_big(x):
        return x.transpose(1, 0, 2)

    def turn_small(x):
        return x.transpose(1, 2, 0)

    states = [
        *(classifier, classifier_first, classifier_second),
        *(turn_big(x) for x in (big_kernel, big_first, big_second)),
        *(turn_small(x) for x in (small_kernel, small_first, small_second)),
        *(norm_gains, gains_first, gains_second),
        *(head_gains, head_first, head_second),
    ]
    updates = whole(
        finish_body, [(x.shape, f32) for x in moments + states], "finish", scalars=1, cost=6
    )(
        z_scalar,
        scalars,
        near,
        *z_shifts(near),
        class_grad,
        big_grad,
        small_grad,
        norm_one,
        norm_two_own,
        head_grad,
        *moments,
        *states,
    )
    renewed = whole(
        renew_body, [(m.shape, f32) for m in matrices], "renew", scalars=1, cost=4
    )(z_scalar, mine_result, *z_shifts(mine_result), *matrices)
    pairs = [item.T for pair in zip(renewed, updates[:5]) for item in pair]
    states = list(updates[5:])
    states[3:6] = [x.transpose(1, 0, 2) for x in states[3:6]]
    states[6:9] = [x.transpose(2, 0, 1) for x in states[6:9]]
    return (
        loss_sum.reshape(()), weight_sum.reshape(()), grad_norm.reshape(()), *pairs, *states
    )


def solution(mesh):
    split_columns = P(None, "chan")
    split_rows = P("chan", None)
    split_first = P("chan", None, None)
    in_specs = (
        (P("chan", "batch", None), P("batch"), P("batch"), P())
        + (split_columns,) * 10
        + (split_rows,) * 3
        + (split_first,) * 6
        + (split_columns,) * 6
    )
    out_specs = (
        (P(), P(), P())
        + (split_columns,) * 10
        + (split_rows,) * 3
        + (split_first,) * 6
        + (split_columns,) * 6
    )
    return jax.shard_map(shards, mesh=mesh, in_specs=in_specs, out_specs=out_specs, check_vma=False)
```

```python
import math

import jax
import jax.numpy as jnp
import numpy as np
from jax import lax
from jax.experimental import pallas as pl
from jax.experimental.pallas import tpu as pltpu
from jax.sharding import PartitionSpec as P

S = 14
KB = 31
KS = 5
NS_STEPS = 5
STEP = 10
AREA = S * S
WIDE = S * 16
TAPS = 2 * S - 1

f32 = jnp.float32
bf16 = jnp.bfloat16
epsilon = 1e-05
highest = lax.Precision.HIGHEST
coef_first = 3.4445
coef_second = -4.775
coef_third = 2.0315
clip_limit = 0.05
momentum_decay = 0.95
muon_rate = 0.05
adam_rate = 0.05
norm_rate = 0.2
beta_first = 0.9
beta_second = 0.95
weight_decay = 0.01
root_two_pi = math.sqrt(2.0 / math.pi)
both = ("batch", "chan")
BACK = 25
SMALL = 0
PLACES = ((160, 16), (176, 16), (0, 64), (64, 64), (128, 32))


def dot(a, b, left=1, right=0, precision=None):
    return lax.dot_general(
        a, b, (((left,), (right,)), ((), ())), precision=precision, preferred_element_type=f32
    )


def gelu_pair(x):
    square = x * x
    t = jnp.tanh(root_two_pi * x * (1.0 + 0.044715 * square))
    half = 0.5 * (1.0 + t)
    slope = half + 0.5 * x * (1.0 - t * t) * (root_two_pi * (1.0 + 0.134145 * square))
    return x * half, slope


def three(x):
    high = lax.reduce_precision(x, 8, 7)
    rest = x - high
    mid = lax.reduce_precision(rest, 8, 7)
    return [high.astype(bf16), mid.astype(bf16), (rest - mid).astype(bf16)]


def core_swap(x):
    return lax.ppermute(x, "chan", [(i, i ^ 1) for i in range(32)])


def same_core():
    return [[2 * i + k for i in range(16)] for k in range(2)]


def z_shifts(x):
    return [lax.ppermute(x, "batch", [(i, (i + k) % 4) for i in range(4)]) for k in range(1, 4)]


def groups_all_to_all(x):
    return lax.all_to_all(x, "chan", 0, 0, tiled=True, axis_index_groups=same_core())


def z_pair(x):
    return lax.ppermute(x, "batch", [(0, 1), (1, 0), (2, 3), (3, 2)])


def z_cross(x):
    return lax.ppermute(x, "batch", [(0, 3), (3, 0), (1, 2), (2, 1)])


def z_gather_rows(x, near):
    z = lax.axis_index("batch")
    far = z_cross(jnp.concatenate([x, near], axis=0))
    rows = []
    for j in range(4):
        at = jnp.bitwise_xor(z, j)
        cross = jnp.where(j == 3 - z, far[0:1], far[1:2])
        rows.append(jnp.where(at == 0, x, jnp.where(at == 1, near, cross)))
    return jnp.concatenate(rows, axis=0)


def widen_matrix():
    e = np.zeros((256, 256), np.float32)
    for y in range(S):
        for x in range(S):
            e[y * S + x, y * 16 + x] = 1
    return jnp.asarray(e, bf16)


def compact_matrix():
    e = np.zeros((896, 512), np.float32)
    for f in range(TAPS):
        for x in range(S):
            e[f * 32 + x, f * S + x] = 1
    return jnp.asarray(e, bf16)


class Source:
    def __init__(self, buffer, copies):
        self.buffer = buffer
        self.copies = copies

    def ready(self):
        for copy in self.copies:
            copy.wait()
        self.copies = []

    def __getitem__(self, index):
        self.ready()
        return self.buffer[index]


class Target:
    def __init__(self, buffer, copies):
        self.buffer = buffer
        self.copies = copies
        self.sent = set()

    def __getitem__(self, index):
        return self.buffer[index]

    def __setitem__(self, index, value):
        self.buffer[index] = value

    @property
    def shape(self):
        return self.buffer.shape

    def send(self, part=None):
        for j in range(len(self.copies)):
            if j not in self.sent and part in (None, j):
                self.copies[j].start()
                self.sent.add(j)

    def finish(self):
        for copy in self.copies:
            copy.wait()


def whole(
    body, outs, name, scratch=(), scalars=0, limit=54, pieces=None, cost=2, small_in=SMALL, small_out=SMALL,
    parts=None, scalar_outs=0, near=(),
):
    pieces = pieces or {}
    parts = parts or {}

    def call(*args):
        arrays = args[scalars:]
        loads = []
        for i, array in enumerate(arrays):
            for load in pieces.get(i, [None]):
                loads.append((i, load))
        sizes = [array.size * array.dtype.itemsize for array in arrays]
        direct = [i in near or (i not in pieces and sizes[i] <= small_in) for i in range(len(arrays))]
        out_sizes = [math.prod(shape) * jnp.dtype(kind).itemsize for shape, kind in outs]
        direct_out = [size <= small_out for size in out_sizes]
        direct_out += [True] * scalar_outs
        moved = [(i, load) for i, load in loads if not direct[i]]
        moved_out = [item for item, near in zip(outs, direct_out) if not near]
        n_out_copies = sum(
            len(parts.get(j, [None])) for j, near in enumerate(direct_out) if not near
        )
        n_results = len(outs) + scalar_outs
        buffers = [
            pltpu.VMEM(arrays[i].shape if load is None else load[0], arrays[i].dtype)
            for i, load in moved
        ]
        n_copies = sum(1 if load is None else load[2] for _, load in moved)
        n_in, n_load, n_out, n_moved = len(arrays), len(moved), len(outs), len(moved_out)

        def kernel(*refs):
            small = refs[:scalars]
            refs = refs[scalars:]
            ins, refs = refs[:n_in], refs[n_in:]
            results, refs = refs[:n_results], refs[n_results:]
            in_buffers, refs = list(refs[:n_load]), refs[n_load:]
            out_buffers, refs = list(refs[:n_moved]), refs[n_moved:]
            in_sems, out_sems, rest = refs[0], refs[1], refs[2:]
            count = 0
            sources = []
            for i, load in loads:
                if direct[i]:
                    sources.append(Source(ins[i], []))
                    continue
                buffer = in_buffers.pop(0)
                ways = [(ins[i], buffer)] if load is None else load[1](ins[i], buffer, small)
                copies = []
                for origin, to in ways:
                    copy = pltpu.make_async_copy(origin, to, in_sems.at[count])
                    copy.start()
                    copies.append(copy)
                    count += 1
                sources.append(Source(buffer, copies))
            targets = []
            count = 0
            for j, (result, near) in enumerate(zip(results, direct_out)):
                if near:
                    targets.append(Target(result, []))
                    continue
                buffer = out_buffers.pop(0)
                copies = []
                for part in parts.get(j, [None]):
                    origin, to = buffer, result
                    if part is not None:
                        origin, to = buffer.at[part], result.at[part]
                    copies.append(pltpu.make_async_copy(origin, to, out_sems.at[count]))
                    count += 1
                targets.append(Target(buffer, copies))
            body(*small, *sources, *targets, *rest)
            for source in sources:
                source.ready()
            for target in targets:
                target.send()
            for target in targets:
                target.finish()

        near_space = pl.BlockSpec(memory_space=pltpu.VMEM)
        far_space = pl.BlockSpec(memory_space=pl.ANY)
        return pl.pallas_call(
            kernel,
            out_shape=[jax.ShapeDtypeStruct(*item) for item in outs]
            + [jax.ShapeDtypeStruct((1, 1), f32)] * scalar_outs,
            in_specs=[pl.BlockSpec(memory_space=pltpu.SMEM)] * scalars
            + [near_space if near else far_space for near in direct],
            out_specs=[near_space if near else far_space for near in direct_out[:n_out]]
            + [pl.BlockSpec(memory_space=pltpu.SMEM)] * scalar_outs,
            scratch_shapes=buffers
            + [pltpu.VMEM(*item) for item in moved_out]
            + [
                pltpu.SemaphoreType.DMA((max(n_copies, 1),)),
                pltpu.SemaphoreType.DMA((max(n_out_copies, 1),)),
            ]
            + list(scratch),
            name=name,
            cost_estimate=pl.CostEstimate(
                flops=cost * 1_000_000_000, bytes_accessed=0, transcendentals=0
            ),
            compiler_params=pltpu.CompilerParams(vmem_limit_bytes=limit * 1024 * 1024),
        )(*args)

    return call


def own_first(start, rows):
    def ways(origin, to, small):
        k = small[0][0]
        part = pl.ds(start, rows)
        return [(origin.at[:, k, part, :], to.at[0]), (origin.at[:, 1 - k, part, :], to.at[1])]

    return ((2, 16, rows, 512), ways, 2)


def by_core(start, rows):
    def ways(origin, to, small):
        part = pl.ds(start, rows)
        return [(origin.at[:, 0, part, :], to.at[0]), (origin.at[:, 1, part, :], to.at[1])]

    return ((2, 16, rows, 512), ways, 2)


def natural(start, rows):
    def ways(origin, to, small):
        return [(origin.at[:, :, pl.ds(start, rows), :], to)]

    return ((16, 2, rows, 512), ways, 1)


def block(ref, half, i, rows):
    n = 256 // rows
    return ref[half, i * n : (i + 1) * n].reshape(256, 512)


def half_of(ref, half, rows):
    return ref[half].reshape(16 * rows, 512)


def valid(rows):
    return lax.broadcasted_iota(jnp.int32, (rows, 256), 1) < AREA


def column(tail, i):
    at = AREA - 128 + 3 * i
    return (tail[:, at : at + 1] + tail[:, at + 1 : at + 2]) + tail[:, at + 2 : at + 3]


def row_sums(x):
    return dot(jnp.ones((8, x.shape[1]), f32), x, 1, 1, highest)[0:1]


def pack_row(row):
    return jnp.concatenate([row[:, j * 128 : (j + 1) * 128] for j in range(8)], axis=0)


def by_turn(k, rows):
    four = rows.reshape(16, 2, 16, 256)
    first, second = four[:, 0].reshape(256, 256), four[:, 1].reshape(256, 256)
    return jnp.where(k == 0, first, second), jnp.where(k == 0, second, first)


def pack_body(z, two, up, down, transit, classes, m_up, m_down, m_transit, m_one, m_two, line, packed, late, near):
    packed[0:16, :] = two[...].astype(bf16)
    packed[16:80, :] = up[...].astype(bf16)
    packed[80:144, :] = down[...].astype(bf16)
    packed[144:176, :] = transit[...].astype(bf16)
    late[0:32, :] = classes[:, 0:512].astype(bf16)
    late[32:64, :] = jnp.concatenate(
        [classes[:, 512:1000], jnp.zeros((32, 24), f32)], axis=1
    ).astype(bf16)
    rows = jnp.concatenate([m_up[...], m_down[...], m_transit[...], m_one[...], m_two[...]], axis=0)
    mine = pick(z[0], rows)
    near[...] = mine
    near.send()
    late[64:128, :] = mine.astype(bf16)
    late[128:144, :] = jnp.concatenate([line[...], jnp.zeros((15, 512), f32)], axis=0).astype(bf16)


def taps_body(shifted, compact, table):
    z = dot(shifted[...], compact[...])
    keep = valid(256)
    for py in range(S):
        at = (S - 1 - py) * S
        rows = jnp.where(keep, z[:, at : at + 256], 0.0).astype(bf16)
        table[:, py * 16 : (py + 1) * 16, :] = rows.reshape(16, 16, 256)
    table[:, WIDE:, :] = jnp.zeros((16, 256 - WIDE, 256), bf16)


def first_body(came, act, slope, normed):
    tail = came[:, 128:256].astype(f32)
    x = came[:, :256].astype(f32) - column(tail, 0)
    a = jnp.where(valid(512), x * column(tail, 1) + column(tail, 2), 0.0).astype(bf16)
    normed[...] = a
    for i in range(2):
        rows = pl.ds(i * 256, 256)
        value, back = gelu_pair(dot(came[rows, 256:768], a))
        act[rows, :] = value.astype(bf16)
        slope[rows, :] = back


def depth_forward_body(u, table, widen, mixed, act):
    for c in range(16):
        wide = dot(u[c], widen[...]).astype(bf16)
        d = dot(wide, table[c])
        mixed[c] = d
        act[c] = gelu_pair(d)[0].astype(bf16)


def tall(rows):
    return jnp.concatenate([rows, jnp.zeros((48, rows.shape[1]), rows.dtype)], axis=0)


def pixel_rows():
    return lax.broadcasted_iota(jnp.int32, (208, 512), 0) < AREA


def unpack_row(packed, h):
    return jnp.concatenate([packed[j : j + 1] for j in range(4 * h, 4 * h + 4)], axis=1)


def middle_body(came, gd, weight, middle, gains, stats):
    turned = came[:, :256].astype(f32).T
    for i in range(2):
        at = AREA + 9 + 3 * i
        gains[i : i + 1, :] = (turned[at : at + 1] + turned[at + 1 : at + 2]) + turned[at + 2 : at + 3]
    gains[2:8, :] = jnp.zeros((6, 512), f32)
    keep = pixel_rows()
    product = dot(gd[...], weight[...].reshape(512, 512), 0, 1)
    x = jnp.where(keep, turned[:208], 0.0) + product[:208]
    middle[...] = x
    middle.send()
    mean = jnp.sum(x, axis=0, keepdims=True) * (1.0 / AREA)
    apart = jnp.where(keep, x - mean, 0.0)
    spread = jnp.sum(apart * apart, axis=0, keepdims=True) * (1.0 / AREA)
    row = jnp.concatenate([mean, spread], axis=1)
    stats[...] = jnp.broadcast_to(pack_row(row)[None], (128, 8, 128))


def forward_body(
    k, stats, middle, gains, up, down, transit, normal, factor, pack, keep_act, slope_hid, slope_t, pooled
):
    parts = stats[...]
    total = jnp.sum(parts, axis=0) * (1.0 / 128)
    apart = parts - total[None]
    spread = jnp.sum(apart * apart, axis=0) * (1.0 / 128)
    center = unpack_row(total, 0)
    scale = lax.rsqrt(unpack_row(total, 1) + unpack_row(spread, 0) + epsilon)
    gain, shift = gains[0:1, :], gains[1:2, :]
    keep = pixel_rows()
    x1 = middle[...]
    xh = (x1 - center) * scale
    normal[...] = jnp.where(keep, xh, 0.0)
    normal.send()
    factor[...] = jnp.broadcast_to(gain * scale, (8, 512))
    a2 = jnp.where(keep, xh * gain + shift, 0.0).astype(bf16)
    pack[:, 1536:2048] = tall(a2)
    for i in range(8):
        value, back = gelu_pair(dot(a2, block(up, i // 4, i % 4, 64), 1, 1))
        low = tall(value.astype(bf16))
        slope_hid[:, i * 256 : (i + 1) * 256] = back
        if i < 4:
            keep_act[:, i * 256 : (i + 1) * 256] = low
        else:
            pack[:, (i - 4) * 256 : (i - 3) * 256] = low
    slope_hid.send()
    keep_act.send()
    total = x1 + dot(keep_act[:208, :], half_of(down, 0, 64))
    total = total + dot(pack[:208, :1024], half_of(down, 1, 64))
    x2 = total.astype(bf16)
    pack[:, 1024:1536] = tall(x2)
    pack.send()
    halves = []
    for i in range(2):
        value, back = gelu_pair(dot(x2, half_of(transit, i, 32), 1, 1))
        slope_t[:, i * 512 : (i + 1) * 512] = jnp.where(keep, back, 0.0)
        halves.append(jnp.sum(value, axis=0, keepdims=True) * (1.0 / AREA))
    turn = k[0] == 1
    row = jnp.concatenate(
        [jnp.where(turn, halves[1], halves[0]), jnp.where(turn, halves[0], halves[1])], axis=1
    )
    pooled[...] = jnp.broadcast_to(pack_row(row)[None], (128, 8, 128))


def head_body(
    place,
    pooled,
    people,
    class_weight,
    gains,
    classes,
    transit,
    down,
    up,
    slope_t,
    slope_hid,
    normal,
    pack,
    keep_hid,
    keep_t,
    dx2,
    da2,
    sums,
    class_grad,
    head_grad,
    loss_out,
    weight_out,
):
    k, crop, at = place[0], place[1], place[2]
    owner_rows = gains[:, :, 0:8, :].reshape(32, 8, 512)[:, 0, :].astype(f32)
    fold_rows = lax.broadcasted_iota(jnp.int32, (32, 1024), 0)
    fold_lanes = lax.broadcasted_iota(jnp.int32, (32, 1024), 1)
    expand = (fold_lanes % 32 == fold_rows).astype(f32)
    keep = fold_lanes // 32 == fold_rows

    def gain_row(i):
        at_lane = 128 * i
        parts = [owner_rows[:, at_lane + 32 * j : at_lane + 32 * j + 32] for j in range(3)]
        parts = jnp.concatenate([(parts[0] + parts[1]) + parts[2], jnp.zeros((32, 96), f32)], axis=1)
        full = jnp.concatenate([expand, jnp.zeros((96, 1024), f32)], axis=0)
        spread = dot(parts, full, 1, 0, highest)
        return jnp.sum(jnp.where(keep, spread, 0.0), axis=0, keepdims=True)

    gain = gain_row(0)
    shift = gain_row(1)
    x = jnp.concatenate([pooled[:, j, :] for j in range(8)], axis=1)
    center = jnp.sum(x, axis=0, keepdims=True) * (1.0 / 128)
    apart = x - center
    scale = lax.rsqrt(jnp.sum(apart * apart, axis=0, keepdims=True) * (1.0 / 128) + epsilon)
    xh = apart * scale
    z = (xh * gain + shift).astype(bf16)
    left = classes[:, :, 0:32].reshape(1024, 512)
    right = classes[:, :, 32:64].reshape(1024, 512)
    logits = jnp.concatenate([dot(z, left), dot(z, right)], axis=1)
    lanes = lax.broadcasted_iota(jnp.int32, (128, 128), 1)
    rows = lax.broadcasted_iota(jnp.int32, (128, 128), 0)
    pairing = (people[:, 1:2] == lanes.astype(f32)).astype(f32)
    average = 0.5 * (logits + dot(pairing, logits, 1, 0, highest))
    wide = lax.broadcasted_iota(jnp.int32, (128, 1024), 1)
    average = jnp.where(wide < 1000, average, -1e30)
    top = jnp.max(average, axis=1, keepdims=True)
    moved = average - top
    expo = jnp.exp(moved)
    norm = jnp.sum(expo, axis=1, keepdims=True)
    onehot = (people[:, 0:1] == wide.astype(f32)).astype(f32)
    weight = 0.5 * jnp.sum(onehot * class_weight[...], axis=1, keepdims=True)
    picked = jnp.sum(jnp.where(onehot > 0, moved, 0.0), axis=1, keepdims=True) - jnp.log(norm)
    weight_sum = jnp.sum(weight, axis=0, keepdims=True)
    loss_sum = -jnp.sum(weight * picked, axis=0, keepdims=True)
    loss_out[0, 0] = loss_sum[0, 0]
    weight_out[0, 0] = weight_sum[0, 0]
    dl = ((weight / weight_sum) * (expo / norm - onehot)).astype(bf16)
    dz = dot(dl[:, :512], left, 1, 1) + dot(dl[:, 512:], right, 1, 1)
    dshift = jnp.sum(dz, axis=0, keepdims=True)
    dgain = jnp.sum(dz * xh, axis=0, keepdims=True)
    dp = (gain * scale) * (dz - (dshift + xh * dgain) * (1.0 / 128))
    crops = lax.broadcasted_iota(jnp.int32, (128, 1024), 0)
    mine = jnp.sum(jnp.where(crops == crop, dp, 0.0), axis=0, keepdims=True) * (1.0 / AREA)
    turn = k == 1
    first = jnp.where(turn, mine[:, 512:], mine[:, :512])
    second = jnp.where(turn, mine[:, :512], mine[:, 512:])

    part = (slope_t[:, :512] * first).astype(bf16)
    keep_t[...] = tall(part)
    keep_t.send()
    grad = dot(part, half_of(transit, 0, 32))
    part = (slope_t[:, 512:] * second).astype(bf16)
    pack[:, 1024:1536] = tall(part)
    grad = grad + dot(part, half_of(transit, 1, 32))
    dx2[...] = grad
    dx2.send()
    low = grad.astype(bf16)
    pack[:, 1536:2048] = tall(low)
    for i in range(8):
        lanes256 = slice(i * 256, (i + 1) * 256)
        part = slope_hid[:, lanes256] * dot(low, block(down, i // 4, i % 4, 64), 1, 1)
        part = tall(part.astype(bf16))
        if i < 4:
            keep_hid[:, lanes256] = part
        else:
            pack[:, (i - 4) * 256 : (i - 3) * 256] = part
    pack.send()
    keep_hid.send()
    grad = dot(keep_hid[:208, :], half_of(up, 0, 64))
    grad = grad + dot(pack[:208, :1024], half_of(up, 1, 64))
    da2[...] = grad
    da2.send()
    row = jnp.concatenate(
        [jnp.sum(grad * normal[...], axis=0, keepdims=True), jnp.sum(grad, axis=0, keepdims=True)],
        axis=1,
    )
    sums[...] = jnp.broadcast_to(pack_row(row)[None], (128, 8, 128))
    sums.send()
    own_rows = lax.broadcasted_iota(jnp.int32, (1024, 128), 0)
    own_lanes = lax.broadcasted_iota(jnp.int32, (1024, 128), 1)
    select = ((own_rows == own_lanes + at) & (own_lanes < 32)).astype(f32)
    z_own = dot(z, select.astype(bf16)).astype(bf16)
    class_grad[...] = dot(z_own, dl, 0, 0)[:32]
    both_rows = jnp.concatenate([dgain, dshift, jnp.zeros((6, 1024), f32)], axis=0)
    head_grad[...] = dot(both_rows, select, 1, 0, highest)


def outer_body(keep_act, keep_hid, keep_t, one, two, one_in, two_in, result):
    def place(part, rows, v, rows_in, v_in, n):
        for i in range(2):
            half = slice(i * 8 * n, (i + 1) * 8 * n)
            block_rows = dot(rows[:, half], v, 0, 0) + dot(rows_in[:, half], v_in, 0, 0)
            result[i * 8 : (i + 1) * 8, part, :] = block_rows.reshape(8, n, 512)

    wide, thin = slice(0, 1024), slice(1024, 1536)
    last = slice(1536, 2048)
    place(slice(64, 128), keep_act[...], two[:, last], one_in[:, wide], two_in[:, last], 64)
    result.send(0)
    place(slice(0, 64), keep_hid[...], one[:, last], two_in[:, wide], one_in[:, last], 64)
    result.send(1)
    place(slice(128, 160), keep_t[...], one[:, thin], two_in[:, thin], one_in[:, thin], 32)
    result.send(2)


def second_body(k, sums, da2, normal, factor, dx2, weight, gd, normed, keep_rows, pack, back, norm):
    total = jnp.sum(sums[...], axis=0)
    norm[...] = total
    gain, shift = unpack_row(total, 0), unpack_row(total, 1)
    inner = da2[...] - (shift + normal[...] * gain) * (1.0 / (128 * AREA))
    grad = dx2[...] + jnp.where(pixel_rows(), factor[0:1, :] * inner, 0.0)
    low = tall(grad).T.astype(bf16)
    keep, send = by_turn(k[0], low)
    keep_rows[...] = keep
    pack[0:256, :] = send
    pack[256:768, :] = gd[...]
    pack[768:1280, :] = normed[...]
    back[...] = dot(weight[...].reshape(512, 512), low, 0, 0).astype(bf16)


def depth_backward_body(u, mixed, grad, table, widen, compact, back, taps, outer, spread):
    outer[...] = jnp.zeros_like(outer)
    for c in range(16):
        wide = dot(u[c], widen[...]).astype(bf16)
        slope = gelu_pair(mixed[c])[1]
        dd = (grad[c].astype(f32) * slope).astype(bf16)
        du = dot(dd, table[c], 1, 1).astype(bf16)
        back[c] = dot(du, widen[...], 1, 1).astype(bf16)
        outer[c, :, :256] = dot(wide, dd, 0, 0)
    total = jnp.zeros((256, 512), f32)
    for py in range(S):
        rows = outer[:, py * 16 : (py + 1) * 16, :].reshape(256, 512)
        at = (S - 1 - py) * S
        total = total + (pltpu.roll(rows, at, 1) if at else rows)
    back.send()
    wide = dot(total, compact[...].astype(f32), 1, 1, highest)
    spread[:, :, :896] = wide.reshape(16, 16, 896)
    spread[:, :, 896:] = jnp.zeros((16, 16, 128), f32)
    taps[...] = sum(pltpu.roll(spread[:, px, :], 13 - px, 1) for px in range(13)) + spread[:, 13, :]


def third_body(
    k, came, du, slope, tap, tap_one, tap_two, tap_three, keep_rows, send_rows, keep_norm, send_norm, tap_sum
):
    tap_sum[...] = (tap[...] + tap_one[...]) + (tap_two[...] + tap_three[...])
    tail = came[:, 128:256].astype(f32)
    dh = (slope[...] * du[...].astype(f32)).astype(bf16)
    keep, send = by_turn(k[0], dh)
    keep_rows[...] = keep
    send_rows[...] = send
    da = dot(came[:, 256:768], dh, 0, 0)
    x = came[:, :256].astype(f32) - column(tail, 0)
    gain, shift = row_sums(da * x), row_sums(da)
    ys = lax.broadcasted_iota(jnp.int32, (16, 512), 0)
    owner = lax.broadcasted_iota(jnp.int32, (16, 512), 1) // 16
    fold_rows = lax.broadcasted_iota(jnp.int32, (512, 128), 0) % 16
    fold_lanes = lax.broadcasted_iota(jnp.int32, (512, 128), 1)
    fold_gain = (fold_rows == fold_lanes).astype(f32)
    fold_shift = (fold_rows == fold_lanes - 16).astype(f32)

    def part(core):
        own = owner == 2 * ys + core
        return dot(jnp.where(own, gain, 0.0), fold_gain, 1, 0, highest) + dot(
            jnp.where(own, shift, 0.0), fold_shift, 1, 0, highest
        )

    keep_norm[...] = part(k[0])
    send_norm[...] = part(1 - k[0])


def last_outer_body(keep_one, keep_two, pack, got_one, got_pack, keep_norm, got_norm, result):
    one = dot(keep_one[...], pack[768:1280, :], 1, 1) + dot(
        got_one[...], got_pack[768:1280, :], 1, 1
    )
    two = dot(keep_two[...], pack[256:768, :], 1, 1) + dot(
        got_pack[0:256, :], got_pack[256:768, :], 1, 1
    )
    both_rows = jnp.concatenate([one.reshape(16, 16, 512), two.reshape(16, 16, 512)], axis=1)
    high = both_rows.astype(bf16).astype(f32)
    rest = both_rows - high
    norm = keep_norm[...] + got_norm[...]
    norm_high = norm.astype(bf16).astype(f32)
    lane = lax.broadcasted_iota(jnp.int32, (16, 128), 1)
    line = jnp.where(lane < 32, norm_high, pltpu.roll(norm - norm_high, 32, 1))[:, None, :]
    side = lax.broadcasted_iota(jnp.int32, (16, 32, 128), 2) < 64
    side = side & (lax.broadcasted_iota(jnp.int32, (16, 32, 128), 1) == 31)
    rest = jnp.concatenate([jnp.where(side, line, rest[:, :, :128]), rest[:, :, 128:]], axis=2)
    result[...] = jnp.concatenate([high, rest], axis=1).astype(bf16)


def pick(z, rows):
    blank = jnp.zeros((32, 512), f32)
    third = jnp.concatenate([rows[128:160], blank], axis=0)
    fourth = jnp.concatenate([rows[160:192], blank], axis=0)
    return jnp.where(
        z == 0, rows[0:64], jnp.where(z == 1, rows[64:128], jnp.where(z == 2, third, fourth))
    )


def everything(x):
    return jnp.sum(jnp.sum(x, axis=1, keepdims=True), axis=0, keepdims=True)


def reduce_body(
    parts, wide, wide_one, wide_two, wide_three, big_grad, small_grad, class_grad, head_grad, norm_two,
    narrow, mine, squares,
):
    sums = (wide[...] + wide_one[...]) + (wide_two[...] + wide_three[...])
    mine[...] = sums
    square = everything(class_grad[...] * class_grad[...])
    square = square + everything(jnp.sum(big_grad[...] * big_grad[...], axis=0))
    square = square + everything(jnp.sum(small_grad[...] * small_grad[...], axis=0))
    square = square + everything(head_grad[...] * head_grad[...])
    square = square + everything(norm_two[...] * norm_two[...])
    squares[...] = jnp.broadcast_to(square, (8, 128))
    total = jnp.sum(parts[...].astype(f32), axis=0)
    line = total[63:64, 0:128]
    lane = lax.broadcasted_iota(jnp.int32, (1, 128), 1)
    line = jnp.where(lane < 32, line + pltpu.roll(line, 96, 1), 0.0)
    row = lax.broadcasted_iota(jnp.int32, (32, 512), 0)
    lane = lax.broadcasted_iota(jnp.int32, (32, 512), 1)
    narrow[0:32, :] = total[:32] + jnp.where((row == 31) & (lane < 64), 0.0, total[32:])
    line = jnp.concatenate([line, jnp.zeros((1, 384), f32)], axis=1)
    narrow[32:40, :] = jnp.broadcast_to(line, (8, 512))
    narrow[40:48, :] = jnp.broadcast_to(everything(sums * sums), (8, 512))


def gather_body(
    z, wide, squares, narrow, narrow_one, narrow_two, narrow_three, scale, near, norm_one, message,
):
    rest = (narrow[...] + narrow_one[...]) + (narrow_two[...] + narrow_three[...])
    last = rest[:32]
    norm = rest[32:33, 0:128] * scale[...]
    norm_one[...] = jnp.broadcast_to(norm, (8, 128))
    square = squares[0:1, 0:1] + rest[40:41, 0:1] + everything(last * last) + everything(norm * norm)
    mine = jnp.where(z[0] == 3, jnp.concatenate([last, jnp.zeros((32, 512), f32)], axis=0), wide[...])
    near[...] = mine
    near.send()
    high = square.astype(bf16)
    rest = square - high.astype(f32)
    mid = rest.astype(bf16)
    low = (rest - mid.astype(f32)).astype(bf16)
    rows16 = lax.broadcasted_iota(jnp.int32, (16, 512), 0)
    lanes16 = lax.broadcasted_iota(jnp.int32, (16, 512), 1)
    tail = jnp.where(
        lanes16 == 0,
        high.astype(f32),
        jnp.where(lanes16 == 1, mid.astype(f32), jnp.where(lanes16 == 2, low.astype(f32), 0.0)),
    )
    tail = jnp.where(rows16 == 0, tail, 0.0)
    line = jnp.concatenate([mine, tail], axis=0).astype(bf16)
    message[...] = jnp.broadcast_to(line[None], (16, 80, 512))


def split(x):
    high = x.astype(bf16)
    return high, (x - high.astype(f32)).astype(bf16)


def mul3(a, b):
    return dot(a[0], b[0]) + (dot(a[0], b[1]) + dot(a[1], b[0]))


def muon_body(
    place, got, got_other, moment, near, near_other, near_moment, near_moment_other,
    result, result_other, scalars, norm_out, u,
):
    k, z = place[0], place[1]

    def tails(ref):
        x = ref[:, 64:80, :].astype(f32)
        return jnp.sum(jnp.sum(x, axis=0), axis=0, keepdims=True)

    square = jnp.sum(tails(got) + tails(got_other), axis=1, keepdims=True)
    norm = jnp.sqrt(square)
    f = jnp.minimum(1.0, clip_limit / (norm + 1e-06))
    line = lax.broadcasted_iota(jnp.int32, (8, 128), 1)
    scalars[...] = jnp.where(line == 0, norm, f)
    norm_out[0, 0] = norm[0, 0]
    scalars.send()
    alpha = (1.0 + momentum_decay) * f
    beta = momentum_decay * momentum_decay
    first = jnp.where((z < 3) | (k == 0), 1.0, 0.0)
    second = jnp.where((z < 3) | (k == 1), 1.0, 0.0)
    parts = ((0, 16, first), (16, 32, second), (32, 64, jnp.float32(1.0)))
    for i, g in enumerate((got, got_other)):
        for y in range(16):
            for low, high, share in parts:
                value = (alpha * share) * g[y, low:high, :].astype(f32)
                value = value + (beta * share) * moment[i, y, low:high, :].astype(f32)
                at = i * 1024 + y * 64
                u[at + low : at + high, :] = value.astype(bf16)
    gram = dot(u[...], u[...], 0, 0)
    rows = lax.broadcasted_iota(jnp.int32, (512, 512), 0)
    cols = lax.broadcasted_iota(jnp.int32, (512, 512), 1)
    eye = (rows == cols).astype(f32)
    total = jnp.sum(jnp.sum(gram * eye, axis=0, keepdims=True), axis=1, keepdims=True)
    inverse = 1.0 / (jnp.sqrt(total) + 1e-07)
    a = gram * (inverse * inverse)
    x = jnp.concatenate(
        [
            (alpha * near[...] + beta * near_moment[...]) * inverse,
            (alpha * near_other[...] + beta * near_moment_other[...]) * inverse,
        ],
        axis=0,
    )
    for step in range(NS_STEPS - 1):
        a2 = split(a)
        square = mul3(a2, a2)
        m2 = split(coef_first * eye + coef_second * a + coef_third * square)
        x = mul3(split(x), m2)
        a = mul3(split(mul3(a2, m2)), m2)
    a2 = split(a)
    once = mul3(split(x), a2)
    x = coef_first * x + coef_second * once + coef_third * mul3(split(once), a2)
    result[...] = x[:64]
    result_other[...] = x[64:]


def adamw(weight, first, second, gradient, rate):
    first = beta_first * first + (1.0 - beta_first) * gradient
    second = beta_second * second + (1.0 - beta_second) * gradient * gradient
    ratio = (
        first / (1.0 - beta_first**STEP) / (jnp.sqrt(second / (1.0 - beta_second**STEP)) + 1e-08)
    )
    return (first, second, weight - rate * (ratio + weight_decay * weight))


def by_matrix(z, got):
    group = []
    for j in range(4):
        back = lax.rem(z - j + 4, 4)
        group.append(
            jnp.where(
                back == 0,
                got[0],
                jnp.where(back == 1, got[1], jnp.where(back == 2, got[2], got[3])),
            )
        )
    return [group[3][:16], group[3][16:32], group[0], group[1], group[2][:32]]


def finish_body(
    z, scalars, mine, one, two, three_back, class_grad, big_grad, small_grad, norm_one, norm_two, head_grad,
    *refs
):
    moments, refs = refs[:5], refs[5:]
    states, refs = refs[:15], refs[15:]
    fresh, updated = refs[:5], refs[5:]
    f = scalars[0:1, 1:2]
    rows = by_matrix(z[0], [mine[...], one[...], two[...], three_back[...]])
    for moment, row, out in zip(moments, rows, fresh):
        out[...] = momentum_decay * moment[...] + f * row
        out.send()
    norm = norm_one[0:1, :]
    grads = [
        class_grad[:, :1000],
        big_grad[...],
        small_grad[...],
        jnp.concatenate([norm[:, 0:16], norm[:, 16:32], norm_two[...]], axis=0),
        head_grad[0:2, 0:32],
    ]
    rates = [adam_rate, adam_rate, adam_rate, norm_rate, norm_rate]
    for i in range(5):
        factor = f if grads[i].ndim == 2 else f.reshape(1, 1, 1)
        first, second, weight = adamw(
            states[3 * i][...], states[3 * i + 1][...], states[3 * i + 2][...],
            grads[i] * factor, rates[i],
        )
        updated[3 * i][...] = first
        updated[3 * i + 1][...] = second
        updated[3 * i + 2][...] = weight
        for j in range(3):
            updated[3 * i + j].send()


def renew_body(z, mine, one, two, three_back, *refs):
    weights, outs = refs[:5], refs[5:]
    rows = by_matrix(z[0], [mine[...], one[...], two[...], three_back[...]])
    for weight, row, (_, n), out in zip(weights, rows, PLACES, outs):
        rate = muon_rate * 0.2 * math.sqrt(max(512, 32 * n))
        out[...] = weight[...] * (1.0 - muon_rate * weight_decay) - rate * row
        out.send()


def shards(
    features,
    labels,
    partner,
    class_weight,
    point_one,
    momentum_one,
    point_two,
    momentum_two,
    expand,
    momentum_up,
    shrink,
    momentum_down,
    transit,
    momentum_transit,
    classifier,
    classifier_first,
    classifier_second,
    big_kernel,
    big_first,
    big_second,
    small_kernel,
    small_first,
    small_second,
    norm_gains,
    gains_first,
    gains_second,
    head_gains,
    head_first,
    head_second,
):
    z = lax.axis_index("batch")
    c = lax.axis_index("chan")
    k = lax.rem(c, 2)
    crop = z * 32 + c
    widen = widen_matrix()
    compact = compact_matrix()
    k_scalar = k.reshape(1).astype(jnp.int32)
    classes = class_weight.shape[0]

    flat = features.astype(f32)
    local_mean = jnp.mean(flat, axis=(1, 2))
    local_spread = jnp.mean(jnp.square(flat - local_mean[:, None, None]), axis=(1, 2))
    vector = jnp.concatenate(
        [local_mean, local_spread, labels.astype(f32), partner.astype(f32)]
    )[None, :]
    paired = z_pair(vector)
    gathered = z_gather_rows(vector, paired)
    means = gathered[:, :16]
    center = jnp.mean(means, axis=0)
    variance = jnp.mean(gathered[:, 16:32], axis=0) + jnp.mean(
        jnp.square(means - center[None]), axis=0
    )
    people = jnp.stack([gathered[:, 32:64].reshape(128), gathered[:, 64:96].reshape(128)], axis=1)
    scale_own = lax.rsqrt(variance + epsilon)

    z_scalar = z.reshape(1).astype(jnp.int32)
    matrices = [w.T for w in (point_one, point_two, expand, shrink, transit)]
    moments = [
        m.T for m in (momentum_one, momentum_two, momentum_up, momentum_down, momentum_transit)
    ]
    head_line = jnp.stack(
        [
            jnp.pad(jnp.concatenate(three(head_gains[i])).astype(f32), (0, 32))
            for i in range(2)
        ]
    ).reshape(1, 256)
    head_line = jnp.pad(head_line, ((0, 0), (0, 256)))
    packed, packed_late, near_moment = whole(
        pack_body,
        [((176, 512), bf16), ((144, 512), bf16), ((64, 512), f32)], "pack",
        scalars=1,
        cost=3,

    )(
        z_scalar,
        *matrices[1:],
        classifier,
        moments[2],
        moments[3],
        moments[4],
        moments[0],
        moments[1],
        head_line,
    )
    weights = lax.all_gather(packed, "chan", axis=0, tiled=False).reshape(16, 2, 176, 512)
    late_weights = lax.all_gather(packed_late, "chan", axis=0, tiled=False)
    late_weights = late_weights.reshape(16, 2, 144, 512)
    near_moment_other = core_swap(near_moment)

    margin = (KB - KS) // 2
    kernel = big_kernel + jnp.pad(small_kernel, ((0, 0), (margin, margin), (margin, margin)))
    centre = kernel[:, 2:29, 2:29].astype(bf16)
    flat_kernel = jnp.pad(
        jnp.pad(centre, ((0, 0), (0, 0), (0, 5))).reshape(16, TAPS * 32), ((0, 0), (0, 48))
    )
    shifted = jnp.stack(
        [flat_kernel[:, 13 - px : 13 - px + 896] for px in range(S)]
        + [jnp.zeros((16, 896), bf16)] * 2,
        axis=1,
    ).reshape(256, 896)
    (table,) = whole(
        taps_body, [((16, 256, 256), bf16)], "taps", small_out=0
    )(shifted, compact)

    extra = []
    for item in (
        center,
        scale_own * norm_gains[0],
        norm_gains[1],
        norm_gains[2],
        norm_gains[3],
    ):
        extra += three(item)
    extra = jnp.stack(extra, axis=1)
    extra = jnp.pad(extra, ((0, 0), (0, 60 - extra.shape[1])))
    fixed = jnp.concatenate([extra, point_one.T.astype(bf16)], axis=1)
    payload = jnp.concatenate(
        [features.transpose(1, 0, 2), jnp.broadcast_to(fixed[None], (32,) + fixed.shape)], axis=2
    )
    came = lax.all_to_all(payload, "chan", 0, 0, tiled=True).reshape(512, 768)
    act_one, slope_one, a1 = whole(
        first_body, [((512, 256), bf16), ((512, 256), f32), ((512, 256), bf16)], "first", cost=4
    )(came)
    u = lax.all_to_all(act_one.reshape(32, 16, 256), "chan", 0, 0, tiled=True).transpose(1, 0, 2)
    mixed, act = whole(
        depth_forward_body, [((16, 32, 256), f32), ((16, 32, 256), bf16)], "depth_forward", cost=4, small_in=0
    )(u, table, widen)
    gd = lax.all_to_all(act.transpose(1, 0, 2), "chan", 0, 0, tiled=True).reshape(512, 256)

    middle, gains, stats = whole(
        middle_body,
        [((208, 512), f32), ((8, 512), f32), ((128, 8, 128), f32)],
        "middle",
        cost=4,
        pieces={2: [natural(0, 16)]},
    )(came, gd, weights)
    stats = lax.all_to_all(stats, both, 0, 0, tiled=True)
    normal_two, factor_two, pack_one, keep_act, slope_hid, slope_t, pooled = whole(
        forward_body,
        [
            ((208, 512), f32),
            ((8, 512), f32),
            ((256, 2048), bf16),
            ((256, 1024), bf16),
            ((208, 2048), f32),
            ((208, 1024), f32),
            ((128, 8, 128), f32),
        ],
        "forward",
        cost=4,
        scalars=1,
        pieces={3: [own_first(16, 64), own_first(80, 64), own_first(144, 32)]},
    )(k_scalar, stats, middle, gains, weights)
    pooled = lax.all_to_all(pooled, both, 0, 0, tiled=True)
    place = jnp.stack([k, crop, k * 512 + (c // 2) * 32]).astype(jnp.int32)
    pack_two, keep_hid, keep_t, dx2, da2, sums, class_grad, head_grad, loss_sum, weight_sum = whole(
        head_body,
        [
            ((256, 2048), bf16),
            ((256, 1024), bf16),
            ((256, 512), bf16),
            ((208, 512), f32),
            ((208, 512), f32),
            ((128, 8, 128), f32),
            ((32, 1024), f32),
            ((8, 128), f32),
        ],
        "head",
        scalar_outs=2,
        cost=4,
        scalars=1,
        pieces={
            3: [
                by_core(128, 16),
                by_core(0, 64),
            ],
            4: [
                own_first(144, 32),
                own_first(80, 64),
                own_first(16, 64),
            ]
        },
    )(
        place,
        pooled,
        people,
        jnp.pad(class_weight, (0, 1024 - classes))[None, :],
        late_weights,
        weights,
        slope_t,
        slope_hid,
        normal_two,
    )
    sums = lax.all_to_all(sums, both, 0, 0, tiled=True)

    (wide_parts,) = whole(
        outer_body,
        [((16, 160, 512), f32)],
        "outer",
        parts={0: [np.s_[:, 64:128], np.s_[:, 0:64], np.s_[:, 128:160]]},
    )(
        keep_act, keep_hid, keep_t, pack_one, pack_two, core_swap(pack_one), core_swap(pack_two)
    )
    wide_sum = lax.psum_scatter(
        wide_parts, "chan", scatter_dimension=0, axis_index_groups=same_core()
    )

    keep_two, pack_three, dgd, norm_two = whole(
        second_body,
        [((256, 256), bf16), ((1280, 256), bf16), ((512, 256), bf16), ((8, 128), f32)],
        "second",
        cost=BACK,
        scalars=1,
        pieces={5: [natural(0, 16)]},
    )(k_scalar, sums, da2, normal_two, factor_two, dx2, weights, gd, a1)
    grad_mixed = lax.all_to_all(
        dgd.reshape(32, 16, 256), "chan", 0, 0, tiled=True
    ).transpose(1, 0, 2)
    back, tap_grad = whole(
        depth_backward_body,
        [((16, 32, 256), bf16), ((16, 1024), f32)],
        "depth_backward",
        small_in=0,
        cost=BACK,
        scratch=[pltpu.VMEM((16, 256, 512), f32), pltpu.VMEM((16, 16, 1024), f32)],
    )(u, mixed, grad_mixed, table, widen, compact)
    du1 = lax.all_to_all(back.transpose(1, 0, 2), "chan", 0, 0, tiled=True).reshape(512, 256)
    keep_one, send_one, keep_norm, send_norm, tap_grad = whole(
        third_body,
        [
            ((256, 256), bf16),
            ((256, 256), bf16),
            ((16, 128), f32),
            ((16, 128), f32),
            ((16, 1024), f32),
        ],
        "third",
        cost=BACK,
        scalars=1,
    )(k_scalar, came, du1, slope_one, tap_grad, *z_shifts(tap_grad))
    (narrow_parts,) = whole(last_outer_body, [((16, 64, 512), bf16)], "last_outer", cost=BACK)(
        keep_one,
        keep_two,
        pack_three,
        core_swap(send_one),
        core_swap(pack_three),
        keep_norm,
        core_swap(send_norm),
    )
    big_grad = tap_grad[:, :864].reshape(16, TAPS, 32)[:, :, :TAPS]
    big_grad = jnp.pad(big_grad, ((0, 0), (2, 2), (2, 2)))
    small_grad = big_grad[:, margin : margin + KS, margin : margin + KS].transpose(1, 2, 0)
    big_grad = big_grad.transpose(1, 0, 2)
    norm_two_own = lax.dynamic_slice_in_dim(norm_two.reshape(2, 512), c * 16, 16, 1)
    line = jnp.concatenate([scale_own, jnp.ones((16,), f32), jnp.zeros((96,), f32)])
    scale_line = line[None]
    wide_sum = jnp.pad(wide_sum.reshape(160, 512), ((0, 96), (0, 0)))

    def for_group(j):
        return lax.dynamic_slice_in_dim(wide_sum, 64 * lax.rem(z + j, 4), 64, 0)

    narrow_sum, mine_wide, squares = whole(
        reduce_body, [((48, 512), f32), ((64, 512), f32), ((8, 128), f32)], "reduce", cost=4
    )(
        groups_all_to_all(narrow_parts),
        for_group(0),
        *[
            lax.ppermute(for_group(j), "batch", [(i, (i + j) % 4) for i in range(4)])
            for j in range(1, 4)
        ],
        big_grad,
        small_grad,
        class_grad,
        head_grad,
        norm_two_own,
    )
    near, norm_one, message = whole(
        gather_body,
        [((64, 512), f32), ((8, 128), f32), ((16, 80, 512), bf16)],
        "gather",
        scalars=1,
        cost=4,
    )(z_scalar, mine_wide, squares, narrow_sum, *z_shifts(narrow_sum), scale_line)
    near_shifts = z_shifts(near)
    arrived = sum(item[0, 0] for item in near_shifts) < 1e30
    got = groups_all_to_all(message)
    got = jnp.where(arrived, got, -got)
    near_other = core_swap(near)
    near_rows, near_rows_other, scalars, grad_norm = whole(
        muon_body,
        [((64, 512), f32), ((64, 512), f32), ((8, 128), f32)],
        "muon",
        cost=4,
        scratch=[pltpu.VMEM((2048, 512), bf16)],
        scalars=1,
        scalar_outs=1,
        pieces={2: [own_first(64, 64)]},
    )(
        jnp.stack([k, z]).astype(jnp.int32),
        got,
        core_swap(got),
        late_weights,
        near,
        near_other,
        near_moment,
        near_moment_other,
    )
    row = np.arange(64)
    first_rows = jnp.asarray((row < 16).astype(np.float32))
    second_rows = jnp.asarray(((row >= 16) & (row < 32)).astype(np.float32))
    own_rows = jnp.where(z < 3, 1.0, jnp.where(k == 0, first_rows, second_rows))[:, None]
    mine_result = jnp.where(own_rows > 0, near_rows, core_swap(near_rows_other))
    def turn_big(x):
        return x.transpose(1, 0, 2)

    def turn_small(x):
        return x.transpose(1, 2, 0)

    states = [
        *(classifier, classifier_first, classifier_second),
        *(turn_big(x) for x in (big_kernel, big_first, big_second)),
        *(turn_small(x) for x in (small_kernel, small_first, small_second)),
        *(norm_gains, gains_first, gains_second),
        *(head_gains, head_first, head_second),
    ]
    updates = whole(
        finish_body, [(x.shape, f32) for x in moments + states], "finish", scalars=1, cost=6
    )(
        z_scalar,
        scalars,
        near,
        *near_shifts,
        class_grad,
        big_grad,
        small_grad,
        norm_one,
        norm_two_own,
        head_grad,
        *moments,
        *states,
    )
    renewed = whole(
        renew_body, [(m.shape, f32) for m in matrices], "renew", scalars=1, cost=4
    )(z_scalar, mine_result, *z_shifts(mine_result), *matrices)
    pairs = [item.T for pair in zip(renewed, updates[:5]) for item in pair]
    states = list(updates[5:])
    states[3:6] = [x.transpose(1, 0, 2) for x in states[3:6]]
    states[6:9] = [x.transpose(2, 0, 1) for x in states[6:9]]
    return (
        loss_sum.reshape(()), weight_sum.reshape(()), grad_norm.reshape(()), *pairs, *states
    )


def solution(mesh):
    split_columns = P(None, "chan")
    split_rows = P("chan", None)
    split_first = P("chan", None, None)
    in_specs = (
        (P("chan", "batch", None), P("batch"), P("batch"), P())
        + (split_columns,) * 10
        + (split_rows,) * 3
        + (split_first,) * 6
        + (split_columns,) * 6
    )
    out_specs = (
        (P(), P(), P())
        + (split_columns,) * 10
        + (split_rows,) * 3
        + (split_first,) * 6
        + (split_columns,) * 6
    )
    return jax.shard_map(shards, mesh=mesh, in_specs=in_specs, out_specs=out_specs, check_vma=False)
```

```python
import math

import jax
import jax.numpy as jnp
import numpy as np
from jax import lax
from jax.experimental import pallas as pl
from jax.experimental.pallas import tpu as pltpu
from jax.sharding import PartitionSpec as P

S = 14
KB = 31
KS = 5
NS_STEPS = 5
STEP = 10
AREA = S * S
WIDE = S * 16
TAPS = 2 * S - 1

f32 = jnp.float32
bf16 = jnp.bfloat16
epsilon = 1e-05
highest = lax.Precision.HIGHEST
coef_first = 3.4445
coef_second = -4.775
coef_third = 2.0315
clip_limit = 0.05
momentum_decay = 0.95
muon_rate = 0.05
adam_rate = 0.05
norm_rate = 0.2
beta_first = 0.9
beta_second = 0.95
weight_decay = 0.01
root_two_pi = math.sqrt(2.0 / math.pi)
both = ("batch", "chan")
BACK = 25
SMALL = 0
PLACES = ((160, 16), (176, 16), (0, 64), (64, 64), (128, 32))


def dot(a, b, left=1, right=0, precision=None):
    return lax.dot_general(
        a, b, (((left,), (right,)), ((), ())), precision=precision, preferred_element_type=f32
    )


def gelu_pair(x):
    square = x * x
    t = jnp.tanh(root_two_pi * x * (1.0 + 0.044715 * square))
    half = 0.5 * (1.0 + t)
    slope = half + 0.5 * x * (1.0 - t * t) * (root_two_pi * (1.0 + 0.134145 * square))
    return x * half, slope


def three(x):
    high = lax.reduce_precision(x, 8, 7)
    rest = x - high
    mid = lax.reduce_precision(rest, 8, 7)
    return [high.astype(bf16), mid.astype(bf16), (rest - mid).astype(bf16)]


def core_swap(x):
    return lax.ppermute(x, "chan", [(i, i ^ 1) for i in range(32)])


def same_core():
    return [[2 * i + k for i in range(16)] for k in range(2)]


def z_shifts(x):
    return [lax.ppermute(x, "batch", [(i, (i + k) % 4) for i in range(4)]) for k in range(1, 4)]


def groups_all_to_all(x):
    return lax.all_to_all(x, "chan", 0, 0, tiled=True, axis_index_groups=same_core())


def z_pair(x):
    return lax.ppermute(x, "batch", [(0, 1), (1, 0), (2, 3), (3, 2)])


def z_cross(x):
    return lax.ppermute(x, "batch", [(0, 3), (3, 0), (1, 2), (2, 1)])


def z_gather_rows(x, near):
    z = lax.axis_index("batch")
    far = z_cross(jnp.concatenate([x, near], axis=0))
    rows = []
    for j in range(4):
        at = jnp.bitwise_xor(z, j)
        cross = jnp.where(j == 3 - z, far[0:1], far[1:2])
        rows.append(jnp.where(at == 0, x, jnp.where(at == 1, near, cross)))
    return jnp.concatenate(rows, axis=0)


def widen_matrix():
    e = np.zeros((256, 256), np.float32)
    for y in range(S):
        for x in range(S):
            e[y * S + x, y * 16 + x] = 1
    return jnp.asarray(e, bf16)


def compact_matrix():
    e = np.zeros((896, 512), np.float32)
    for f in range(TAPS):
        for x in range(S):
            e[f * 32 + x, f * S + x] = 1
    return jnp.asarray(e, bf16)


class Source:
    def __init__(self, buffer, copies):
        self.buffer = buffer
        self.copies = copies

    def ready(self):
        for copy in self.copies:
            copy.wait()
        self.copies = []

    def __getitem__(self, index):
        self.ready()
        return self.buffer[index]


class Target:
    def __init__(self, buffer, copies):
        self.buffer = buffer
        self.copies = copies
        self.sent = set()

    def __getitem__(self, index):
        return self.buffer[index]

    def __setitem__(self, index, value):
        self.buffer[index] = value

    @property
    def shape(self):
        return self.buffer.shape

    def send(self, part=None):
        for j in range(len(self.copies)):
            if j not in self.sent and part in (None, j):
                self.copies[j].start()
                self.sent.add(j)

    def finish(self):
        for copy in self.copies:
            copy.wait()


def whole(
    body, outs, name, scratch=(), scalars=0, limit=54, pieces=None, cost=2, small_in=SMALL, small_out=SMALL,
    parts=None, scalar_outs=0, near=(),
):
    pieces = pieces or {}
    parts = parts or {}

    def call(*args):
        arrays = args[scalars:]
        loads = []
        for i, array in enumerate(arrays):
            for load in pieces.get(i, [None]):
                loads.append((i, load))
        sizes = [array.size * array.dtype.itemsize for array in arrays]
        direct = [i in near or (i not in pieces and sizes[i] <= small_in) for i in range(len(arrays))]
        out_sizes = [math.prod(shape) * jnp.dtype(kind).itemsize for shape, kind in outs]
        direct_out = [size <= small_out for size in out_sizes]
        direct_out += [True] * scalar_outs
        moved = [(i, load) for i, load in loads if not direct[i]]
        moved_out = [item for item, near in zip(outs, direct_out) if not near]
        n_out_copies = sum(
            len(parts.get(j, [None])) for j, near in enumerate(direct_out) if not near
        )
        n_results = len(outs) + scalar_outs
        buffers = [
            pltpu.VMEM(arrays[i].shape if load is None else load[0], arrays[i].dtype)
            for i, load in moved
        ]
        n_copies = sum(1 if load is None else load[2] for _, load in moved)
        n_in, n_load, n_out, n_moved = len(arrays), len(moved), len(outs), len(moved_out)

        def kernel(*refs):
            small = refs[:scalars]
            refs = refs[scalars:]
            ins, refs = refs[:n_in], refs[n_in:]
            results, refs = refs[:n_results], refs[n_results:]
            in_buffers, refs = list(refs[:n_load]), refs[n_load:]
            out_buffers, refs = list(refs[:n_moved]), refs[n_moved:]
            in_sems, out_sems, rest = refs[0], refs[1], refs[2:]
            count = 0
            sources = []
            for i, load in loads:
                if direct[i]:
                    sources.append(Source(ins[i], []))
                    continue
                buffer = in_buffers.pop(0)
                ways = [(ins[i], buffer)] if load is None else load[1](ins[i], buffer, small)
                copies = []
                for origin, to in ways:
                    copy = pltpu.make_async_copy(origin, to, in_sems.at[count])
                    copy.start()
                    copies.append(copy)
                    count += 1
                sources.append(Source(buffer, copies))
            targets = []
            count = 0
            for j, (result, near) in enumerate(zip(results, direct_out)):
                if near:
                    targets.append(Target(result, []))
                    continue
                buffer = out_buffers.pop(0)
                copies = []
                for part in parts.get(j, [None]):
                    origin, to = buffer, result
                    if part is not None:
                        origin, to = buffer.at[part], result.at[part]
                    copies.append(pltpu.make_async_copy(origin, to, out_sems.at[count]))
                    count += 1
                targets.append(Target(buffer, copies))
            body(*small, *sources, *targets, *rest)
            for source in sources:
                source.ready()
            for target in targets:
                target.send()
            for target in targets:
                target.finish()

        near_space = pl.BlockSpec(memory_space=pltpu.VMEM)
        far_space = pl.BlockSpec(memory_space=pl.ANY)
        return pl.pallas_call(
            kernel,
            out_shape=[jax.ShapeDtypeStruct(*item) for item in outs]
            + [jax.ShapeDtypeStruct((1, 1), f32)] * scalar_outs,
            in_specs=[pl.BlockSpec(memory_space=pltpu.SMEM)] * scalars
            + [near_space if near else far_space for near in direct],
            out_specs=[near_space if near else far_space for near in direct_out[:n_out]]
            + [pl.BlockSpec(memory_space=pltpu.SMEM)] * scalar_outs,
            scratch_shapes=buffers
            + [pltpu.VMEM(*item) for item in moved_out]
            + [
                pltpu.SemaphoreType.DMA((max(n_copies, 1),)),
                pltpu.SemaphoreType.DMA((max(n_out_copies, 1),)),
            ]
            + list(scratch),
            name=name,
            cost_estimate=pl.CostEstimate(
                flops=cost * 1_000_000_000, bytes_accessed=0, transcendentals=0
            ),
            compiler_params=pltpu.CompilerParams(vmem_limit_bytes=limit * 1024 * 1024),
        )(*args)

    return call


def own_first(start, rows):
    def ways(origin, to, small):
        k = small[0][0]
        part = pl.ds(start, rows)
        return [(origin.at[:, k, part, :], to.at[0]), (origin.at[:, 1 - k, part, :], to.at[1])]

    return ((2, 16, rows, 512), ways, 2)


def by_core(start, rows):
    def ways(origin, to, small):
        part = pl.ds(start, rows)
        return [(origin.at[:, 0, part, :], to.at[0]), (origin.at[:, 1, part, :], to.at[1])]

    return ((2, 16, rows, 512), ways, 2)


def natural(start, rows):
    def ways(origin, to, small):
        return [(origin.at[:, :, pl.ds(start, rows), :], to)]

    return ((16, 2, rows, 512), ways, 1)


def block(ref, half, i, rows):
    n = 256 // rows
    return ref[half, i * n : (i + 1) * n].reshape(256, 512)


def half_of(ref, half, rows):
    return ref[half].reshape(16 * rows, 512)


def valid(rows):
    return lax.broadcasted_iota(jnp.int32, (rows, 256), 1) < AREA


def column(tail, i):
    at = AREA - 128 + 3 * i
    return (tail[:, at : at + 1] + tail[:, at + 1 : at + 2]) + tail[:, at + 2 : at + 3]


def row_sums(x):
    return dot(jnp.ones((8, x.shape[1]), f32), x, 1, 1, highest)[0:1]


def pack_row(row):
    return jnp.concatenate([row[:, j * 128 : (j + 1) * 128] for j in range(8)], axis=0)


def by_turn(k, rows):
    four = rows.reshape(16, 2, 16, 256)
    first, second = four[:, 0].reshape(256, 256), four[:, 1].reshape(256, 256)
    return jnp.where(k == 0, first, second), jnp.where(k == 0, second, first)


def pack_body(z, two, up, down, transit, classes, m_up, m_down, m_transit, m_one, m_two, line, packed, late, near):
    packed[0:16, :] = two[...].astype(bf16)
    packed[16:80, :] = up[...].astype(bf16)
    packed[80:144, :] = down[...].astype(bf16)
    packed[144:176, :] = transit[...].astype(bf16)
    late[0:32, :] = classes[:, 0:512].astype(bf16)
    late[32:64, :] = jnp.concatenate(
        [classes[:, 512:1000], jnp.zeros((32, 24), f32)], axis=1
    ).astype(bf16)
    rows = jnp.concatenate([m_up[...], m_down[...], m_transit[...], m_one[...], m_two[...]], axis=0)
    mine = pick(z[0], rows)
    near[...] = mine
    near.send()
    late[64:128, :] = mine.astype(bf16)
    late[128:144, :] = jnp.concatenate([line[...], jnp.zeros((15, 512), f32)], axis=0).astype(bf16)


def taps_body(shifted, compact, table):
    z = dot(shifted[...], compact[...])
    keep = valid(256)
    for py in range(S):
        at = (S - 1 - py) * S
        rows = jnp.where(keep, z[:, at : at + 256], 0.0).astype(bf16)
        table[:, py * 16 : (py + 1) * 16, :] = rows.reshape(16, 16, 256)
    table[:, WIDE:, :] = jnp.zeros((16, 256 - WIDE, 256), bf16)


def first_body(came, act, slope, normed):
    tail = came[:, 128:256].astype(f32)
    x = came[:, :256].astype(f32) - column(tail, 0)
    a = jnp.where(valid(512), x * column(tail, 1) + column(tail, 2), 0.0).astype(bf16)
    normed[...] = a
    for i in range(2):
        rows = pl.ds(i * 256, 256)
        value, back = gelu_pair(dot(came[rows, 256:768], a))
        act[rows, :] = value.astype(bf16)
        slope[rows, :] = back


def depth_forward_body(u, table, widen, mixed, act):
    for c in range(16):
        wide = dot(u[c], widen[...]).astype(bf16)
        d = dot(wide, table[c])
        mixed[c] = d
        act[c] = gelu_pair(d)[0].astype(bf16)


def tall(rows):
    return jnp.concatenate([rows, jnp.zeros((48, rows.shape[1]), rows.dtype)], axis=0)


def pixel_rows():
    return lax.broadcasted_iota(jnp.int32, (208, 512), 0) < AREA


def unpack_row(packed, h):
    return jnp.concatenate([packed[j : j + 1] for j in range(4 * h, 4 * h + 4)], axis=1)


def middle_body(came, gd, weight, middle, gains, stats):
    turned = came[:, :256].astype(f32).T
    for i in range(2):
        at = AREA + 9 + 3 * i
        gains[i : i + 1, :] = (turned[at : at + 1] + turned[at + 1 : at + 2]) + turned[at + 2 : at + 3]
    gains[2:8, :] = jnp.zeros((6, 512), f32)
    keep = pixel_rows()
    product = dot(gd[...], weight[...].reshape(512, 512), 0, 1)
    x = jnp.where(keep, turned[:208], 0.0) + product[:208]
    middle[...] = x
    middle.send()
    mean = jnp.sum(x, axis=0, keepdims=True) * (1.0 / AREA)
    apart = jnp.where(keep, x - mean, 0.0)
    spread = jnp.sum(apart * apart, axis=0, keepdims=True) * (1.0 / AREA)
    row = jnp.concatenate([mean, spread], axis=1)
    stats[...] = jnp.broadcast_to(pack_row(row)[None], (128, 8, 128))


def forward_body(
    k, stats, middle, gains, up, down, transit, normal, factor, pack, keep_act, slope_hid, slope_t, pooled
):
    parts = stats[...]
    total = jnp.sum(parts, axis=0) * (1.0 / 128)
    apart = parts - total[None]
    spread = jnp.sum(apart * apart, axis=0) * (1.0 / 128)
    center = unpack_row(total, 0)
    scale = lax.rsqrt(unpack_row(total, 1) + unpack_row(spread, 0) + epsilon)
    gain, shift = gains[0:1, :], gains[1:2, :]
    keep = pixel_rows()
    x1 = middle[...]
    xh = (x1 - center) * scale
    normal[...] = jnp.where(keep, xh, 0.0)
    normal.send()
    factor[...] = jnp.broadcast_to(gain * scale, (8, 512))
    a2 = jnp.where(keep, xh * gain + shift, 0.0).astype(bf16)
    pack[:, 1536:2048] = tall(a2)
    for i in range(8):
        hid = dot(a2, block(up, i // 4, i % 4, 64), 1, 1)
        low = tall(gelu_pair(hid)[0].astype(bf16))
        slope_hid[:, i * 256 : (i + 1) * 256] = hid
        if i < 4:
            keep_act[:, i * 256 : (i + 1) * 256] = low
        else:
            pack[:, (i - 4) * 256 : (i - 3) * 256] = low
    slope_hid.send()
    keep_act.send()
    total = x1 + dot(keep_act[:208, :], half_of(down, 0, 64))
    total = total + dot(pack[:208, :1024], half_of(down, 1, 64))
    x2 = total.astype(bf16)
    pack[:, 1024:1536] = tall(x2)
    pack.send()
    halves = []
    for i in range(2):
        t = dot(x2, half_of(transit, i, 32), 1, 1)
        slope_t[:, i * 512 : (i + 1) * 512] = t
        halves.append(jnp.sum(gelu_pair(t)[0], axis=0, keepdims=True) * (1.0 / AREA))
    turn = k[0] == 1
    row = jnp.concatenate(
        [jnp.where(turn, halves[1], halves[0]), jnp.where(turn, halves[0], halves[1])], axis=1
    )
    pooled[...] = jnp.broadcast_to(pack_row(row)[None], (128, 8, 128))


def slopes_body(hid, t, slope_hid, slope_t):
    for i in range(8):
        lanes = slice(i * 256, (i + 1) * 256)
        slope_hid[:, lanes] = gelu_pair(hid[:, lanes])[1]
    slope_hid.send()
    keep = pixel_rows()
    for i in range(2):
        lanes = slice(i * 512, (i + 1) * 512)
        slope_t[:, lanes] = jnp.where(keep, gelu_pair(t[:, lanes])[1], 0.0)


def head_body(
    place,
    pooled,
    people,
    class_weight,
    gains,
    classes,
    transit,
    down,
    up,
    slope_t,
    slope_hid,
    normal,
    pack,
    keep_hid,
    keep_t,
    dx2,
    da2,
    sums,
    z_out,
    dl_out,
    head_rows,
    loss_out,
    weight_out,
):
    k, crop = place[0], place[1]
    owner_rows = gains[:, :, 0:8, :].reshape(32, 8, 512)[:, 0, :].astype(f32)
    fold_rows = lax.broadcasted_iota(jnp.int32, (32, 1024), 0)
    fold_lanes = lax.broadcasted_iota(jnp.int32, (32, 1024), 1)
    expand = (fold_lanes % 32 == fold_rows).astype(f32)
    keep = fold_lanes // 32 == fold_rows

    def gain_row(i):
        at_lane = 128 * i
        parts = [owner_rows[:, at_lane + 32 * j : at_lane + 32 * j + 32] for j in range(3)]
        parts = jnp.concatenate([(parts[0] + parts[1]) + parts[2], jnp.zeros((32, 96), f32)], axis=1)
        full = jnp.concatenate([expand, jnp.zeros((96, 1024), f32)], axis=0)
        spread = dot(parts, full, 1, 0, highest)
        return jnp.sum(jnp.where(keep, spread, 0.0), axis=0, keepdims=True)

    gain = gain_row(0)
    shift = gain_row(1)
    x = jnp.concatenate([pooled[:, j, :] for j in range(8)], axis=1)
    center = jnp.sum(x, axis=0, keepdims=True) * (1.0 / 128)
    apart = x - center
    scale = lax.rsqrt(jnp.sum(apart * apart, axis=0, keepdims=True) * (1.0 / 128) + epsilon)
    xh = apart * scale
    z = (xh * gain + shift).astype(bf16)
    z_out[...] = z
    z_out.send()
    left = classes[:, :, 0:32].reshape(1024, 512)
    right = classes[:, :, 32:64].reshape(1024, 512)
    logits = jnp.concatenate([dot(z, left), dot(z, right)], axis=1)
    lanes = lax.broadcasted_iota(jnp.int32, (128, 128), 1)
    rows = lax.broadcasted_iota(jnp.int32, (128, 128), 0)
    pairing = (people[:, 1:2] == lanes.astype(f32)).astype(f32)
    average = 0.5 * (logits + dot(pairing, logits, 1, 0, highest))
    wide = lax.broadcasted_iota(jnp.int32, (128, 1024), 1)
    average = jnp.where(wide < 1000, average, -1e30)
    top = jnp.max(average, axis=1, keepdims=True)
    moved = average - top
    expo = jnp.exp(moved)
    norm = jnp.sum(expo, axis=1, keepdims=True)
    onehot = (people[:, 0:1] == wide.astype(f32)).astype(f32)
    weight = 0.5 * jnp.sum(onehot * class_weight[...], axis=1, keepdims=True)
    picked = jnp.sum(jnp.where(onehot > 0, moved, 0.0), axis=1, keepdims=True) - jnp.log(norm)
    weight_sum = jnp.sum(weight, axis=0, keepdims=True)
    loss_sum = -jnp.sum(weight * picked, axis=0, keepdims=True)
    loss_out[0, 0] = loss_sum[0, 0]
    weight_out[0, 0] = weight_sum[0, 0]
    dl = ((weight / weight_sum) * (expo / norm - onehot)).astype(bf16)
    dl_out[...] = dl
    dl_out.send()
    dz = dot(dl[:, :512], left, 1, 1) + dot(dl[:, 512:], right, 1, 1)
    dshift = jnp.sum(dz, axis=0, keepdims=True)
    dgain = jnp.sum(dz * xh, axis=0, keepdims=True)
    dp = (gain * scale) * (dz - (dshift + xh * dgain) * (1.0 / 128))
    crops = lax.broadcasted_iota(jnp.int32, (128, 1024), 0)
    mine = jnp.sum(jnp.where(crops == crop, dp, 0.0), axis=0, keepdims=True) * (1.0 / AREA)
    turn = k == 1
    first = jnp.where(turn, mine[:, 512:], mine[:, :512])
    second = jnp.where(turn, mine[:, :512], mine[:, 512:])

    part = (slope_t[:, :512] * first).astype(bf16)
    keep_t[...] = tall(part)
    keep_t.send()
    grad = dot(part, half_of(transit, 0, 32))
    part = (slope_t[:, 512:] * second).astype(bf16)
    pack[:, 1024:1536] = tall(part)
    grad = grad + dot(part, half_of(transit, 1, 32))
    dx2[...] = grad
    dx2.send()
    low = grad.astype(bf16)
    pack[:, 1536:2048] = tall(low)
    for i in range(8):
        lanes256 = slice(i * 256, (i + 1) * 256)
        part = slope_hid[:, lanes256] * dot(low, block(down, i // 4, i % 4, 64), 1, 1)
        part = tall(part.astype(bf16))
        if i < 4:
            keep_hid[:, lanes256] = part
        else:
            pack[:, (i - 4) * 256 : (i - 3) * 256] = part
    pack.send()
    keep_hid.send()
    grad = dot(keep_hid[:208, :], half_of(up, 0, 64))
    grad = grad + dot(pack[:208, :1024], half_of(up, 1, 64))
    da2[...] = grad
    da2.send()
    row = jnp.concatenate(
        [jnp.sum(grad * normal[...], axis=0, keepdims=True), jnp.sum(grad, axis=0, keepdims=True)],
        axis=1,
    )
    sums[...] = jnp.broadcast_to(pack_row(row)[None], (128, 8, 128))
    sums.send()
    head_rows[...] = jnp.concatenate([dgain, dshift, jnp.zeros((6, 1024), f32)], axis=0)


def classes_body(place, z, dl, head_rows, class_grad, head_grad):
    own_rows = lax.broadcasted_iota(jnp.int32, (1024, 128), 0)
    own_lanes = lax.broadcasted_iota(jnp.int32, (1024, 128), 1)
    select = ((own_rows == own_lanes + place[2]) & (own_lanes < 32)).astype(f32)
    z_own = dot(z[...], select.astype(bf16)).astype(bf16)
    class_grad[...] = dot(z_own, dl[...], 0, 0)[:32]
    head_grad[...] = dot(head_rows[...], select, 1, 0, highest)


def outer_body(keep_act, keep_hid, keep_t, one, two, one_in, two_in, result):
    def place(part, rows, v, rows_in, v_in, n):
        for i in range(2):
            half = slice(i * 8 * n, (i + 1) * 8 * n)
            block_rows = dot(rows[:, half], v, 0, 0) + dot(rows_in[:, half], v_in, 0, 0)
            result[i * 8 : (i + 1) * 8, part, :] = block_rows.reshape(8, n, 512)

    wide, thin = slice(0, 1024), slice(1024, 1536)
    last = slice(1536, 2048)
    place(slice(64, 128), keep_act[...], two[:, last], one_in[:, wide], two_in[:, last], 64)
    result.send(0)
    place(slice(0, 64), keep_hid[...], one[:, last], two_in[:, wide], one_in[:, last], 64)
    result.send(1)
    place(slice(128, 160), keep_t[...], one[:, thin], two_in[:, thin], one_in[:, thin], 32)
    result.send(2)


def second_body(k, sums, da2, normal, factor, dx2, weight, gd, normed, keep_rows, pack, back, norm):
    total = jnp.sum(sums[...], axis=0)
    norm[...] = total
    gain, shift = unpack_row(total, 0), unpack_row(total, 1)
    inner = da2[...] - (shift + normal[...] * gain) * (1.0 / (128 * AREA))
    grad = dx2[...] + jnp.where(pixel_rows(), factor[0:1, :] * inner, 0.0)
    low = tall(grad).T.astype(bf16)
    keep, send = by_turn(k[0], low)
    keep_rows[...] = keep
    pack[0:256, :] = send
    pack[256:768, :] = gd[...]
    pack[768:1280, :] = normed[...]
    back[...] = dot(weight[...].reshape(512, 512), low, 0, 0).astype(bf16)


def depth_backward_body(u, mixed, grad, table, widen, compact, back, taps, outer, spread):
    outer[...] = jnp.zeros_like(outer)
    for c in range(16):
        wide = dot(u[c], widen[...]).astype(bf16)
        slope = gelu_pair(mixed[c])[1]
        dd = (grad[c].astype(f32) * slope).astype(bf16)
        du = dot(dd, table[c], 1, 1).astype(bf16)
        back[c] = dot(du, widen[...], 1, 1).astype(bf16)
        outer[c, :, :256] = dot(wide, dd, 0, 0)
    total = jnp.zeros((256, 512), f32)
    for py in range(S):
        rows = outer[:, py * 16 : (py + 1) * 16, :].reshape(256, 512)
        at = (S - 1 - py) * S
        total = total + (pltpu.roll(rows, at, 1) if at else rows)
    back.send()
    wide = dot(total, compact[...].astype(f32), 1, 1, highest)
    spread[:, :, :896] = wide.reshape(16, 16, 896)
    spread[:, :, 896:] = jnp.zeros((16, 16, 128), f32)
    taps[...] = sum(pltpu.roll(spread[:, px, :], 13 - px, 1) for px in range(13)) + spread[:, 13, :]


def third_body(
    k, came, du, slope, tap, tap_one, tap_two, tap_three, keep_rows, send_rows, keep_norm, send_norm, tap_sum
):
    tap_sum[...] = (tap[...] + tap_one[...]) + (tap_two[...] + tap_three[...])
    tail = came[:, 128:256].astype(f32)
    dh = (slope[...] * du[...].astype(f32)).astype(bf16)
    keep, send = by_turn(k[0], dh)
    keep_rows[...] = keep
    send_rows[...] = send
    da = dot(came[:, 256:768], dh, 0, 0)
    x = came[:, :256].astype(f32) - column(tail, 0)
    gain, shift = row_sums(da * x), row_sums(da)
    ys = lax.broadcasted_iota(jnp.int32, (16, 512), 0)
    owner = lax.broadcasted_iota(jnp.int32, (16, 512), 1) // 16
    fold_rows = lax.broadcasted_iota(jnp.int32, (512, 128), 0) % 16
    fold_lanes = lax.broadcasted_iota(jnp.int32, (512, 128), 1)
    fold_gain = (fold_rows == fold_lanes).astype(f32)
    fold_shift = (fold_rows == fold_lanes - 16).astype(f32)

    def part(core):
        own = owner == 2 * ys + core
        return dot(jnp.where(own, gain, 0.0), fold_gain, 1, 0, highest) + dot(
            jnp.where(own, shift, 0.0), fold_shift, 1, 0, highest
        )

    keep_norm[...] = part(k[0])
    send_norm[...] = part(1 - k[0])


def last_outer_body(keep_one, keep_two, pack, got_one, got_pack, keep_norm, got_norm, result):
    one = dot(keep_one[...], pack[768:1280, :], 1, 1) + dot(
        got_one[...], got_pack[768:1280, :], 1, 1
    )
    two = dot(keep_two[...], pack[256:768, :], 1, 1) + dot(
        got_pack[0:256, :], got_pack[256:768, :], 1, 1
    )
    both_rows = jnp.concatenate([one.reshape(16, 16, 512), two.reshape(16, 16, 512)], axis=1)
    high = both_rows.astype(bf16).astype(f32)
    rest = both_rows - high
    norm = keep_norm[...] + got_norm[...]
    norm_high = norm.astype(bf16).astype(f32)
    lane = lax.broadcasted_iota(jnp.int32, (16, 128), 1)
    line = jnp.where(lane < 32, norm_high, pltpu.roll(norm - norm_high, 32, 1))[:, None, :]
    side = lax.broadcasted_iota(jnp.int32, (16, 32, 128), 2) < 64
    side = side & (lax.broadcasted_iota(jnp.int32, (16, 32, 128), 1) == 31)
    rest = jnp.concatenate([jnp.where(side, line, rest[:, :, :128]), rest[:, :, 128:]], axis=2)
    result[...] = jnp.concatenate([high, rest], axis=1).astype(bf16)


def pick(z, rows):
    blank = jnp.zeros((32, 512), f32)
    third = jnp.concatenate([rows[128:160], blank], axis=0)
    fourth = jnp.concatenate([rows[160:192], blank], axis=0)
    return jnp.where(
        z == 0, rows[0:64], jnp.where(z == 1, rows[64:128], jnp.where(z == 2, third, fourth))
    )


def everything(x):
    return jnp.sum(jnp.sum(x, axis=1, keepdims=True), axis=0, keepdims=True)


def reduce_body(
    parts, wide, wide_one, wide_two, wide_three, big_grad, small_grad, class_grad, head_grad, norm_two,
    scale, narrow, mine, squares, scale_out,
):
    sums = (wide[...] + wide_one[...]) + (wide_two[...] + wide_three[...])
    mine[...] = sums
    scale_out[...] = jnp.broadcast_to(scale[...], (8, 128))
    square = everything(class_grad[...] * class_grad[...])
    square = square + everything(jnp.sum(big_grad[...] * big_grad[...], axis=0))
    square = square + everything(jnp.sum(small_grad[...] * small_grad[...], axis=0))
    square = square + everything(head_grad[...] * head_grad[...])
    square = square + everything(norm_two[...] * norm_two[...])
    squares[...] = jnp.broadcast_to(square, (8, 128))
    total = jnp.sum(parts[...].astype(f32), axis=0)
    line = total[63:64, 0:128]
    lane = lax.broadcasted_iota(jnp.int32, (1, 128), 1)
    line = jnp.where(lane < 32, line + pltpu.roll(line, 96, 1), 0.0)
    row = lax.broadcasted_iota(jnp.int32, (32, 512), 0)
    lane = lax.broadcasted_iota(jnp.int32, (32, 512), 1)
    narrow[0:32, :] = total[:32] + jnp.where((row == 31) & (lane < 64), 0.0, total[32:])
    line = jnp.concatenate([line, jnp.zeros((1, 384), f32)], axis=1)
    narrow[32:40, :] = jnp.broadcast_to(line, (8, 512))
    narrow[40:48, :] = jnp.broadcast_to(everything(sums * sums), (8, 512))


def gather_body(
    z, wide, squares, narrow, narrow_one, narrow_two, narrow_three, scale,
    near, near_low, norm_one, message,
):
    rest = (narrow[...] + narrow_one[...]) + (narrow_two[...] + narrow_three[...])
    last = rest[:32]
    norm = rest[32:33, 0:128] * scale[0:1, :]
    norm_one[...] = jnp.broadcast_to(norm, (8, 128))
    square = squares[0:1, 0:1] + rest[40:41, 0:1] + everything(last * last) + everything(norm * norm)
    mine = jnp.where(z[0] == 3, jnp.concatenate([last, jnp.zeros((32, 512), f32)], axis=0), wide[...])
    near[...] = mine
    near.send()
    near_low[...] = mine.astype(bf16)
    near_low.send()
    high = square.astype(bf16)
    rest = square - high.astype(f32)
    mid = rest.astype(bf16)
    low = (rest - mid.astype(f32)).astype(bf16)
    rows16 = lax.broadcasted_iota(jnp.int32, (16, 512), 0)
    lanes16 = lax.broadcasted_iota(jnp.int32, (16, 512), 1)
    tail = jnp.where(
        lanes16 == 0,
        high.astype(f32),
        jnp.where(lanes16 == 1, mid.astype(f32), jnp.where(lanes16 == 2, low.astype(f32), 0.0)),
    )
    tail = jnp.where(rows16 == 0, tail, 0.0)
    line = jnp.concatenate([mine, tail], axis=0).astype(bf16)
    message[...] = jnp.broadcast_to(line[None], (16, 80, 512))


def split(x):
    high = x.astype(bf16)
    return high, (x - high.astype(f32)).astype(bf16)


def mul3(a, b):
    return dot(a[0], b[0]) + (dot(a[0], b[1]) + dot(a[1], b[0]))


def muon_body(
    k_place, z_place, got, got_other, moment, near, near_other, near_moment, near_moment_other,
    result, result_other, scalars, norm_out, u,
):
    k, z = k_place[0], z_place[0]

    def tails(ref):
        x = ref[:, 64:80, :].astype(f32)
        return jnp.sum(jnp.sum(x, axis=0), axis=0, keepdims=True)

    square = jnp.sum(tails(got) + tails(got_other), axis=1, keepdims=True)
    norm = jnp.sqrt(square)
    f = jnp.minimum(1.0, clip_limit / (norm + 1e-06))
    line = lax.broadcasted_iota(jnp.int32, (8, 128), 1)
    scalars[...] = jnp.where(line == 0, norm, f)
    norm_out[0, 0] = norm[0, 0]
    scalars.send()
    alpha = (1.0 + momentum_decay) * f
    beta = momentum_decay * momentum_decay
    first = jnp.where((z < 3) | (k == 0), 1.0, 0.0)
    second = jnp.where((z < 3) | (k == 1), 1.0, 0.0)
    parts = ((0, 16, first), (16, 32, second), (32, 64, jnp.float32(1.0)))
    for i, g in enumerate((got, got_other)):
        for y in range(16):
            for low, high, share in parts:
                value = (alpha * share) * g[y, low:high, :].astype(f32)
                value = value + (beta * share) * moment[i, y, low:high, :].astype(f32)
                at = i * 1024 + y * 64
                u[at + low : at + high, :] = value.astype(bf16)
    gram = dot(u[...], u[...], 0, 0)
    rows = lax.broadcasted_iota(jnp.int32, (512, 512), 0)
    cols = lax.broadcasted_iota(jnp.int32, (512, 512), 1)
    eye = (rows == cols).astype(f32)
    total = jnp.sum(jnp.sum(gram * eye, axis=0, keepdims=True), axis=1, keepdims=True)
    inverse = 1.0 / (jnp.sqrt(total) + 1e-07)
    a = gram * (inverse * inverse)
    x = jnp.concatenate(
        [
            (alpha * near[...] + beta * near_moment[...]) * inverse,
            (alpha * near_other[...] + beta * near_moment_other[...]) * inverse,
        ],
        axis=0,
    )
    for step in range(NS_STEPS - 1):
        a2 = split(a)
        square = mul3(a2, a2)
        m2 = split(coef_first * eye + coef_second * a + coef_third * square)
        x = mul3(split(x), m2)
        a = mul3(split(mul3(a2, m2)), m2)
    a2 = split(a)
    once = mul3(split(x), a2)
    x = coef_first * x + coef_second * once + coef_third * mul3(split(once), a2)
    result[...] = x[:64]
    result_other[...] = x[64:]


def adamw(weight, first, second, gradient, rate):
    first = beta_first * first + (1.0 - beta_first) * gradient
    second = beta_second * second + (1.0 - beta_second) * gradient * gradient
    ratio = (
        first / (1.0 - beta_first**STEP) / (jnp.sqrt(second / (1.0 - beta_second**STEP)) + 1e-08)
    )
    return (first, second, weight - rate * (ratio + weight_decay * weight))


def by_matrix(z, got):
    group = []
    for j in range(4):
        back = lax.rem(z - j + 4, 4)
        group.append(
            jnp.where(
                back == 0,
                got[0],
                jnp.where(back == 1, got[1], jnp.where(back == 2, got[2], got[3])),
            )
        )
    return [group[3][:16], group[3][16:32], group[0], group[1], group[2][:32]]


def finish_body(
    z, scalars, mine, one, two, three_back, class_grad, big_grad, small_grad, norm_one, norm_two, head_grad,
    *refs
):
    moments, refs = refs[:5], refs[5:]
    states, refs = refs[:15], refs[15:]
    fresh, updated = refs[:5], refs[5:]
    f = scalars[0:1, 1:2]
    rows = by_matrix(z[0], [mine[...], one[...], two[...], three_back[...]])
    for moment, row, out in zip(moments, rows, fresh):
        out[...] = momentum_decay * moment[...] + f * row.astype(f32)
        out.send()
    norm = norm_one[0:1, :]
    grads = [
        class_grad[:, :1000],
        big_grad[...],
        small_grad[...],
        jnp.concatenate([norm[:, 0:16], norm[:, 16:32], norm_two[...]], axis=0),
        head_grad[0:2, 0:32],
    ]
    rates = [adam_rate, adam_rate, adam_rate, norm_rate, norm_rate]
    for i in range(5):
        factor = f if grads[i].ndim == 2 else f.reshape(1, 1, 1)
        first, second, weight = adamw(
            states[3 * i][...], states[3 * i + 1][...], states[3 * i + 2][...],
            grads[i] * factor, rates[i],
        )
        updated[3 * i][...] = first
        updated[3 * i + 1][...] = second
        updated[3 * i + 2][...] = weight
        for j in range(3):
            updated[3 * i + j].send()


def renew_body(z, mine, one, two, three_back, *refs):
    weights, outs = refs[:5], refs[5:]
    rows = by_matrix(z[0], [mine[...], one[...], two[...], three_back[...]])
    for weight, row, (_, n), out in zip(weights, rows, PLACES, outs):
        rate = muon_rate * 0.2 * math.sqrt(max(512, 32 * n))
        out[...] = weight[...] * (1.0 - muon_rate * weight_decay) - rate * row.astype(f32)
        out.send()


def shards(
    features,
    labels,
    partner,
    class_weight,
    point_one,
    momentum_one,
    point_two,
    momentum_two,
    expand,
    momentum_up,
    shrink,
    momentum_down,
    transit,
    momentum_transit,
    classifier,
    classifier_first,
    classifier_second,
    big_kernel,
    big_first,
    big_second,
    small_kernel,
    small_first,
    small_second,
    norm_gains,
    gains_first,
    gains_second,
    head_gains,
    head_first,
    head_second,
):
    z = lax.axis_index("batch")
    c = lax.axis_index("chan")
    k = lax.rem(c, 2)
    crop = z * 32 + c
    widen = widen_matrix()
    compact = compact_matrix()
    k_scalar = k.reshape(1).astype(jnp.int32)
    classes = class_weight.shape[0]

    flat = features.astype(f32)
    local_mean = jnp.mean(flat, axis=(1, 2))
    local_spread = jnp.mean(jnp.square(flat - local_mean[:, None, None]), axis=(1, 2))
    vector = jnp.concatenate(
        [local_mean, local_spread, labels.astype(f32), partner.astype(f32)]
    )[None, :]
    paired = z_pair(vector)
    gathered = z_gather_rows(vector, paired)
    means = gathered[:, :16]
    center = jnp.mean(means, axis=0)
    variance = jnp.mean(gathered[:, 16:32], axis=0) + jnp.mean(
        jnp.square(means - center[None]), axis=0
    )
    people = jnp.stack([gathered[:, 32:64].reshape(128), gathered[:, 64:96].reshape(128)], axis=1)
    scale_own = lax.rsqrt(variance + epsilon)

    z_scalar = z.reshape(1).astype(jnp.int32)
    matrices = [w.T for w in (point_one, point_two, expand, shrink, transit)]
    moments = [
        m.T for m in (momentum_one, momentum_two, momentum_up, momentum_down, momentum_transit)
    ]
    head_line = jnp.stack(
        [
            jnp.pad(jnp.concatenate(three(head_gains[i])).astype(f32), (0, 32))
            for i in range(2)
        ]
    ).reshape(1, 256)
    head_line = jnp.pad(head_line, ((0, 0), (0, 256)))
    packed, packed_late, near_moment = whole(
        pack_body,
        [((176, 512), bf16), ((144, 512), bf16), ((64, 512), f32)], "pack",
        scalars=1,
        cost=3,

    )(
        z_scalar,
        *matrices[1:],
        classifier,
        moments[2],
        moments[3],
        moments[4],
        moments[0],
        moments[1],
        head_line,
    )
    weights = lax.all_gather(packed, "chan", axis=0, tiled=False).reshape(16, 2, 176, 512)
    late_weights = lax.all_gather(packed_late, "chan", axis=0, tiled=False)
    late_weights = late_weights.reshape(16, 2, 144, 512)
    near_moment_other = core_swap(near_moment)

    margin = (KB - KS) // 2
    kernel = big_kernel + jnp.pad(small_kernel, ((0, 0), (margin, margin), (margin, margin)))
    centre = kernel[:, 2:29, 2:29].astype(bf16)
    flat_kernel = jnp.pad(
        jnp.pad(centre, ((0, 0), (0, 0), (0, 5))).reshape(16, TAPS * 32), ((0, 0), (0, 48))
    )
    shifted = jnp.stack(
        [flat_kernel[:, 13 - px : 13 - px + 896] for px in range(S)]
        + [jnp.zeros((16, 896), bf16)] * 2,
        axis=1,
    ).reshape(256, 896)
    (table,) = whole(
        taps_body, [((16, 256, 256), bf16)], "taps", small_out=0
    )(shifted, compact)

    extra = []
    for item in (
        center,
        scale_own * norm_gains[0],
        norm_gains[1],
        norm_gains[2],
        norm_gains[3],
    ):
        extra += three(item)
    extra = jnp.stack(extra, axis=1)
    extra = jnp.pad(extra, ((0, 0), (0, 60 - extra.shape[1])))
    fixed = jnp.concatenate([extra, point_one.T.astype(bf16)], axis=1)
    payload = jnp.concatenate(
        [features.transpose(1, 0, 2), jnp.broadcast_to(fixed[None], (32,) + fixed.shape)], axis=2
    )
    came = lax.all_to_all(payload, "chan", 0, 0, tiled=True).reshape(512, 768)
    act_one, slope_one, a1 = whole(
        first_body, [((512, 256), bf16), ((512, 256), f32), ((512, 256), bf16)], "first", cost=4
    )(came)
    u = lax.all_to_all(act_one.reshape(32, 16, 256), "chan", 0, 0, tiled=True).transpose(1, 0, 2)
    mixed, act = whole(
        depth_forward_body, [((16, 32, 256), f32), ((16, 32, 256), bf16)], "depth_forward", cost=4,
    )(u, table, widen)
    gd = lax.all_to_all(act.transpose(1, 0, 2), "chan", 0, 0, tiled=True).reshape(512, 256)

    middle, gains, stats = whole(
        middle_body,
        [((208, 512), f32), ((8, 512), f32), ((128, 8, 128), f32)],
        "middle",
        cost=4,
        pieces={2: [natural(0, 16)]},
    )(came, gd, weights)
    stats = lax.all_to_all(stats, both, 0, 0, tiled=True)
    normal_two, factor_two, pack_one, keep_act, hid, t, pooled = whole(
        forward_body,
        [
            ((208, 512), f32),
            ((8, 512), f32),
            ((256, 2048), bf16),
            ((256, 1024), bf16),
            ((208, 2048), f32),
            ((208, 1024), f32),
            ((128, 8, 128), f32),
        ],
        "forward",
        cost=4,
        scalars=1,
        pieces={3: [own_first(16, 64), own_first(80, 64), own_first(144, 32)]},
    )(k_scalar, stats, middle, gains, weights)
    pooled = lax.all_to_all(pooled, both, 0, 0, tiled=True)
    slope_hid, slope_t = whole(
        slopes_body, [((208, 2048), f32), ((208, 1024), f32)], "slopes"
    )(hid, t)
    place = jnp.stack([k, crop, k * 512 + (c // 2) * 32]).astype(jnp.int32)
    pack_two, keep_hid, keep_t, dx2, da2, sums, z_low, dlogits, head_rows, loss_sum, weight_sum = whole(
        head_body,
        [
            ((256, 2048), bf16),
            ((256, 1024), bf16),
            ((256, 512), bf16),
            ((208, 512), f32),
            ((208, 512), f32),
            ((128, 8, 128), f32),
            ((128, 1024), bf16),
            ((128, 1024), bf16),
            ((8, 1024), f32),
        ],
        "head",
        scalar_outs=2,
        cost=4,
        scalars=1,
        pieces={
            3: [
                by_core(128, 16),
                by_core(0, 64),
            ],
            4: [
                own_first(144, 32),
                own_first(80, 64),
                own_first(16, 64),
            ]
        },
    )(
        place,
        pooled,
        people,
        jnp.pad(class_weight, (0, 1024 - classes))[None, :],
        late_weights,
        weights,
        slope_t,
        slope_hid,
        normal_two,
    )
    sums = lax.all_to_all(sums, both, 0, 0, tiled=True)
    class_grad, head_grad = whole(
        classes_body, [((32, 1024), f32), ((8, 128), f32)], "classes", scalars=1
    )(place, z_low, dlogits, head_rows)

    (wide_parts,) = whole(
        outer_body,
        [((16, 160, 512), f32)],
        "outer",
        parts={0: [np.s_[:, 64:128], np.s_[:, 0:64], np.s_[:, 128:160]]},
    )(
        keep_act, keep_hid, keep_t, pack_one, pack_two, core_swap(pack_one), core_swap(pack_two)
    )
    wide_sum = lax.psum_scatter(
        wide_parts, "chan", scatter_dimension=0, axis_index_groups=same_core()
    )

    keep_two, pack_three, dgd, norm_two = whole(
        second_body,
        [((256, 256), bf16), ((1280, 256), bf16), ((512, 256), bf16), ((8, 128), f32)],
        "second",
        cost=BACK,
        scalars=1,
        pieces={5: [natural(0, 16)]},
    )(k_scalar, sums, da2, normal_two, factor_two, dx2, weights, gd, a1)
    grad_mixed = lax.all_to_all(
        dgd.reshape(32, 16, 256), "chan", 0, 0, tiled=True
    ).transpose(1, 0, 2)
    back, tap_grad = whole(
        depth_backward_body,
        [((16, 32, 256), bf16), ((16, 1024), f32)],
        "depth_backward",
        small_in=0,
        cost=BACK,
        scratch=[pltpu.VMEM((16, 256, 512), f32), pltpu.VMEM((16, 16, 1024), f32)],
    )(u, mixed, grad_mixed, table, widen, compact)
    du1 = lax.all_to_all(back.transpose(1, 0, 2), "chan", 0, 0, tiled=True).reshape(512, 256)
    keep_one, send_one, keep_norm, send_norm, tap_grad = whole(
        third_body,
        [
            ((256, 256), bf16),
            ((256, 256), bf16),
            ((16, 128), f32),
            ((16, 128), f32),
            ((16, 1024), f32),
        ],
        "third",
        cost=BACK,
        scalars=1,
    )(k_scalar, came, du1, slope_one, tap_grad, *z_shifts(tap_grad))
    (narrow_parts,) = whole(last_outer_body, [((16, 64, 512), bf16)], "last_outer", cost=BACK)(
        keep_one,
        keep_two,
        pack_three,
        core_swap(send_one),
        core_swap(pack_three),
        keep_norm,
        core_swap(send_norm),
    )
    big_grad = tap_grad[:, :864].reshape(16, TAPS, 32)[:, :, :TAPS]
    big_grad = jnp.pad(big_grad, ((0, 0), (2, 2), (2, 2)))
    small_grad = big_grad[:, margin : margin + KS, margin : margin + KS].transpose(1, 2, 0)
    big_grad = big_grad.transpose(1, 0, 2)
    norm_two_own = lax.dynamic_slice_in_dim(norm_two.reshape(2, 512), c * 16, 16, 1)
    line = jnp.concatenate([scale_own, jnp.ones((16,), f32), jnp.zeros((96,), f32)])
    scale_line = line[None]
    wide_sum = jnp.pad(wide_sum.reshape(160, 512), ((0, 96), (0, 0)))

    def for_group(j):
        return lax.dynamic_slice_in_dim(wide_sum, 64 * lax.rem(z + j, 4), 64, 0)

    narrow_sum, mine_wide, squares, scale_line = whole(
        reduce_body,
        [((48, 512), f32), ((64, 512), f32), ((8, 128), f32), ((8, 128), f32)], "reduce", cost=4
    )(
        groups_all_to_all(narrow_parts),
        for_group(0),
        *[
            lax.ppermute(for_group(j), "batch", [(i, (i + j) % 4) for i in range(4)])
            for j in range(1, 4)
        ],
        big_grad,
        small_grad,
        class_grad,
        head_grad,
        norm_two_own,
        scale_line,
    )
    near, near_low, norm_one, message = whole(
        gather_body,
        [((64, 512), f32), ((64, 512), bf16), ((8, 128), f32), ((16, 80, 512), bf16)],
        "gather",
        scalars=1,
        cost=4,
    )(z_scalar, mine_wide, squares, narrow_sum, *z_shifts(narrow_sum), scale_line)
    near_shifts = z_shifts(near_low)
    arrived = sum(item[0, 0].astype(f32) for item in near_shifts) < 1e30
    got = groups_all_to_all(message)
    got = jnp.where(arrived, got, -got)
    near_other = core_swap(near)
    near_rows, near_rows_other, scalars, grad_norm = whole(
        muon_body,
        [((64, 512), f32), ((64, 512), f32), ((8, 128), f32)],
        "muon",
        cost=4,
        scratch=[pltpu.VMEM((2048, 512), bf16)],
        scalars=2,
        scalar_outs=1,
        pieces={2: [own_first(64, 64)]},
    )(
        k_scalar,
        z_scalar,
        got,
        core_swap(got),
        late_weights,
        near,
        near_other,
        near_moment,
        near_moment_other,
    )
    row = np.arange(64)
    first_rows = jnp.asarray((row < 16).astype(np.float32))
    second_rows = jnp.asarray(((row >= 16) & (row < 32)).astype(np.float32))
    own_rows = jnp.where(z < 3, 1.0, jnp.where(k == 0, first_rows, second_rows))[:, None]
    mine_result = jnp.where(own_rows > 0, near_rows, core_swap(near_rows_other)).astype(bf16)
    def turn_big(x):
        return x.transpose(1, 0, 2)

    def turn_small(x):
        return x.transpose(1, 2, 0)

    states = [
        *(classifier, classifier_first, classifier_second),
        *(turn_big(x) for x in (big_kernel, big_first, big_second)),
        *(turn_small(x) for x in (small_kernel, small_first, small_second)),
        *(norm_gains, gains_first, gains_second),
        *(head_gains, head_first, head_second),
    ]
    updates = whole(
        finish_body, [(x.shape, f32) for x in moments + states], "finish", scalars=1, cost=6
    )(
        z_scalar,
        scalars,
        near_low,
        *near_shifts,
        class_grad,
        big_grad,
        small_grad,
        norm_one,
        norm_two_own,
        head_grad,
        *moments,
        *states,
    )
    renewed = whole(
        renew_body, [(m.shape, f32) for m in matrices], "renew", scalars=1, cost=4
    )(z_scalar, mine_result, *z_shifts(mine_result), *matrices)
    pairs = [item.T for pair in zip(renewed, updates[:5]) for item in pair]
    states = list(updates[5:])
    states[3:6] = [x.transpose(1, 0, 2) for x in states[3:6]]
    states[6:9] = [x.transpose(2, 0, 1) for x in states[6:9]]
    return (
        loss_sum.reshape(()), weight_sum.reshape(()), grad_norm.reshape(()), *pairs, *states
    )


def solution(mesh):
    split_columns = P(None, "chan")
    split_rows = P("chan", None)
    split_first = P("chan", None, None)
    in_specs = (
        (P("chan", "batch", None), P("batch"), P("batch"), P())
        + (split_columns,) * 10
        + (split_rows,) * 3
        + (split_first,) * 6
        + (split_columns,) * 6
    )
    out_specs = (
        (P(), P(), P())
        + (split_columns,) * 10
        + (split_rows,) * 3
        + (split_first,) * 6
        + (split_columns,) * 6
    )
    return jax.shard_map(shards, mesh=mesh, in_specs=in_specs, out_specs=out_specs, check_vma=False)
```

```python
import math

import jax
import jax.numpy as jnp
import numpy as np
from jax import lax
from jax.experimental import pallas as pl
from jax.experimental.pallas import tpu as pltpu
from jax.sharding import PartitionSpec as P

S = 14
KB = 31
KS = 5
NS_STEPS = 5
STEP = 10
AREA = S * S
WIDE = S * 16
TAPS = 2 * S - 1

f32 = jnp.float32
bf16 = jnp.bfloat16
epsilon = 1e-05
highest = lax.Precision.HIGHEST
coef_first = 3.4445
coef_second = -4.775
coef_third = 2.0315
clip_limit = 0.05
momentum_decay = 0.95
muon_rate = 0.05
adam_rate = 0.05
norm_rate = 0.2
beta_first = 0.9
beta_second = 0.95
weight_decay = 0.01
root_two_pi = math.sqrt(2.0 / math.pi)
both = ("batch", "chan")
BACK = 25
SMALL = 0
PLACES = ((160, 16), (176, 16), (0, 64), (64, 64), (128, 32))


def dot(a, b, left=1, right=0, precision=None):
    return lax.dot_general(
        a, b, (((left,), (right,)), ((), ())), precision=precision, preferred_element_type=f32
    )


def gelu_pair(x):
    square = x * x
    t = jnp.tanh(root_two_pi * x * (1.0 + 0.044715 * square))
    half = 0.5 * (1.0 + t)
    slope = half + 0.5 * x * (1.0 - t * t) * (root_two_pi * (1.0 + 0.134145 * square))
    return x * half, slope


def three(x):
    high = lax.reduce_precision(x, 8, 7)
    rest = x - high
    mid = lax.reduce_precision(rest, 8, 7)
    return [high.astype(bf16), mid.astype(bf16), (rest - mid).astype(bf16)]


def core_swap(x):
    return lax.ppermute(x, "chan", [(i, i ^ 1) for i in range(32)])


def same_core():
    return [[2 * i + k for i in range(16)] for k in range(2)]


def z_shifts(x):
    return [lax.ppermute(x, "batch", [(i, (i + k) % 4) for i in range(4)]) for k in range(1, 4)]


def groups_all_to_all(x):
    return lax.all_to_all(x, "chan", 0, 0, tiled=True, axis_index_groups=same_core())


def z_pair(x):
    return lax.ppermute(x, "batch", [(0, 1), (1, 0), (2, 3), (3, 2)])


def z_cross(x):
    return lax.ppermute(x, "batch", [(0, 3), (3, 0), (1, 2), (2, 1)])


def z_gather_rows(x, near):
    z = lax.axis_index("batch")
    far = z_cross(jnp.concatenate([x, near], axis=0))
    rows = []
    for j in range(4):
        at = jnp.bitwise_xor(z, j)
        cross = jnp.where(j == 3 - z, far[0:1], far[1:2])
        rows.append(jnp.where(at == 0, x, jnp.where(at == 1, near, cross)))
    return jnp.concatenate(rows, axis=0)


def widen_matrix():
    e = np.zeros((256, 256), np.float32)
    for y in range(S):
        for x in range(S):
            e[y * S + x, y * 16 + x] = 1
    return jnp.asarray(e, bf16)


def compact_matrix():
    e = np.zeros((896, 512), np.float32)
    for f in range(TAPS):
        for x in range(S):
            e[f * 32 + x, f * S + x] = 1
    return jnp.asarray(e, bf16)


class Source:
    def __init__(self, buffer, copies):
        self.buffer = buffer
        self.copies = copies

    def ready(self):
        for copy in self.copies:
            copy.wait()
        self.copies = []

    def __getitem__(self, index):
        self.ready()
        return self.buffer[index]


class Target:
    def __init__(self, buffer, copies):
        self.buffer = buffer
        self.copies = copies
        self.sent = set()

    def __getitem__(self, index):
        return self.buffer[index]

    def __setitem__(self, index, value):
        self.buffer[index] = value

    @property
    def shape(self):
        return self.buffer.shape

    def send(self, part=None):
        for j in range(len(self.copies)):
            if j not in self.sent and part in (None, j):
                self.copies[j].start()
                self.sent.add(j)

    def finish(self):
        for copy in self.copies:
            copy.wait()


def whole(
    body, outs, name, scratch=(), scalars=0, limit=54, pieces=None, cost=2, small_in=SMALL, small_out=SMALL,
    parts=None, scalar_outs=0, near=(),
):
    pieces = pieces or {}
    parts = parts or {}

    def call(*args):
        arrays = args[scalars:]
        loads = []
        for i, array in enumerate(arrays):
            for load in pieces.get(i, [None]):
                loads.append((i, load))
        sizes = [array.size * array.dtype.itemsize for array in arrays]
        direct = [i in near or (i not in pieces and sizes[i] <= small_in) for i in range(len(arrays))]
        out_sizes = [math.prod(shape) * jnp.dtype(kind).itemsize for shape, kind in outs]
        direct_out = [size <= small_out for size in out_sizes]
        direct_out += [True] * scalar_outs
        moved = [(i, load) for i, load in loads if not direct[i]]
        moved_out = [item for item, near in zip(outs, direct_out) if not near]
        n_out_copies = sum(
            len(parts.get(j, [None])) for j, near in enumerate(direct_out) if not near
        )
        n_results = len(outs) + scalar_outs
        buffers = [
            pltpu.VMEM(arrays[i].shape if load is None else load[0], arrays[i].dtype)
            for i, load in moved
        ]
        n_copies = sum(1 if load is None else load[2] for _, load in moved)
        n_in, n_load, n_out, n_moved = len(arrays), len(moved), len(outs), len(moved_out)

        def kernel(*refs):
            small = refs[:scalars]
            refs = refs[scalars:]
            ins, refs = refs[:n_in], refs[n_in:]
            results, refs = refs[:n_results], refs[n_results:]
            in_buffers, refs = list(refs[:n_load]), refs[n_load:]
            out_buffers, refs = list(refs[:n_moved]), refs[n_moved:]
            in_sems, out_sems, rest = refs[0], refs[1], refs[2:]
            count = 0
            sources = []
            for i, load in loads:
                if direct[i]:
                    sources.append(Source(ins[i], []))
                    continue
                buffer = in_buffers.pop(0)
                ways = [(ins[i], buffer)] if load is None else load[1](ins[i], buffer, small)
                copies = []
                for origin, to in ways:
                    copy = pltpu.make_async_copy(origin, to, in_sems.at[count])
                    copy.start()
                    copies.append(copy)
                    count += 1
                sources.append(Source(buffer, copies))
            targets = []
            count = 0
            for j, (result, near) in enumerate(zip(results, direct_out)):
                if near:
                    targets.append(Target(result, []))
                    continue
                buffer = out_buffers.pop(0)
                copies = []
                for part in parts.get(j, [None]):
                    origin, to = buffer, result
                    if part is not None:
                        origin, to = buffer.at[part], result.at[part]
                    copies.append(pltpu.make_async_copy(origin, to, out_sems.at[count]))
                    count += 1
                targets.append(Target(buffer, copies))
            body(*small, *sources, *targets, *rest)
            for source in sources:
                source.ready()
            for target in targets:
                target.send()
            for target in targets:
                target.finish()

        near_space = pl.BlockSpec(memory_space=pltpu.VMEM)
        far_space = pl.BlockSpec(memory_space=pl.ANY)
        return pl.pallas_call(
            kernel,
            out_shape=[jax.ShapeDtypeStruct(*item) for item in outs]
            + [jax.ShapeDtypeStruct((1, 1), f32)] * scalar_outs,
            in_specs=[pl.BlockSpec(memory_space=pltpu.SMEM)] * scalars
            + [near_space if near else far_space for near in direct],
            out_specs=[near_space if near else far_space for near in direct_out[:n_out]]
            + [pl.BlockSpec(memory_space=pltpu.SMEM)] * scalar_outs,
            scratch_shapes=buffers
            + [pltpu.VMEM(*item) for item in moved_out]
            + [
                pltpu.SemaphoreType.DMA((max(n_copies, 1),)),
                pltpu.SemaphoreType.DMA((max(n_out_copies, 1),)),
            ]
            + list(scratch),
            name=name,
            cost_estimate=pl.CostEstimate(
                flops=cost * 1_000_000_000, bytes_accessed=0, transcendentals=0
            ),
            compiler_params=pltpu.CompilerParams(vmem_limit_bytes=limit * 1024 * 1024),
        )(*args)

    return call


def own_first(start, rows):
    def ways(origin, to, small):
        k = small[0][0]
        part = pl.ds(start, rows)
        return [(origin.at[:, k, part, :], to.at[0]), (origin.at[:, 1 - k, part, :], to.at[1])]

    return ((2, 16, rows, 512), ways, 2)


def by_core(start, rows):
    def ways(origin, to, small):
        part = pl.ds(start, rows)
        return [(origin.at[:, 0, part, :], to.at[0]), (origin.at[:, 1, part, :], to.at[1])]

    return ((2, 16, rows, 512), ways, 2)


def natural(start, rows):
    def ways(origin, to, small):
        return [(origin.at[:, :, pl.ds(start, rows), :], to)]

    return ((16, 2, rows, 512), ways, 1)


def block(ref, half, i, rows):
    n = 256 // rows
    return ref[half, i * n : (i + 1) * n].reshape(256, 512)


def half_of(ref, half, rows):
    return ref[half].reshape(16 * rows, 512)


def valid(rows):
    return lax.broadcasted_iota(jnp.int32, (rows, 256), 1) < AREA


def column(tail, i):
    at = AREA - 128 + 3 * i
    return (tail[:, at : at + 1] + tail[:, at + 1 : at + 2]) + tail[:, at + 2 : at + 3]


def row_sums(x):
    return dot(jnp.ones((8, x.shape[1]), f32), x, 1, 1, highest)[0:1]


def pack_row(row):
    return jnp.concatenate([row[:, j * 128 : (j + 1) * 128] for j in range(8)], axis=0)


def by_turn(k, rows):
    four = rows.reshape(16, 2, 16, 256)
    first, second = four[:, 0].reshape(256, 256), four[:, 1].reshape(256, 256)
    return jnp.where(k == 0, first, second), jnp.where(k == 0, second, first)


def pack_body(z, two, up, down, transit, classes, m_up, m_down, m_transit, m_one, m_two, line, packed, late, near):
    packed[0:16, :] = two[...].astype(bf16)
    packed[16:80, :] = up[...].astype(bf16)
    packed[80:144, :] = down[...].astype(bf16)
    packed[144:176, :] = transit[...].astype(bf16)
    late[0:32, :] = classes[:, 0:512].astype(bf16)
    late[32:64, :] = jnp.concatenate(
        [classes[:, 512:1000], jnp.zeros((32, 24), f32)], axis=1
    ).astype(bf16)
    rows = jnp.concatenate([m_up[...], m_down[...], m_transit[...], m_one[...], m_two[...]], axis=0)
    mine = pick(z[0], rows)
    near[...] = mine
    near.send()
    late[64:128, :] = mine.astype(bf16)
    late[128:144, :] = jnp.concatenate([line[...], jnp.zeros((15, 512), f32)], axis=0).astype(bf16)


def taps_body(shifted, compact, table):
    z = dot(shifted[...], compact[...])
    keep = valid(256)
    for py in range(S):
        at = (S - 1 - py) * S
        rows = jnp.where(keep, z[:, at : at + 256], 0.0).astype(bf16)
        table[:, py * 16 : (py + 1) * 16, :] = rows.reshape(16, 16, 256)
    table[:, WIDE:, :] = jnp.zeros((16, 256 - WIDE, 256), bf16)


def first_body(came, act, slope, normed):
    tail = came[:, 128:256].astype(f32)
    x = came[:, :256].astype(f32) - column(tail, 0)
    a = jnp.where(valid(512), x * column(tail, 1) + column(tail, 2), 0.0).astype(bf16)
    normed[...] = a
    for i in range(2):
        rows = pl.ds(i * 256, 256)
        h = dot(came[rows, 256:768], a)
        act[rows, :] = gelu_pair(h)[0].astype(bf16)
        slope[rows, :] = h


def slope_body(x, slope):
    slope[...] = gelu_pair(x[...])[1]


def depth_forward_body(u, table, widen, mixed, act):
    for c in range(16):
        wide = dot(u[c], widen[...]).astype(bf16)
        d = dot(wide, table[c])
        mixed[c] = d
        act[c] = gelu_pair(d)[0].astype(bf16)


def tall(rows):
    return jnp.concatenate([rows, jnp.zeros((48, rows.shape[1]), rows.dtype)], axis=0)


def pixel_rows():
    return lax.broadcasted_iota(jnp.int32, (208, 512), 0) < AREA


def unpack_row(packed, h):
    return jnp.concatenate([packed[j : j + 1] for j in range(4 * h, 4 * h + 4)], axis=1)


def middle_body(came, gd, weight, middle, gains, stats):
    turned = came[:, :256].astype(f32).T
    for i in range(2):
        at = AREA + 9 + 3 * i
        gains[i : i + 1, :] = (turned[at : at + 1] + turned[at + 1 : at + 2]) + turned[at + 2 : at + 3]
    gains[2:8, :] = jnp.zeros((6, 512), f32)
    keep = pixel_rows()
    product = dot(gd[...], weight[...].reshape(512, 512), 0, 1)
    x = jnp.where(keep, turned[:208], 0.0) + product[:208]
    middle[...] = x
    middle.send()
    mean = jnp.sum(x, axis=0, keepdims=True) * (1.0 / AREA)
    apart = jnp.where(keep, x - mean, 0.0)
    spread = jnp.sum(apart * apart, axis=0, keepdims=True) * (1.0 / AREA)
    row = jnp.concatenate([mean, spread], axis=1)
    stats[...] = jnp.broadcast_to(pack_row(row)[None], (128, 8, 128))


def forward_body(
    k, stats, middle, gains, up, down, transit, normal, factor, pack, keep_act, slope_hid, slope_t, pooled
):
    parts = stats[...]
    total = jnp.sum(parts, axis=0) * (1.0 / 128)
    apart = parts - total[None]
    spread = jnp.sum(apart * apart, axis=0) * (1.0 / 128)
    center = unpack_row(total, 0)
    scale = lax.rsqrt(unpack_row(total, 1) + unpack_row(spread, 0) + epsilon)
    gain, shift = gains[0:1, :], gains[1:2, :]
    keep = pixel_rows()
    x1 = middle[...]
    xh = (x1 - center) * scale
    normal[...] = jnp.where(keep, xh, 0.0)
    normal.send()
    factor[...] = jnp.broadcast_to(gain * scale, (8, 512))
    a2 = jnp.where(keep, xh * gain + shift, 0.0).astype(bf16)
    pack[:, 1536:2048] = tall(a2)
    for i in range(8):
        hid = dot(a2, block(up, i // 4, i % 4, 64), 1, 1)
        low = tall(gelu_pair(hid)[0].astype(bf16))
        slope_hid[:, i * 256 : (i + 1) * 256] = hid
        if i < 4:
            keep_act[:, i * 256 : (i + 1) * 256] = low
        else:
            pack[:, (i - 4) * 256 : (i - 3) * 256] = low
    slope_hid.send()
    keep_act.send()
    total = x1 + dot(keep_act[:208, :], half_of(down, 0, 64))
    total = total + dot(pack[:208, :1024], half_of(down, 1, 64))
    x2 = total.astype(bf16)
    pack[:, 1024:1536] = tall(x2)
    pack.send()
    halves = []
    for i in range(2):
        t = dot(x2, half_of(transit, i, 32), 1, 1)
        slope_t[:, i * 512 : (i + 1) * 512] = t
        halves.append(jnp.sum(gelu_pair(t)[0], axis=0, keepdims=True) * (1.0 / AREA))
    turn = k[0] == 1
    row = jnp.concatenate(
        [jnp.where(turn, halves[1], halves[0]), jnp.where(turn, halves[0], halves[1])], axis=1
    )
    pooled[...] = jnp.broadcast_to(pack_row(row)[None], (128, 8, 128))


def slopes_body(hid, t, slope_hid, slope_t):
    for i in range(8):
        lanes = slice(i * 256, (i + 1) * 256)
        slope_hid[:, lanes] = gelu_pair(hid[:, lanes])[1]
    slope_hid.send()
    keep = pixel_rows()
    for i in range(2):
        lanes = slice(i * 512, (i + 1) * 512)
        slope_t[:, lanes] = jnp.where(keep, gelu_pair(t[:, lanes])[1], 0.0)


def head_body(
    place,
    pooled,
    people,
    class_weight,
    gains,
    classes,
    transit,
    down,
    up,
    slope_t,
    slope_hid,
    normal,
    pack,
    keep_hid,
    keep_t,
    dx2,
    da2,
    sums,
    z_out,
    dl_out,
    head_rows,
    loss_out,
    weight_out,
):
    k, crop = place[0], place[1]
    owner_rows = gains[:, :, 0:8, :].reshape(32, 8, 512)[:, 0, :].astype(f32)
    fold_rows = lax.broadcasted_iota(jnp.int32, (32, 1024), 0)
    fold_lanes = lax.broadcasted_iota(jnp.int32, (32, 1024), 1)
    expand = (fold_lanes % 32 == fold_rows).astype(f32)
    keep = fold_lanes // 32 == fold_rows

    def gain_row(i):
        at_lane = 128 * i
        parts = [owner_rows[:, at_lane + 32 * j : at_lane + 32 * j + 32] for j in range(3)]
        parts = jnp.concatenate([(parts[0] + parts[1]) + parts[2], jnp.zeros((32, 96), f32)], axis=1)
        full = jnp.concatenate([expand, jnp.zeros((96, 1024), f32)], axis=0)
        spread = dot(parts, full, 1, 0, highest)
        return jnp.sum(jnp.where(keep, spread, 0.0), axis=0, keepdims=True)

    gain = gain_row(0)
    shift = gain_row(1)
    x = jnp.concatenate([pooled[:, j, :] for j in range(8)], axis=1)
    center = jnp.sum(x, axis=0, keepdims=True) * (1.0 / 128)
    apart = x - center
    scale = lax.rsqrt(jnp.sum(apart * apart, axis=0, keepdims=True) * (1.0 / 128) + epsilon)
    xh = apart * scale
    z = (xh * gain + shift).astype(bf16)
    z_out[...] = z
    z_out.send()
    left = classes[:, :, 0:32].reshape(1024, 512)
    right = classes[:, :, 32:64].reshape(1024, 512)
    logits = jnp.concatenate([dot(z, left), dot(z, right)], axis=1)
    lanes = lax.broadcasted_iota(jnp.int32, (128, 128), 1)
    rows = lax.broadcasted_iota(jnp.int32, (128, 128), 0)
    pairing = (people[:, 1:2] == lanes.astype(f32)).astype(f32)
    average = 0.5 * (logits + dot(pairing, logits, 1, 0, highest))
    wide = lax.broadcasted_iota(jnp.int32, (128, 1024), 1)
    average = jnp.where(wide < 1000, average, -1e30)
    top = jnp.max(average, axis=1, keepdims=True)
    moved = average - top
    expo = jnp.exp(moved)
    norm = jnp.sum(expo, axis=1, keepdims=True)
    onehot = (people[:, 0:1] == wide.astype(f32)).astype(f32)
    weight = 0.5 * jnp.sum(onehot * class_weight[...], axis=1, keepdims=True)
    picked = jnp.sum(jnp.where(onehot > 0, moved, 0.0), axis=1, keepdims=True) - jnp.log(norm)
    weight_sum = jnp.sum(weight, axis=0, keepdims=True)
    loss_sum = -jnp.sum(weight * picked, axis=0, keepdims=True)
    loss_out[0, 0] = loss_sum[0, 0]
    weight_out[0, 0] = weight_sum[0, 0]
    dl = ((weight / weight_sum) * (expo / norm - onehot)).astype(bf16)
    dl_out[...] = dl
    dl_out.send()
    dz = dot(dl[:, :512], left, 1, 1) + dot(dl[:, 512:], right, 1, 1)
    dshift = jnp.sum(dz, axis=0, keepdims=True)
    dgain = jnp.sum(dz * xh, axis=0, keepdims=True)
    dp = (gain * scale) * (dz - (dshift + xh * dgain) * (1.0 / 128))
    crops = lax.broadcasted_iota(jnp.int32, (128, 1024), 0)
    mine = jnp.sum(jnp.where(crops == crop, dp, 0.0), axis=0, keepdims=True) * (1.0 / AREA)
    turn = k == 1
    first = jnp.where(turn, mine[:, 512:], mine[:, :512])
    second = jnp.where(turn, mine[:, :512], mine[:, 512:])

    part = (slope_t[:, :512] * first).astype(bf16)
    keep_t[...] = tall(part)
    keep_t.send()
    grad = dot(part, half_of(transit, 0, 32))
    part = (slope_t[:, 512:] * second).astype(bf16)
    pack[:, 1024:1536] = tall(part)
    grad = grad + dot(part, half_of(transit, 1, 32))
    dx2[...] = grad
    dx2.send()
    low = grad.astype(bf16)
    pack[:, 1536:2048] = tall(low)
    for i in range(8):
        lanes256 = slice(i * 256, (i + 1) * 256)
        part = slope_hid[:, lanes256] * dot(low, block(down, i // 4, i % 4, 64), 1, 1)
        part = tall(part.astype(bf16))
        if i < 4:
            keep_hid[:, lanes256] = part
        else:
            pack[:, (i - 4) * 256 : (i - 3) * 256] = part
    pack.send()
    keep_hid.send()
    grad = dot(keep_hid[:208, :], half_of(up, 0, 64))
    grad = grad + dot(pack[:208, :1024], half_of(up, 1, 64))
    da2[...] = grad
    da2.send()
    row = jnp.concatenate(
        [jnp.sum(grad * normal[...], axis=0, keepdims=True), jnp.sum(grad, axis=0, keepdims=True)],
        axis=1,
    )
    sums[...] = jnp.broadcast_to(pack_row(row)[None], (128, 8, 128))
    sums.send()
    head_rows[...] = jnp.concatenate([dgain, dshift, jnp.zeros((6, 1024), f32)], axis=0)


def classes_body(place, z, dl, head_rows, class_grad, head_grad):
    own_rows = lax.broadcasted_iota(jnp.int32, (1024, 128), 0)
    own_lanes = lax.broadcasted_iota(jnp.int32, (1024, 128), 1)
    select = ((own_rows == own_lanes + place[2]) & (own_lanes < 32)).astype(f32)
    z_own = dot(z[...], select.astype(bf16)).astype(bf16)
    class_grad[...] = dot(z_own, dl[...], 0, 0)[:32]
    head_grad[...] = dot(head_rows[...], select, 1, 0, highest)


def outer_body(keep_act, keep_hid, keep_t, one, two, one_in, two_in, result):
    def place(part, rows, v, rows_in, v_in, n):
        for i in range(2):
            half = slice(i * 8 * n, (i + 1) * 8 * n)
            block_rows = dot(rows[:, half], v, 0, 0) + dot(rows_in[:, half], v_in, 0, 0)
            result[i * 8 : (i + 1) * 8, part, :] = block_rows.reshape(8, n, 512)

    wide, thin = slice(0, 1024), slice(1024, 1536)
    last = slice(1536, 2048)
    place(slice(64, 128), keep_act[...], two[:, last], one_in[:, wide], two_in[:, last], 64)
    result.send(0)
    place(slice(0, 64), keep_hid[...], one[:, last], two_in[:, wide], one_in[:, last], 64)
    result.send(1)
    place(slice(128, 160), keep_t[...], one[:, thin], two_in[:, thin], one_in[:, thin], 32)
    result.send(2)


def second_body(k, sums, da2, normal, factor, dx2, weight, gd, normed, keep_rows, pack, back, norm):
    total = jnp.sum(sums[...], axis=0)
    norm[...] = total
    gain, shift = unpack_row(total, 0), unpack_row(total, 1)
    inner = da2[...] - (shift + normal[...] * gain) * (1.0 / (128 * AREA))
    grad = dx2[...] + jnp.where(pixel_rows(), factor[0:1, :] * inner, 0.0)
    low = tall(grad).T.astype(bf16)
    keep, send = by_turn(k[0], low)
    keep_rows[...] = keep
    pack[0:256, :] = send
    pack[256:768, :] = gd[...]
    pack[768:1280, :] = normed[...]
    back[...] = dot(weight[...].reshape(512, 512), low, 0, 0).astype(bf16)


def depth_backward_body(u, mixed, grad, table, widen, compact, back, taps, outer, spread):
    outer[...] = jnp.zeros_like(outer)
    for c in range(16):
        wide = dot(u[c], widen[...]).astype(bf16)
        slope = mixed[c]
        dd = (grad[c].astype(f32) * slope).astype(bf16)
        du = dot(dd, table[c], 1, 1).astype(bf16)
        back[c] = dot(du, widen[...], 1, 1).astype(bf16)
        outer[c, :, :256] = dot(wide, dd, 0, 0)
    total = jnp.zeros((256, 512), f32)
    for py in range(S):
        rows = outer[:, py * 16 : (py + 1) * 16, :].reshape(256, 512)
        at = (S - 1 - py) * S
        total = total + (pltpu.roll(rows, at, 1) if at else rows)
    back.send()
    wide = dot(total, compact[...].astype(f32), 1, 1, highest)
    spread[:, :, :896] = wide.reshape(16, 16, 896)
    spread[:, :, 896:] = jnp.zeros((16, 16, 128), f32)
    taps[...] = sum(pltpu.roll(spread[:, px, :], 13 - px, 1) for px in range(13)) + spread[:, 13, :]


def third_body(
    k, came, du, slope, tap, tap_one, tap_two, tap_three, keep_rows, send_rows, keep_norm, send_norm, tap_sum
):
    tap_sum[...] = (tap[...] + tap_one[...]) + (tap_two[...] + tap_three[...])
    tail = came[:, 128:256].astype(f32)
    dh = (slope[...] * du[...].astype(f32)).astype(bf16)
    keep, send = by_turn(k[0], dh)
    keep_rows[...] = keep
    send_rows[...] = send
    da = dot(came[:, 256:768], dh, 0, 0)
    x = came[:, :256].astype(f32) - column(tail, 0)
    gain, shift = row_sums(da * x), row_sums(da)
    ys = lax.broadcasted_iota(jnp.int32, (16, 512), 0)
    owner = lax.broadcasted_iota(jnp.int32, (16, 512), 1) // 16
    fold_rows = lax.broadcasted_iota(jnp.int32, (512, 128), 0) % 16
    fold_lanes = lax.broadcasted_iota(jnp.int32, (512, 128), 1)
    fold_gain = (fold_rows == fold_lanes).astype(f32)
    fold_shift = (fold_rows == fold_lanes - 16).astype(f32)

    def part(core):
        own = owner == 2 * ys + core
        return dot(jnp.where(own, gain, 0.0), fold_gain, 1, 0, highest) + dot(
            jnp.where(own, shift, 0.0), fold_shift, 1, 0, highest
        )

    keep_norm[...] = part(k[0])
    send_norm[...] = part(1 - k[0])


def last_outer_body(keep_one, keep_two, pack, got_one, got_pack, keep_norm, got_norm, result):
    one = dot(keep_one[...], pack[768:1280, :], 1, 1) + dot(
        got_one[...], got_pack[768:1280, :], 1, 1
    )
    two = dot(keep_two[...], pack[256:768, :], 1, 1) + dot(
        got_pack[0:256, :], got_pack[256:768, :], 1, 1
    )
    both_rows = jnp.concatenate([one.reshape(16, 16, 512), two.reshape(16, 16, 512)], axis=1)
    high = both_rows.astype(bf16).astype(f32)
    rest = both_rows - high
    norm = keep_norm[...] + got_norm[...]
    norm_high = norm.astype(bf16).astype(f32)
    lane = lax.broadcasted_iota(jnp.int32, (16, 128), 1)
    line = jnp.where(lane < 32, norm_high, pltpu.roll(norm - norm_high, 32, 1))[:, None, :]
    side = lax.broadcasted_iota(jnp.int32, (16, 32, 128), 2) < 64
    side = side & (lax.broadcasted_iota(jnp.int32, (16, 32, 128), 1) == 31)
    rest = jnp.concatenate([jnp.where(side, line, rest[:, :, :128]), rest[:, :, 128:]], axis=2)
    result[...] = jnp.concatenate([high, rest], axis=1).astype(bf16)


def pick(z, rows):
    blank = jnp.zeros((32, 512), f32)
    third = jnp.concatenate([rows[128:160], blank], axis=0)
    fourth = jnp.concatenate([rows[160:192], blank], axis=0)
    return jnp.where(
        z == 0, rows[0:64], jnp.where(z == 1, rows[64:128], jnp.where(z == 2, third, fourth))
    )


def everything(x):
    return jnp.sum(jnp.sum(x, axis=1, keepdims=True), axis=0, keepdims=True)


def reduce_body(
    parts, wide, wide_one, wide_two, wide_three, big_grad, small_grad, class_grad, head_grad, norm_two,
    scale, narrow, mine, squares, scale_out,
):
    sums = (wide[...] + wide_one[...]) + (wide_two[...] + wide_three[...])
    mine[...] = sums
    scale_out[...] = jnp.broadcast_to(scale[...], (8, 128))
    square = everything(class_grad[...] * class_grad[...])
    square = square + everything(jnp.sum(big_grad[...] * big_grad[...], axis=0))
    square = square + everything(jnp.sum(small_grad[...] * small_grad[...], axis=0))
    square = square + everything(head_grad[...] * head_grad[...])
    square = square + everything(norm_two[...] * norm_two[...])
    squares[...] = jnp.broadcast_to(square, (8, 128))
    total = jnp.sum(parts[...].astype(f32), axis=0)
    line = total[63:64, 0:128]
    lane = lax.broadcasted_iota(jnp.int32, (1, 128), 1)
    line = jnp.where(lane < 32, line + pltpu.roll(line, 96, 1), 0.0)
    row = lax.broadcasted_iota(jnp.int32, (32, 512), 0)
    lane = lax.broadcasted_iota(jnp.int32, (32, 512), 1)
    narrow[0:32, :] = total[:32] + jnp.where((row == 31) & (lane < 64), 0.0, total[32:])
    line = jnp.concatenate([line, jnp.zeros((1, 384), f32)], axis=1)
    narrow[32:40, :] = jnp.broadcast_to(line, (8, 512))
    narrow[40:48, :] = jnp.broadcast_to(everything(sums * sums), (8, 512))


def gather_body(
    z, wide, squares, narrow, narrow_one, narrow_two, narrow_three, scale,
    near, near_low, norm_one, message,
):
    rest = (narrow[...] + narrow_one[...]) + (narrow_two[...] + narrow_three[...])
    last = rest[:32]
    norm = rest[32:33, 0:128] * scale[0:1, :]
    norm_one[...] = jnp.broadcast_to(norm, (8, 128))
    square = squares[0:1, 0:1] + rest[40:41, 0:1] + everything(last * last) + everything(norm * norm)
    mine = jnp.where(z[0] == 3, jnp.concatenate([last, jnp.zeros((32, 512), f32)], axis=0), wide[...])
    near[...] = mine
    near.send()
    near_low[...] = mine.astype(bf16)
    near_low.send()
    high = square.astype(bf16)
    rest = square - high.astype(f32)
    mid = rest.astype(bf16)
    low = (rest - mid.astype(f32)).astype(bf16)
    rows16 = lax.broadcasted_iota(jnp.int32, (16, 512), 0)
    lanes16 = lax.broadcasted_iota(jnp.int32, (16, 512), 1)
    tail = jnp.where(
        lanes16 == 0,
        high.astype(f32),
        jnp.where(lanes16 == 1, mid.astype(f32), jnp.where(lanes16 == 2, low.astype(f32), 0.0)),
    )
    tail = jnp.where(rows16 == 0, tail, 0.0)
    line = jnp.concatenate([mine, tail], axis=0).astype(bf16)
    message[...] = jnp.broadcast_to(line[None], (16, 80, 512))


def split(x):
    high = x.astype(bf16)
    return high, (x - high.astype(f32)).astype(bf16)


def mul3(a, b):
    return dot(a[0], b[0]) + (dot(a[0], b[1]) + dot(a[1], b[0]))


def muon_body(
    k_place, z_place, got, got_other, moment, near, near_other, near_moment, near_moment_other,
    result, result_other, scalars, norm_out, u,
):
    k, z = k_place[0], z_place[0]

    def tails(ref):
        x = ref[:, 64:80, :].astype(f32)
        return jnp.sum(jnp.sum(x, axis=0), axis=0, keepdims=True)

    square = jnp.sum(tails(got) + tails(got_other), axis=1, keepdims=True)
    norm = jnp.sqrt(square)
    f = jnp.minimum(1.0, clip_limit / (norm + 1e-06))
    line = lax.broadcasted_iota(jnp.int32, (8, 128), 1)
    scalars[...] = jnp.where(line == 0, norm, f)
    norm_out[0, 0] = norm[0, 0]
    scalars.send()
    alpha = (1.0 + momentum_decay) * f
    beta = momentum_decay * momentum_decay
    first = jnp.where((z < 3) | (k == 0), 1.0, 0.0)
    second = jnp.where((z < 3) | (k == 1), 1.0, 0.0)
    parts = ((0, 16, first), (16, 32, second), (32, 64, jnp.float32(1.0)))
    for i, g in enumerate((got, got_other)):
        for y in range(16):
            for low, high, share in parts:
                value = (alpha * share) * g[y, low:high, :].astype(f32)
                value = value + (beta * share) * moment[i, y, low:high, :].astype(f32)
                at = i * 1024 + y * 64
                u[at + low : at + high, :] = value.astype(bf16)
    gram = dot(u[...], u[...], 0, 0)
    rows = lax.broadcasted_iota(jnp.int32, (512, 512), 0)
    cols = lax.broadcasted_iota(jnp.int32, (512, 512), 1)
    eye = (rows == cols).astype(f32)
    total = jnp.sum(jnp.sum(gram * eye, axis=0, keepdims=True), axis=1, keepdims=True)
    inverse = 1.0 / (jnp.sqrt(total) + 1e-07)
    a = gram * (inverse * inverse)
    x = jnp.concatenate(
        [
            (alpha * near[...] + beta * near_moment[...]) * inverse,
            (alpha * near_other[...] + beta * near_moment_other[...]) * inverse,
        ],
        axis=0,
    )
    for step in range(NS_STEPS - 1):
        a2 = split(a)
        square = mul3(a2, a2)
        m2 = split(coef_first * eye + coef_second * a + coef_third * square)
        x = mul3(split(x), m2)
        a = mul3(split(mul3(a2, m2)), m2)
    a2 = split(a)
    once = mul3(split(x), a2)
    x = coef_first * x + coef_second * once + coef_third * mul3(split(once), a2)
    result[...] = x[:64]
    result_other[...] = x[64:]


def adamw(weight, first, second, gradient, rate):
    first = beta_first * first + (1.0 - beta_first) * gradient
    second = beta_second * second + (1.0 - beta_second) * gradient * gradient
    ratio = (
        first / (1.0 - beta_first**STEP) / (jnp.sqrt(second / (1.0 - beta_second**STEP)) + 1e-08)
    )
    return (first, second, weight - rate * (ratio + weight_decay * weight))


def by_matrix(z, got):
    group = []
    for j in range(4):
        back = lax.rem(z - j + 4, 4)
        group.append(
            jnp.where(
                back == 0,
                got[0],
                jnp.where(back == 1, got[1], jnp.where(back == 2, got[2], got[3])),
            )
        )
    return [group[3][:16], group[3][16:32], group[0], group[1], group[2][:32]]


def finish_body(
    z, scalars, mine, one, two, three_back, class_grad, big_grad, small_grad, norm_one, norm_two, head_grad,
    *refs
):
    moments, refs = refs[:5], refs[5:]
    states, refs = refs[:15], refs[15:]
    fresh, updated = refs[:5], refs[5:]
    f = scalars[0:1, 1:2]
    rows = by_matrix(z[0], [mine[...], one[...], two[...], three_back[...]])
    for moment, row, out in zip(moments, rows, fresh):
        out[...] = momentum_decay * moment[...] + f * row.astype(f32)
        out.send()
    norm = norm_one[0:1, :]
    grads = [
        class_grad[:, :1000],
        big_grad[...],
        small_grad[...],
        jnp.concatenate([norm[:, 0:16], norm[:, 16:32], norm_two[...]], axis=0),
        head_grad[0:2, 0:32],
    ]
    rates = [adam_rate, adam_rate, adam_rate, norm_rate, norm_rate]
    for i in range(5):
        factor = f if grads[i].ndim == 2 else f.reshape(1, 1, 1)
        first, second, weight = adamw(
            states[3 * i][...], states[3 * i + 1][...], states[3 * i + 2][...],
            grads[i] * factor, rates[i],
        )
        updated[3 * i][...] = first
        updated[3 * i + 1][...] = second
        updated[3 * i + 2][...] = weight
        for j in range(3):
            updated[3 * i + j].send()


def renew_body(z, mine, one, two, three_back, *refs):
    weights, outs = refs[:5], refs[5:]
    rows = by_matrix(z[0], [mine[...], one[...], two[...], three_back[...]])
    for weight, row, (_, n), out in zip(weights, rows, PLACES, outs):
        rate = muon_rate * 0.2 * math.sqrt(max(512, 32 * n))
        out[...] = weight[...] * (1.0 - muon_rate * weight_decay) - rate * row.astype(f32)
        out.send()


def shards(
    features,
    labels,
    partner,
    class_weight,
    point_one,
    momentum_one,
    point_two,
    momentum_two,
    expand,
    momentum_up,
    shrink,
    momentum_down,
    transit,
    momentum_transit,
    classifier,
    classifier_first,
    classifier_second,
    big_kernel,
    big_first,
    big_second,
    small_kernel,
    small_first,
    small_second,
    norm_gains,
    gains_first,
    gains_second,
    head_gains,
    head_first,
    head_second,
):
    z = lax.axis_index("batch")
    c = lax.axis_index("chan")
    k = lax.rem(c, 2)
    crop = z * 32 + c
    widen = widen_matrix()
    compact = compact_matrix()
    k_scalar = k.reshape(1).astype(jnp.int32)
    classes = class_weight.shape[0]

    flat = features.astype(f32)
    local_mean = jnp.mean(flat, axis=(1, 2))
    local_spread = jnp.mean(jnp.square(flat - local_mean[:, None, None]), axis=(1, 2))
    vector = jnp.concatenate(
        [local_mean, local_spread, labels.astype(f32), partner.astype(f32)]
    )[None, :]
    paired = z_pair(vector)
    gathered = z_gather_rows(vector, paired)
    means = gathered[:, :16]
    center = jnp.mean(means, axis=0)
    variance = jnp.mean(gathered[:, 16:32], axis=0) + jnp.mean(
        jnp.square(means - center[None]), axis=0
    )
    people = jnp.stack([gathered[:, 32:64].reshape(128), gathered[:, 64:96].reshape(128)], axis=1)
    scale_own = lax.rsqrt(variance + epsilon)

    z_scalar = z.reshape(1).astype(jnp.int32)
    matrices = [w.T for w in (point_one, point_two, expand, shrink, transit)]
    moments = [
        m.T for m in (momentum_one, momentum_two, momentum_up, momentum_down, momentum_transit)
    ]
    head_line = jnp.stack(
        [
            jnp.pad(jnp.concatenate(three(head_gains[i])).astype(f32), (0, 32))
            for i in range(2)
        ]
    ).reshape(1, 256)
    head_line = jnp.pad(head_line, ((0, 0), (0, 256)))
    packed, packed_late, near_moment = whole(
        pack_body,
        [((176, 512), bf16), ((144, 512), bf16), ((64, 512), f32)], "pack",
        scalars=1,
        cost=3,

    )(
        z_scalar,
        *matrices[1:],
        classifier,
        moments[2],
        moments[3],
        moments[4],
        moments[0],
        moments[1],
        head_line,
    )
    weights = lax.all_gather(packed, "chan", axis=0, tiled=False).reshape(16, 2, 176, 512)
    late_weights = lax.all_gather(packed_late, "chan", axis=0, tiled=False)
    late_weights = late_weights.reshape(16, 2, 144, 512)
    near_moment_other = core_swap(near_moment)

    margin = (KB - KS) // 2
    kernel = big_kernel + jnp.pad(small_kernel, ((0, 0), (margin, margin), (margin, margin)))
    centre = kernel[:, 2:29, 2:29].astype(bf16)
    flat_kernel = jnp.pad(
        jnp.pad(centre, ((0, 0), (0, 0), (0, 5))).reshape(16, TAPS * 32), ((0, 0), (0, 48))
    )
    shifted = jnp.stack(
        [flat_kernel[:, 13 - px : 13 - px + 896] for px in range(S)]
        + [jnp.zeros((16, 896), bf16)] * 2,
        axis=1,
    ).reshape(256, 896)
    (table,) = whole(
        taps_body, [((16, 256, 256), bf16)], "taps", small_out=0
    )(shifted, compact)

    extra = []
    for item in (
        center,
        scale_own * norm_gains[0],
        norm_gains[1],
        norm_gains[2],
        norm_gains[3],
    ):
        extra += three(item)
    extra = jnp.stack(extra, axis=1)
    extra = jnp.pad(extra, ((0, 0), (0, 60 - extra.shape[1])))
    fixed = jnp.concatenate([extra, point_one.T.astype(bf16)], axis=1)
    payload = jnp.concatenate(
        [features.transpose(1, 0, 2), jnp.broadcast_to(fixed[None], (32,) + fixed.shape)], axis=2
    )
    came = lax.all_to_all(payload, "chan", 0, 0, tiled=True).reshape(512, 768)
    act_one, slope_one, a1 = whole(
        first_body, [((512, 256), bf16), ((512, 256), f32), ((512, 256), bf16)], "first", cost=4
    )(came)
    (slope_one,) = whole(slope_body, [((512, 256), f32)], "slope_one", cost=1)(slope_one)
    u = lax.all_to_all(act_one.reshape(32, 16, 256), "chan", 0, 0, tiled=True).transpose(1, 0, 2)
    mixed, act = whole(
        depth_forward_body, [((16, 32, 256), f32), ((16, 32, 256), bf16)], "depth_forward", cost=4,
    )(u, table, widen)
    (mixed,) = whole(slope_body, [((16, 32, 256), f32)], "slope_mixed", cost=1)(mixed)
    gd = lax.all_to_all(act.transpose(1, 0, 2), "chan", 0, 0, tiled=True).reshape(512, 256)

    middle, gains, stats = whole(
        middle_body,
        [((208, 512), f32), ((8, 512), f32), ((128, 8, 128), f32)],
        "middle",
        cost=4,
        pieces={2: [natural(0, 16)]},
    )(came, gd, weights)
    stats = lax.all_to_all(stats, both, 0, 0, tiled=True)
    normal_two, factor_two, pack_one, keep_act, hid, t, pooled = whole(
        forward_body,
        [
            ((208, 512), f32),
            ((8, 512), f32),
            ((256, 2048), bf16),
            ((256, 1024), bf16),
            ((208, 2048), f32),
            ((208, 1024), f32),
            ((128, 8, 128), f32),
        ],
        "forward",
        cost=4,
        scalars=1,
        pieces={3: [own_first(16, 64), own_first(80, 64), own_first(144, 32)]},
    )(k_scalar, stats, middle, gains, weights)
    pooled = lax.all_to_all(pooled, both, 0, 0, tiled=True)
    slope_hid, slope_t = whole(
        slopes_body, [((208, 2048), f32), ((208, 1024), f32)], "slopes"
    )(hid, t)
    place = jnp.stack([k, crop, k * 512 + (c // 2) * 32]).astype(jnp.int32)
    pack_two, keep_hid, keep_t, dx2, da2, sums, z_low, dlogits, head_rows, loss_sum, weight_sum = whole(
        head_body,
        [
            ((256, 2048), bf16),
            ((256, 1024), bf16),
            ((256, 512), bf16),
            ((208, 512), f32),
            ((208, 512), f32),
            ((128, 8, 128), f32),
            ((128, 1024), bf16),
            ((128, 1024), bf16),
            ((8, 1024), f32),
        ],
        "head",
        scalar_outs=2,
        cost=4,
        scalars=1,
        pieces={
            3: [
                by_core(128, 16),
                by_core(0, 64),
            ],
            4: [
                own_first(144, 32),
                own_first(80, 64),
                own_first(16, 64),
            ]
        },
    )(
        place,
        pooled,
        people,
        jnp.pad(class_weight, (0, 1024 - classes))[None, :],
        late_weights,
        weights,
        slope_t,
        slope_hid,
        normal_two,
    )
    sums = lax.all_to_all(sums, both, 0, 0, tiled=True)
    class_grad, head_grad = whole(
        classes_body, [((32, 1024), f32), ((8, 128), f32)], "classes", scalars=1
    )(place, z_low, dlogits, head_rows)

    (wide_parts,) = whole(
        outer_body,
        [((16, 160, 512), f32)],
        "outer",
        parts={0: [np.s_[:, 64:128], np.s_[:, 0:64], np.s_[:, 128:160]]},
    )(
        keep_act, keep_hid, keep_t, pack_one, pack_two, core_swap(pack_one), core_swap(pack_two)
    )
    wide_sum = lax.psum_scatter(
        wide_parts, "chan", scatter_dimension=0, axis_index_groups=same_core()
    )

    keep_two, pack_three, dgd, norm_two = whole(
        second_body,
        [((256, 256), bf16), ((1280, 256), bf16), ((512, 256), bf16), ((8, 128), f32)],
        "second",
        cost=BACK,
        scalars=1,
        pieces={5: [natural(0, 16)]},
    )(k_scalar, sums, da2, normal_two, factor_two, dx2, weights, gd, a1)
    grad_mixed = lax.all_to_all(
        dgd.reshape(32, 16, 256), "chan", 0, 0, tiled=True
    ).transpose(1, 0, 2)
    back, tap_grad = whole(
        depth_backward_body,
        [((16, 32, 256), bf16), ((16, 1024), f32)],
        "depth_backward",
        small_in=0,
        cost=BACK,
        scratch=[pltpu.VMEM((16, 256, 512), f32), pltpu.VMEM((16, 16, 1024), f32)],
    )(u, mixed, grad_mixed, table, widen, compact)
    du1 = lax.all_to_all(back.transpose(1, 0, 2), "chan", 0, 0, tiled=True).reshape(512, 256)
    keep_one, send_one, keep_norm, send_norm, tap_grad = whole(
        third_body,
        [
            ((256, 256), bf16),
            ((256, 256), bf16),
            ((16, 128), f32),
            ((16, 128), f32),
            ((16, 1024), f32),
        ],
        "third",
        cost=BACK,
        scalars=1,
    )(k_scalar, came, du1, slope_one, tap_grad, *z_shifts(tap_grad))
    (narrow_parts,) = whole(last_outer_body, [((16, 64, 512), bf16)], "last_outer", cost=BACK)(
        keep_one,
        keep_two,
        pack_three,
        core_swap(send_one),
        core_swap(pack_three),
        keep_norm,
        core_swap(send_norm),
    )
    big_grad = tap_grad[:, :864].reshape(16, TAPS, 32)[:, :, :TAPS]
    big_grad = jnp.pad(big_grad, ((0, 0), (2, 2), (2, 2)))
    small_grad = big_grad[:, margin : margin + KS, margin : margin + KS].transpose(1, 2, 0)
    big_grad = big_grad.transpose(1, 0, 2)
    norm_two_own = lax.dynamic_slice_in_dim(norm_two.reshape(2, 512), c * 16, 16, 1)
    line = jnp.concatenate([scale_own, jnp.ones((16,), f32), jnp.zeros((96,), f32)])
    scale_line = line[None]
    wide_sum = jnp.pad(wide_sum.reshape(160, 512), ((0, 96), (0, 0)))

    def for_group(j):
        return lax.dynamic_slice_in_dim(wide_sum, 64 * lax.rem(z + j, 4), 64, 0)

    narrow_sum, mine_wide, squares, scale_line = whole(
        reduce_body,
        [((48, 512), f32), ((64, 512), f32), ((8, 128), f32), ((8, 128), f32)], "reduce", cost=4
    )(
        groups_all_to_all(narrow_parts),
        for_group(0),
        *[
            lax.ppermute(for_group(j), "batch", [(i, (i + j) % 4) for i in range(4)])
            for j in range(1, 4)
        ],
        big_grad,
        small_grad,
        class_grad,
        head_grad,
        norm_two_own,
        scale_line,
    )
    near, near_low, norm_one, message = whole(
        gather_body,
        [((64, 512), f32), ((64, 512), bf16), ((8, 128), f32), ((16, 80, 512), bf16)],
        "gather",
        scalars=1,
        cost=4,
    )(z_scalar, mine_wide, squares, narrow_sum, *z_shifts(narrow_sum), scale_line)
    near_shifts = z_shifts(near_low)
    arrived = sum(item[0, 0].astype(f32) for item in near_shifts) < 1e30
    got = groups_all_to_all(message)
    got = jnp.where(arrived, got, -got)
    near_other = core_swap(near)
    near_rows, near_rows_other, scalars, grad_norm = whole(
        muon_body,
        [((64, 512), f32), ((64, 512), f32), ((8, 128), f32)],
        "muon",
        cost=4,
        scratch=[pltpu.VMEM((2048, 512), bf16)],
        scalars=2,
        scalar_outs=1,
        pieces={2: [own_first(64, 64)]},
    )(
        k_scalar,
        z_scalar,
        got,
        core_swap(got),
        late_weights,
        near,
        near_other,
        near_moment,
        near_moment_other,
    )
    row = np.arange(64)
    first_rows = jnp.asarray((row < 16).astype(np.float32))
    second_rows = jnp.asarray(((row >= 16) & (row < 32)).astype(np.float32))
    own_rows = jnp.where(z < 3, 1.0, jnp.where(k == 0, first_rows, second_rows))[:, None]
    mine_result = jnp.where(own_rows > 0, near_rows, core_swap(near_rows_other)).astype(bf16)
    def turn_big(x):
        return x.transpose(1, 0, 2)

    def turn_small(x):
        return x.transpose(1, 2, 0)

    states = [
        *(classifier, classifier_first, classifier_second),
        *(turn_big(x) for x in (big_kernel, big_first, big_second)),
        *(turn_small(x) for x in (small_kernel, small_first, small_second)),
        *(norm_gains, gains_first, gains_second),
        *(head_gains, head_first, head_second),
    ]
    updates = whole(
        finish_body, [(x.shape, f32) for x in moments + states], "finish", scalars=1, cost=6
    )(
        z_scalar,
        scalars,
        near_low,
        *near_shifts,
        class_grad,
        big_grad,
        small_grad,
        norm_one,
        norm_two_own,
        head_grad,
        *moments,
        *states,
    )
    renewed = whole(
        renew_body, [(m.shape, f32) for m in matrices], "renew", scalars=1, cost=4
    )(z_scalar, mine_result, *z_shifts(mine_result), *matrices)
    pairs = [item.T for pair in zip(renewed, updates[:5]) for item in pair]
    states = list(updates[5:])
    states[3:6] = [x.transpose(1, 0, 2) for x in states[3:6]]
    states[6:9] = [x.transpose(2, 0, 1) for x in states[6:9]]
    return (
        loss_sum.reshape(()), weight_sum.reshape(()), grad_norm.reshape(()), *pairs, *states
    )


def solution(mesh):
    split_columns = P(None, "chan")
    split_rows = P("chan", None)
    split_first = P("chan", None, None)
    in_specs = (
        (P("chan", "batch", None), P("batch"), P("batch"), P())
        + (split_columns,) * 10
        + (split_rows,) * 3
        + (split_first,) * 6
        + (split_columns,) * 6
    )
    out_specs = (
        (P(), P(), P())
        + (split_columns,) * 10
        + (split_rows,) * 3
        + (split_first,) * 6
        + (split_columns,) * 6
    )
    return jax.shard_map(shards, mesh=mesh, in_specs=in_specs, out_specs=out_specs, check_vma=False)
```
